32 devices in a mesh: dp: 8 (over z, y), pipe: 4 (over x, core).
Axes of the slice: x: 2, y: 2, z: 4, core: 2. Of those that a mesh axis runs over, the one named last changes fastest.
Arguments:
- frames: bfloat16 [32, 8, 3, 8, 64], P('dp'), may hold values from -40 to 40
- cut_mask: int32 [32, 7], P('dp'), may hold values 0 or 1
- offsets: int32 [32], P('dp'), may hold values from 2 to 6
- stem_kernel: bfloat16 [147, 64], replicated, may hold values from -0.5 to 0.5
- diff_kernel: bfloat16 [9, 6, 64], replicated, may hold values from -0.875 to 0.875
- stem_gain: float32 [64], replicated, may hold values from 0.1 to 1.9
- stem_bias: float32 [64], replicated, may hold values from -4 to 4
- reduce_weight: bfloat16 [2048, 512], replicated, may hold values from -0.125 to 0.125
- reduce_gain: float32 [512], replicated, may hold values from 0.1 to 1.9
- reduce_bias: float32 [512], replicated, may hold values from -4 to 4
- squeeze_weight: bfloat16 [512, 32], replicated, may hold values from -0.25 to 0.25
- fine_kernel: bfloat16 [9, 32, 32], replicated, may hold values from -0.375 to 0.375
- coarse_kernel: bfloat16 [9, 32, 32], replicated, may hold values from -0.375 to 0.375
- excite_weight: bfloat16 [32, 512], replicated, may hold values from -1 to 1
- middle_kernel: bfloat16 [9, 512, 512], replicated, may hold values from -0.09375 to 0.09375
- expand_weight: bfloat16 [512, 2048], replicated, may hold values from -0.25 to 0.25
- expand_gain: float32 [2048], replicated, may hold values from 0.1 to 1.9
- expand_bias: float32 [2048], replicated, may hold values from -4 to 4
- cotangent: bfloat16 [32, 8, 2, 8, 2048], P('dp'), may hold values from -6 to 6
Outputs:
- frame_grad: float32 [32, 8, 3, 8, 64], P(('dp', 'pipe'))
- stem_kernel_grad: float32 [147, 64], replicated
- diff_kernel_grad: float32 [9, 6, 64], replicated
- stem_gain_grad: float32 [64], replicated
- stem_bias_grad: float32 [64], replicated
- reduce_weight_grad: float32 [2048, 512], replicated
- reduce_gain_grad: float32 [512], replicated
- reduce_bias_grad: float32 [512], replicated
- squeeze_weight_grad: float32 [512, 32], replicated
- fine_kernel_grad: float32 [9, 32, 32], replicated
- coarse_kernel_grad: float32 [9, 32, 32], replicated
- excite_weight_grad: float32 [32, 512], replicated
- middle_kernel_grad: float32 [9, 512, 512], replicated
- expand_weight_grad: float32 [512, 2048], replicated
- expand_gain_grad: float32 [2048], replicated
- expand_bias_grad: float32 [2048], replicated
The draws below stay inside these ranges and needn't reach their ends.
Inputs may be any that keep to these rules, and one draw needn't show every extreme that they name: Each clip holds two videos, of offsets[c] and 8 - offsets[c] frames.
All inputs are finite; a program needn't handle non-finite values. No bound on the sum of `cut_mask` on one device may be relied on, other than what follows from the above.
Results may differ from the reference program's by a relative error of at most 0.02.
Values may be sent and summed in bfloat16 or wider, within the bound.
No kernel may reach another device: no remote copies, remote signals or barrier semaphores. Data moves between devices by JAX's collectives and lax.ppermute only.
A program may use at most 256 MiB of HBM per device.

```python
import jax
import jax.numpy as jnp
from jax import lax

STEM = 64
WIDE = 2048
MID = 512
SQ = 32
FRAMES = 8
MICRO = 4
CPM = 1
H = 8
W = 64
BH = 2
BW = 8
CLIPS = 32
N_DP = 8


def draw_frames(key, part):
    key = jax.random.fold_in(key, 17)
    first_key, second_key = jax.random.split(key, 2)
    position = jnp.arange(CLIPS, dtype=jnp.float32) / max(CLIPS - 1, 1)
    ramp = jnp.exp(jnp.log(3.0) * position)
    base = jax.random.truncated_normal(first_key, -4.0, 4.0, (CLIPS, FRAMES, 3, H, W), jnp.float32)
    frame_scale = jnp.exp(jax.random.uniform(second_key, (CLIPS, FRAMES, 1, 1, 1), jnp.float32, -0.7, 0.7))
    return (base * frame_scale * ramp[:, None, None, None, None]).astype(jnp.bfloat16)


def touch_ends(values, stream_key, low, largest):
    extent = values.shape
    place = [jax.random.randint(jax.random.fold_in(stream_key, axis), (), 0, extent[axis]) for axis in range(len(extent))]
    values = values.at[tuple(place)].set(low)
    longest = extent.index(max(extent))
    place[longest] = (place[longest] + 1) % extent[longest]
    return values.at[tuple(place)].set(largest)


def steps_of(key, dims, shards, low, largest):
    def one(dim, shards_of):
        draws = jax.random.uniform(jax.random.fold_in(jax.random.fold_in(key, 6), dim), (shards_of,), jnp.float32, low / len(shards), largest / len(shards))
        return jnp.repeat(jnp.exp(draws), dims[dim] // shards_of).reshape((-1,) + (1,) * (len(dims) - dim - 1))

    loudness = one(*shards[0])
    for cut in shards[1:]:
        loudness = loudness * one(*cut)
    return loudness


def normal_values(stream_key, shape, spread, reach, cuts=(), held_as=jnp.bfloat16):
    factor_of = steps_of(stream_key, shape, cuts, -0.22, 0.18) if cuts else 1.0
    values = jax.random.normal(stream_key, shape, jnp.float32) * spread * factor_of
    return jnp.minimum(jnp.maximum(values, -reach), reach).astype(held_as)


def setup_inputs(seed: int = 0) -> dict:
    splits = jax.random.split(jax.random.key(seed), 20)
    return {
        "frames": draw_frames(jax.random.fold_in(splits[19], 71), 0),
        "cut_mask": touch_ends((jax.random.randint(splits[1], (CLIPS, FRAMES - 1), 0, 4) < 3).astype(jnp.int32), jax.random.fold_in(splits[1], 1), 0, 1),
        "offsets": touch_ends(jax.random.randint(splits[2], (CLIPS,), 2, 7), jax.random.fold_in(splits[2], 1), 2, 6).astype(jnp.int32),
        "stem_kernel": normal_values(splits[3], (147, STEM), 147 ** -0.5, 0.5),
        "diff_kernel": normal_values(splits[4], (9, 6, STEM), 54 ** -0.5, 0.875),
        "stem_gain": jnp.clip(1.0 + 0.18 * jax.random.normal(splits[5], (STEM,), jnp.float32), 0.1, 1.9),
        "stem_bias": normal_values(splits[6], (STEM,), 0.3, 4.0, (), jnp.float32),
        "reduce_weight": normal_values(splits[7], (WIDE, MID), WIDE ** -0.5, 0.125),
        "reduce_gain": jnp.clip(1.0 + 0.18 * jax.random.normal(splits[8], (MID,), jnp.float32), 0.1, 1.9),
        "reduce_bias": normal_values(splits[9], (MID,), 0.3, 4.0, (), jnp.float32),
        "squeeze_weight": normal_values(splits[10], (MID, SQ), MID ** -0.5, 0.25),
        "fine_kernel": normal_values(splits[11], (9, SQ, SQ), (9 * SQ) ** -0.5, 0.375),
        "coarse_kernel": normal_values(splits[12], (9, SQ, SQ), (9 * SQ) ** -0.5, 0.375),
        "excite_weight": normal_values(splits[13], (SQ, MID), SQ ** -0.5, 1.0),
        "middle_kernel": normal_values(splits[14], (9, MID, MID), (9 * MID) ** -0.5, 0.09375),
        "expand_weight": normal_values(splits[15], (MID, WIDE), MID ** -0.5, 0.25),
        "expand_gain": jnp.clip(1.0 + 0.18 * jax.random.normal(splits[16], (WIDE,), jnp.float32), 0.1, 1.9),
        "expand_bias": normal_values(splits[17], (WIDE,), 0.3, 4.0, (), jnp.float32),
        "cotangent": normal_values(splits[18], (CLIPS, FRAMES, BH, BW, WIDE), 1.0, 6.0, ((0, 8),)),
    }


HIGHEST = lax.Precision.HIGHEST
EPSILON = 1e-05

@jax.custom_vjp
def low(v):
    return lax.optimization_barrier(v.astype(jnp.bfloat16)).astype(jnp.float32)

@jax.custom_vjp
def low_back(v):
    return v

def low_keep(v):
    return (low(v), None)

def low_pass(kept, grad):
    return (grad,)

def back_keep(v):
    return (v, None)

def back_low(kept, grad):
    return (low(grad),)
low.defvjp(low_keep, low_pass)
low_back.defvjp(back_keep, back_low)

def matmul(left, right):
    return jnp.dot(left, right, precision=HIGHEST, preferred_element_type=jnp.float32)

def patches_of(feature_maps, kernel_size):
    margin = kernel_size // 2
    map_count, height, map_width, channels = feature_maps.shape
    padded = jnp.pad(feature_maps, ((0, 0), (margin, margin), (margin, margin), (0, 0)))
    pieces = [padded[:, row_shift:row_shift + height, col_shift:col_shift + map_width, :] for row_shift in range(kernel_size) for col_shift in range(kernel_size)]
    return jnp.stack(pieces, 3).reshape(map_count * height * map_width, kernel_size * kernel_size * channels)

def avg_pool(feature_maps):
    map_count, height, map_width, channels = feature_maps.shape
    return lax.optimization_barrier(jnp.mean(feature_maps.reshape(map_count, height // 2, 2, map_width // 2, 2, channels), axis=(2, 4)))

def upsample(feature_maps):
    return jnp.repeat(jnp.repeat(feature_maps, 2, axis=1), 2, axis=2)

def batch_norm(value_list, gain, bias):
    mean_val = lax.optimization_barrier(jnp.mean(value_list, axis=0))
    variance = lax.optimization_barrier(jnp.mean(value_list * value_list, axis=0)) - mean_val * mean_val
    return (value_list - mean_val) * lax.rsqrt(variance + EPSILON) * gain + bias

def to_wide(feature_maps):
    map_count, height, map_width, channels = feature_maps.shape
    blocks = feature_maps.reshape(map_count, height // 4, 4, map_width // 8, 8, channels).transpose(0, 1, 3, 2, 4, 5)
    return blocks.reshape(map_count * (height // 4) * (map_width // 8), 32 * channels)

def frame_steps(frames_last, valid_micro):
    step_diff = (frames_last[:, 1:] - frames_last[:, :-1]) * valid_micro[:, :, None, None, None]
    zero_step = jnp.zeros_like(step_diff[:, :1])
    return jnp.concatenate([jnp.concatenate([zero_step, step_diff], 1), jnp.concatenate([step_diff, zero_step], 1)], -1)

def micro_forward(frames_micro, valid_micro, weights):
    w_stem, w_diff, stem_gain, stem_bias, w_reduce, reduce_gain, reduce_bias, w_squeeze, w_fine, w_coarse, w_excite, w_middle, w_expand, expand_gain, expand_bias = weights
    clip_count = frames_micro.shape[0]
    map_count = clip_count * FRAMES
    frames_last = jnp.transpose(frames_micro, (0, 1, 3, 4, 2))
    direct = low_back(matmul(patches_of(frames_last.reshape(map_count, H, W, 3), 7), w_stem))
    step_maps = frame_steps(frames_last, valid_micro).reshape(map_count, H, W, 6)
    pooled = low(avg_pool(step_maps))
    side_part = low_back(matmul(patches_of(pooled, 3), w_diff.reshape(54, STEM)))
    side_part = upsample(side_part.reshape(map_count, H // 2, W // 2, STEM)).reshape(map_count * H * W, STEM)
    stem_out = jax.nn.silu(batch_norm(direct + side_part, stem_gain, stem_bias))
    wide_maps = low_back(low(to_wide(stem_out.reshape(map_count, H, W, STEM))))
    reduced = low_back(matmul(wide_maps, w_reduce))
    narrow = jax.nn.silu(batch_norm(reduced, reduce_gain, reduce_bias))
    squeezed = low_back(matmul(low(narrow), w_squeeze)).reshape(clip_count, FRAMES, BH, BW, SQ)
    change = (squeezed[:, 1:] - squeezed[:, :-1]) * valid_micro[:, :, None, None, None]
    change = jnp.concatenate([change, jnp.zeros_like(change[:, :1])], 1).reshape(map_count, BH, BW, SQ)
    fine_part = matmul(patches_of(low(change), 3), w_fine.reshape(9 * SQ, SQ))
    coarse = low_back(matmul(patches_of(low(avg_pool(change)), 3), w_coarse.reshape(9 * SQ, SQ)))
    coarse = upsample(coarse.reshape(map_count, BH // 2, BW // 2, SQ)).reshape(map_count * BH * BW, SQ)
    summed = low_back(fine_part + coarse)
    excite = low_back(matmul(low(summed), w_excite))
    gated_out = low_back(low(narrow * (1.0 + jax.nn.sigmoid(excite))))
    hidden = low_back(matmul(patches_of(gated_out.reshape(map_count, BH, BW, MID), 3), w_middle.reshape(9 * MID, MID)))
    hidden = low_back(low(jax.nn.silu(hidden)))
    expanded = low_back(matmul(hidden, w_expand))
    return jax.nn.silu(batch_norm(expanded, expand_gain, expand_bias) + low_back(wide_maps))

def reference(frames, cut_mask, offsets, stem_kernel, diff_kernel, stem_gain, stem_bias, reduce_weight, reduce_gain, reduce_bias, squeeze_weight, fine_kernel, coarse_kernel, excite_weight, middle_kernel, expand_weight, expand_gain, expand_bias, cotangent):
    later_frame = jnp.arange(1, FRAMES, dtype=jnp.int32)
    valid_step = (cut_mask * (later_frame[None, :] != offsets[:, None]).astype(jnp.int32)).astype(jnp.float32)
    weights = tuple((item_w.astype(jnp.float32) for item_w in (stem_kernel, diff_kernel, stem_gain, stem_bias, reduce_weight, reduce_gain, reduce_bias, squeeze_weight, fine_kernel, coarse_kernel, excite_weight, middle_kernel, expand_weight, expand_gain, expand_bias)))
    checked = jax.checkpoint(micro_forward)

    def forward(frames_full, weight_set):
        grouped = frames_full.reshape(N_DP, MICRO, CPM, FRAMES, 3, H, W)
        valid_grouped = valid_step.reshape(N_DP, MICRO, CPM, FRAMES - 1)
        outputs = []
        for microbatch_index in range(MICRO):
            frames_micro = grouped[:, microbatch_index].reshape(N_DP * CPM, FRAMES, 3, H, W)
            valid_micro = valid_grouped[:, microbatch_index].reshape(N_DP * CPM, FRAMES - 1)
            result = checked(frames_micro, valid_micro, weight_set)
            outputs.append(result.reshape(N_DP, CPM, FRAMES, BH, BW, WIDE))
        return jnp.stack(outputs, 1).reshape(CLIPS, FRAMES, BH, BW, WIDE)
    _, pullback = jax.vjp(forward, frames.astype(jnp.float32), weights)
    frame_grad, weight_grads = pullback(cotangent.astype(jnp.float32))
    return (frame_grad, weight_grads[0], weight_grads[1], weight_grads[2], weight_grads[3], weight_grads[4], weight_grads[5], weight_grads[6], weight_grads[7], weight_grads[8], weight_grads[9], weight_grads[10], weight_grads[11], weight_grads[12], weight_grads[13], weight_grads[14])
```

```python
import functools

import jax
import jax.numpy as jnp
from jax import lax
from jax.experimental import pallas as pl
from jax.experimental.pallas import tpu as pltpu
from jax.sharding import PartitionSpec as P

FRAMES = 8
MICRO = 4
EPSILON = 1e-05
BF = jnp.bfloat16
F32 = jnp.float32

STEM = 64
SLOT = 16


def dot(left, right):
    return jnp.dot(left, right, preferred_element_type=F32)


def dot_nt(left, right):
    return lax.dot_general(left, right, (((1,), (1,)), ((), ())), preferred_element_type=F32)


def dot_tn(left, right):
    return lax.dot_general(left, right, (((0,), (0,)), ((), ())), preferred_element_type=F32)


def dot_exact(left, right):
    return jnp.dot(left, right, preferred_element_type=F32, precision=lax.Precision.HIGHEST)


def iota(shape, dim):
    return lax.broadcasted_iota(jnp.int32, shape, dim)


def sigmoid(v):
    return 1.0 / (1.0 + jnp.exp(-v))


def swish_slope(v):
    s = sigmoid(v)
    return s * (1.0 + v * (1.0 - s))


def valid_scalars(place_ref, cut_ref, offset_ref):
    clip = place_ref[0]
    stop = offset_ref[clip]
    return [
        jnp.where(stop == t + 1, 0, cut_ref[clip, t]).astype(F32) for t in range(FRAMES - 1)
    ]


def frame_column(scalars, rows, lanes):
    return jnp.concatenate([jnp.full((rows, lanes), s, F32) for s in scalars], 0)


def norm_scale(sums, row_total):
    mean = sums[0:1] * (1.0 / row_total)
    variance = sums[1:2] * (1.0 / row_total) - mean * mean
    return mean, lax.rsqrt(variance + EPSILON)


def column_sums(first, second):
    return jnp.concatenate(
        [jnp.sum(first, 0, keepdims=True), jnp.sum(second, 0, keepdims=True)], 0
    )


def fold_lanes(sums):
    for step in (64, 128, 256):
        sums = sums + pltpu.roll(sums, step, 1)
    return sums


def shift_rows(v, dy, dx):
    rows = v.shape[0]
    if dx:
        rolled = pltpu.roll(v, (-dx) % rows, 0)
        wb = lax.rem(iota(v.shape, 0), 8)
        v = jnp.where((wb + dx >= 0) & (wb + dx < 8), rolled, 0.0)
    half = rows // 2
    if dy == 1:
        v = jnp.concatenate([v[half:], jnp.zeros_like(v[half:])], 0)
    elif dy == -1:
        v = jnp.concatenate([jnp.zeros_like(v[:half]), v[:half]], 0)
    return v


def cell_sum(v):
    half = v.shape[0] // 2
    both = v[:half] + v[half:]
    even = lax.rem(iota(both.shape, 0), 2) == 0
    both = both + jnp.where(even, pltpu.roll(both, half - 1, 0), pltpu.roll(both, 1, 0))
    return jnp.concatenate([both, both], 0)


def taps(v):
    return [shift_rows(v, ky - 1, kx - 1) for ky in range(3) for kx in range(3)]


def back_taps(v):
    return [shift_rows(v, 1 - ky, 1 - kx) for ky in range(3) for kx in range(3)]


def coarse_taps(v):
    return [shift_rows(v, 0, 2 * (k - 1)) for k in range(3)]


def window_select(rows, cols, kind):
    place = iota((rows, cols), 0)
    col = iota((rows, cols), 1)
    lane = lax.rem(place, 128)
    tap_row = lax.div(place, 128)
    channel = lax.div(lane, SLOT)
    slot = lax.rem(lane, SLOT)
    if kind == "stem":
        hit = (col == (7 * tap_row + slot) * 3 + channel) & (slot < 7) & (channel < 3)
        return jnp.where(hit, 1.0, 0.0)
    cell = lax.div(slot - 1, 2)
    hit = (col == (3 * tap_row + cell) * 6 + channel) & (slot >= 1) & (slot < 7) & (channel < 6)
    return jnp.where(hit, 0.25, 0.0)


def spread_select():
    w = iota((64, 128), 0)
    lane = iota((64, 128), 1)
    return jnp.where(w == 8 * lax.div(lane, SLOT) + lax.rem(lane, SLOT) - 3, 1.0, 0.0)


def gather_select():
    row = iota((384, 128), 0)
    col = iota((384, 128), 1)
    return jnp.where(col == lax.div(row, 128) * SLOT + lax.rem(row, SLOT), 1.0, 0.0)


def own_block():
    row = iota((8, 128), 0)
    lane = iota((8, 128), 1)
    return jnp.where(lax.div(lane, SLOT) == row, 1.0, 0.0)


def stem_front(
    place, cut, offset, frames, kernel, diff, v_out, sums_out, u_out, u2_out, win_out, win2_out,
    spread, tiles,
):
    valid = valid_scalars(place, cut, offset)
    flat = frames[0].astype(F32).reshape(192, 64)
    spread[...] = dot(flat.astype(BF), spread_select().astype(BF))
    mask = own_block()
    for f in range(8):
        for c in range(3):
            for h in range(8):
                line = f * 24 + c * 8 + h
                tiles[h * 64 + f * 8 : h * 64 + f * 8 + 8, c * 128 : c * 128 + 128] = (
                    jnp.broadcast_to(spread[line : line + 1, :], (8, 128)) * mask
                )
    pixels = dot(tiles[...].astype(BF), gather_select().astype(BF))
    rows = [pixels[64 * h : 64 * h + 64] for h in range(8)]
    gate = frame_column([jnp.float32(0.0)] + valid, 8, 128)
    steps = []
    for h2 in range(4):
        both = rows[2 * h2] + rows[2 * h2 + 1]
        step = (both - jnp.concatenate([jnp.zeros((8, 128), F32), both[:-8]], 0)) * gate
        later = jnp.concatenate([step[8:], jnp.zeros((8, 128), F32)], 0)
        steps.append((step + pltpu.roll(later, 48, 1)).astype(BF))
    rows = [r.astype(BF) for r in rows]
    blank = jnp.zeros((64, 128), BF)
    for dy in range(7):
        for h in range(8):
            source = h + dy - 3
            win_out[64 * h : 64 * h + 64, 128 * dy : 128 * dy + 128] = (
                rows[source] if 0 <= source < 8 else blank
            )
    for dy in range(3):
        for h in range(4):
            source = h + dy - 1
            win2_out[64 * h : 64 * h + 64, 128 * dy : 128 * dy + 128] = (
                steps[source] if 0 <= source < 4 else blank
            )
    low_half = iota((896, 128), 1) < 64
    wide_kernel = jnp.concatenate([kernel[...], kernel[...]], 1)
    placed = dot(window_select(896, 147, "stem").astype(BF), wide_kernel)
    wide_diff = jnp.concatenate([diff[...], diff[...]], 1)
    placed2 = dot(window_select(384, 54, "diff").astype(BF), wide_diff)
    for q in range(4):
        first = pltpu.roll(placed, 2 * q, 0) if q else placed
        second = pltpu.roll(placed, 2 * q + 1, 0)
        u_out[:, 128 * q : 128 * q + 128] = jnp.where(low_half, first, second).astype(BF)
        u2_out[:, 128 * q : 128 * q + 128] = (
            pltpu.roll(placed2, 2 * q, 0) if q else placed2
        ).astype(BF)
    v = dot(win_out[...], u_out[...])
    side = dot(win2_out[...], u2_out[...])
    first = jnp.zeros((1, 512), F32)
    second = jnp.zeros((1, 512), F32)
    for h in range(8):
        piece = v[64 * h : 64 * h + 64] + side[64 * (h // 2) : 64 * (h // 2) + 64]
        v_out[64 * h : 64 * h + 64, :] = piece
        first = first + jnp.sum(piece, 0, keepdims=True)
        second = second + jnp.sum(piece * piece, 0, keepdims=True)
    sums_out[0:1, :] = first
    sums_out[1:2, :] = second


def stem_close(row_total, v, sums, gain, bias, weight, wide_out, red_out, sums_out):
    mean, scale = norm_scale(fold_lanes(sums[...]), row_total)
    factor = scale * gain[...]
    for h in range(8):
        y = (v[64 * h : 64 * h + 64, :] - mean) * factor + bias[...]
        wide_out[
            64 * (h // 4) : 64 * (h // 4) + 64, 512 * (h % 4) : 512 * (h % 4) + 512
        ] = (y * sigmoid(y)).astype(BF)
    red = dot(wide_out[...], weight[...])
    red_out[...] = red
    sums_out[...] = column_sums(red, red * red)


def gate_front(
    row_total, place, cut, offset, red, sums, gain, bias, squeeze, fine, coarse, excite,
    middle, expand, narrow_out, gate_out, fine_rows_out, coarse_rows_out, summed_out, gated_out,
    hpre_out, hidden_out, exp_out, sums_out,
):
    valid = valid_scalars(place, cut, offset)
    mean, scale = norm_scale(sums[...], row_total)
    y = (red[...] - mean) * scale * gain[...] + bias[...]
    narrow = y * sigmoid(y)
    narrow_out[...] = narrow
    squeezed = dot(narrow.astype(BF), squeeze[...])
    keep = frame_column(valid + [jnp.float32(0.0)], 8, 32)
    parts = []
    for hb in range(2):
        part = squeezed[64 * hb : 64 * hb + 64]
        later = jnp.concatenate([part[8:], part[:8]], 0)
        parts.append((later - part) * keep)
    change = jnp.concatenate(parts, 0)
    fine_rows = jnp.concatenate(taps(change), 1).astype(BF)
    pooled = 0.25 * cell_sum(change)
    coarse_rows = jnp.concatenate(coarse_taps(pooled), 1).astype(BF)
    fine_rows_out[...] = fine_rows
    coarse_rows_out[...] = coarse_rows
    summed = (dot(fine_rows, fine[...]) + dot(coarse_rows, coarse[96:192, :])).astype(BF)
    summed_out[...] = summed
    gate = sigmoid(dot(summed, excite[...]))
    gate_out[...] = gate
    gated = narrow * (1.0 + gate)
    gated_out[...] = gated.astype(BF)
    total = jnp.zeros((128, 512), F32)
    for k, piece in enumerate(taps(gated)):
        total = total + dot(piece.astype(BF), middle[k])
    hpre_out[...] = total
    hidden = (total * sigmoid(total)).astype(BF)
    hidden_out[...] = hidden
    expanded = dot(hidden, expand[...])
    exp_out[...] = expanded
    sums_out[...] = column_sums(expanded, expanded * expanded)


def out_back(row_total, place, expanded, sums, gain, bias, wide, cot, og_out, sums_out):
    del place
    mean, scale = norm_scale(sums[...], row_total)
    for hb in range(2):
        part = slice(64 * hb, 64 * hb + 64)
        normal = (expanded[part, :] - mean) * scale
        y = normal * gain[...] + bias[...] + wide[part, :].astype(F32)
        weightless = cot[0, :, hb, :, :].astype(F32).reshape(64, 2048)
        og = weightless * swish_slope(y)
        og_out[part, :] = og
        here = column_sums(og, og * normal)
        if hb == 0:
            sums_out[...] = here
        else:
            sums_out[...] = sums_out[...] + here


def norm_pull(grad, normal, scale, gain, grad_sums, row_total):
    return (
        gain
        * scale
        * (
            grad
            - grad_sums[0:1] * (1.0 / row_total)
            - normal * (grad_sums[1:2] * (1.0 / row_total))
        )
    )


def expand_back(
    row_total, expanded, sums, gain, og, grad_sums, hpre, hidden, gated, expand,
    hg_out, dexpand_out,
):
    mean, scale = norm_scale(sums[...], row_total)
    normal = (expanded[...] - mean) * scale
    dv = norm_pull(og[...], normal, scale, gain[...], grad_sums[...], row_total).astype(BF)
    dhid = dot_nt(dv, expand[...]).astype(BF).astype(F32)
    hg_out[...] = (dhid * swish_slope(hpre[...])).astype(BF)
    dexpand_out[...] = dot_tn(hidden[...], dv).astype(BF)


def gate_back(
    row_total, place, cut, offset, hg, red, sums, gain, bias, narrow, gate, fine_rows,
    coarse_rows, summed, squeeze, fine, coarse, excite, middle, rg_out, sums_out, dsqueeze_out,
    dfine_out, dcoarse_out, dexcite_out,
):
    valid = valid_scalars(place, cut, offset)
    total = jnp.zeros((128, 512), F32)
    for k, piece in enumerate(back_taps(hg[...].astype(F32))):
        total = total + dot_nt(piece.astype(BF), middle[k])
    gg = total.astype(BF).astype(F32)
    gate_v = gate[...]
    narrow_v = narrow[...]
    narrow_grad = gg * (1.0 + gate_v)
    excite_grad = (gg * narrow_v * gate_v * (1.0 - gate_v)).astype(BF)
    dexcite_out[...] = dot_tn(summed[...], excite_grad)
    summed_low = dot_nt(excite_grad, excite[...]).astype(BF)
    summed_grad = summed_low.astype(F32)
    coarse_low = cell_sum(summed_grad).astype(BF)
    dfine_out[...] = dot_tn(fine_rows[...], summed_low)
    dcoarse_out[...] = 0.25 * dot_tn(coarse_rows[...], coarse_low)
    spread = dot_nt(summed_low, fine[...])
    change_grad = jnp.zeros((128, 32), F32)
    for k in range(9):
        change_grad = change_grad + shift_rows(
            spread[:, 32 * k : 32 * k + 32], 1 - k // 3, 1 - k % 3
        )
    spread = dot_nt(coarse_low, coarse[96:192, :])
    pooled_grad = jnp.zeros((128, 32), F32)
    for k in range(3):
        pooled_grad = pooled_grad + shift_rows(spread[:, 32 * k : 32 * k + 32], 0, 2 * (1 - k))
    change_grad = change_grad + 0.25 * pooled_grad
    keep = frame_column(valid + [jnp.float32(0.0)], 8, 32)
    parts = []
    for hb in range(2):
        step = change_grad[64 * hb : 64 * hb + 64] * keep
        earlier = jnp.concatenate([step[56:], step[:56]], 0)
        parts.append(earlier - step)
    squeezed_grad = jnp.concatenate(parts, 0).astype(BF)
    dsqueeze_out[...] = dot_tn(narrow_v.astype(BF), squeezed_grad)
    narrow_grad = narrow_grad + dot_nt(squeezed_grad, squeeze[...])
    mean, scale = norm_scale(sums[...], row_total)
    normal = (red[...] - mean) * scale
    y = normal * gain[...] + bias[...]
    rg = narrow_grad * swish_slope(y)
    rg_out[...] = rg
    sums_out[...] = column_sums(rg, rg * normal)


def middle_weight(gated, hg, out):
    left = gated[...]
    for k, piece in enumerate(back_taps(hg[...].astype(F32))):
        out[k] = dot_tn(left, piece.astype(BF)).astype(BF)


def reduce_back(
    row_total, stem_total, red, sums, gain, rg, grad_sums, wide, og, weight, v, stem_sums,
    stem_gain, stem_bias, rs_out, sums_out, dreduce_out,
):
    mean, scale = norm_scale(sums[...], row_total)
    normal = (red[...] - mean) * scale
    dv = norm_pull(rg[...], normal, scale, gain[...], grad_sums[...], row_total).astype(BF)
    wide_grad = dot_nt(dv, weight[...]) + og[...].astype(BF).astype(F32)
    wide_grad = wide_grad.astype(BF).astype(F32)
    mean, scale = norm_scale(fold_lanes(stem_sums[...]), stem_total)
    first = jnp.zeros((1, 512), F32)
    second = jnp.zeros((1, 512), F32)
    for h in range(8):
        normal = (v[64 * h : 64 * h + 64, :] - mean) * scale
        y = normal * stem_gain[...] + stem_bias[...]
        rs = (
            wide_grad[64 * (h // 4) : 64 * (h // 4) + 64, 512 * (h % 4) : 512 * (h % 4) + 512]
            * swish_slope(y)
        )
        rs_out[64 * h : 64 * h + 64, :] = rs
        first = first + jnp.sum(rs, 0, keepdims=True)
        second = second + jnp.sum(rs * normal, 0, keepdims=True)
    sums_out[0:1, :] = first
    sums_out[1:2, :] = second
    dreduce_out[...] = dot_tn(wide[...], dv).astype(BF)


def stem_back(
    stem_total, place, cut, offset, v, stem_sums, gain, rs, grad_sums, win, win2, u, u2,
    frames_out, kernel_out, diff_out, sums_out, lines,
):
    valid = valid_scalars(place, cut, offset)
    mean, scale = norm_scale(fold_lanes(stem_sums[...]), stem_total)
    totals = fold_lanes(grad_sums[...])
    sums_out[...] = totals
    rows = []
    pairs = []
    for h in range(8):
        part = slice(64 * h, 64 * h + 64)
        normal = (v[part, :] - mean) * scale
        pre = norm_pull(rs[part, :], normal, scale, gain[...], totals, stem_total)
        rows.append(pre.astype(BF))
        if h % 2:
            pairs.append((before + pre).astype(BF))
        before = pre
    dv = jnp.concatenate(rows, 0)
    dside = jnp.concatenate(pairs, 0)

    low_half = iota((896, 128), 1) < 64
    du = dot_tn(win[...], dv)
    placed = jnp.zeros((896, 128), F32)
    for q in range(4):
        part = du[:, 128 * q : 128 * q + 128]
        first = pltpu.roll(part, 896 - 2 * q, 0) if q else part
        placed = placed + jnp.where(low_half, first, pltpu.roll(part, 896 - 2 * q - 1, 0))
    placed = placed + pltpu.roll(placed, 64, 1)
    kernel_out[...] = lax.dot_general(
        window_select(896, 147, "stem"), placed, (((0,), (0,)), ((), ())),
        preferred_element_type=F32, precision=lax.Precision.HIGHEST,
    )[:, :64]
    du2 = dot_tn(win2[...], dside)
    placed = jnp.zeros((384, 128), F32)
    for q in range(4):
        part = du2[:, 128 * q : 128 * q + 128]
        placed = placed + (pltpu.roll(part, 384 - 2 * q, 0) if q else part)
    placed = placed + pltpu.roll(placed, 64, 1)
    diff_out[...] = lax.dot_general(
        window_select(384, 54, "diff"), placed, (((0,), (0,)), ((), ())),
        preferred_element_type=F32, precision=lax.Precision.HIGHEST,
    )[:, :64]

    dwin = dot_nt(dv, u[...])
    dwin2 = dot_nt(dside, u2[...])
    gate = frame_column([jnp.float32(0.0)] + valid, 8, 128)
    steps = []
    for h2 in range(4):
        total = jnp.zeros((64, 128), F32)
        for dy in range(3):
            target = h2 + 1 - dy
            if 0 <= target < 4:
                total = total + dwin2[64 * target : 64 * target + 64, 128 * dy : 128 * dy + 128]
        later = pltpu.roll(total, 80, 1)
        later = jnp.concatenate([jnp.zeros((8, 128), F32), later[:-8]], 0)
        step = (total + later) * gate
        steps.append(step - jnp.concatenate([step[8:], jnp.zeros((8, 128), F32)], 0))
    pixels = []
    for h in range(8):
        total = steps[h // 2]
        for dy in range(7):
            target = h + 3 - dy
            if 0 <= target < 8:
                total = total + dwin[64 * target : 64 * target + 64, 128 * dy : 128 * dy + 128]
        pixels.append(total)
    pixels = jnp.concatenate(pixels, 0)
    back = lax.dot_general(
        pixels, gather_select(), (((1,), (1,)), ((), ())),
        preferred_element_type=F32, precision=lax.Precision.HIGHEST,
    )
    mask = own_block()
    for f in range(8):
        for c in range(3):
            for h in range(8):
                line = f * 24 + c * 8 + h
                block = back[h * 64 + f * 8 : h * 64 + f * 8 + 8, c * 128 : c * 128 + 128]
                lines[line : line + 1, :] = jnp.sum(block * mask, 0, keepdims=True)
    flat = lax.dot_general(
        lines[...], spread_select(), (((1,), (1,)), ((), ())),
        preferred_element_type=F32, precision=lax.Precision.HIGHEST,
    )
    frames_out[...] = flat.reshape(8, 3, 8, 64)


def shape(dims, dtype=F32):
    return jax.ShapeDtypeStruct(dims, dtype)


def whole(dims):
    count = len(dims)
    return pl.BlockSpec(dims, lambda i, *scalars: (0,) * count)


def run(kernel, outs, arrays, scalars=(), scratch=(), clip=None, cost=1_000_000):
    in_specs = []
    for position, array in enumerate(arrays):
        if position == clip:
            rest = len(array.shape) - 1
            in_specs.append(
                pl.BlockSpec(
                    (1,) + array.shape[1:], lambda i, place, *more: (place[0],) + (0,) * rest
                )
            )
        else:
            in_specs.append(whole(array.shape))
    return pl.pallas_call(
        kernel,
        grid_spec=pltpu.PrefetchScalarGridSpec(
            num_scalar_prefetch=len(scalars),
            grid=(1,),
            in_specs=in_specs,
            out_specs=[whole(o.shape) for o in outs],
            scratch_shapes=scratch,
        ),
        out_shape=outs,
        compiler_params=pltpu.CompilerParams(vmem_limit_bytes=50 * 1024 * 1024),
        cost_estimate=pl.CostEstimate(flops=cost, bytes_accessed=cost, transcendentals=0),
    )(*scalars, *arrays)


def swap_sum(value, axis):
    count = lax.axis_size(axis)
    distance = 1
    while distance < count:
        route = [(i, i ^ distance) for i in range(count)]
        value = value + lax.ppermute(value, axis, route)
        distance *= 2
    return value


def body(
    frames,
    cut_mask,
    offsets,
    stem_kernel,
    diff_kernel,
    stem_gain,
    stem_bias,
    reduce_weight,
    reduce_gain,
    reduce_bias,
    squeeze_weight,
    fine_kernel,
    coarse_kernel,
    excite_weight,
    middle_kernel,
    expand_weight,
    expand_gain,
    expand_bias,
    cotangent,
):
    groups = lax.axis_size("dp")
    assert frames.shape[0] == MICRO == lax.axis_size("pipe")
    stem_total = float(4096 * groups)
    row_total = float(128 * groups)
    place = lax.axis_index("pipe").astype(jnp.int32).reshape(1)
    scalars = (place, cut_mask, offsets)
    diff_flat = diff_kernel.reshape(54, STEM)
    fine_flat = fine_kernel.reshape(288, 32)
    coarse_flat = coarse_kernel.reshape(288, 32)
    gain_s = jnp.tile(stem_gain, 8)[None]
    bias_s = jnp.tile(stem_bias, 8)[None]
    gain_r = reduce_gain[None]
    bias_r = reduce_bias[None]
    gain_x = expand_gain[None]
    bias_x = expand_bias[None]

    v, stem_sums, u, u2, win, win2 = run(
        stem_front,
        [
            shape((512, 512)),
            shape((2, 512)),
            shape((896, 512), BF),
            shape((384, 512), BF),
            shape((512, 896), BF),
            shape((256, 384), BF),
        ],
        (frames, stem_kernel, diff_flat),
        scalars,
        [pltpu.VMEM((192, 128), F32), pltpu.VMEM((512, 384), F32)],
        clip=0,
    )
    stem_sums = swap_sum(stem_sums, "dp")
    wide, red, red_sums = run(
        functools.partial(stem_close, stem_total),
        [shape((128, 2048), BF), shape((128, 512)), shape((2, 512))],
        (v, stem_sums, gain_s, bias_s, reduce_weight),
    )
    red_sums = swap_sum(red_sums, "dp")
    (
        narrow, gate, fine_rows, coarse_rows, summed, gated, hpre, hidden, expanded, exp_sums
    ) = run(
        functools.partial(gate_front, row_total),
        [
            shape((128, 512)),
            shape((128, 512)),
            shape((128, 288), BF),
            shape((128, 96), BF),
            shape((128, 32), BF),
            shape((128, 512), BF),
            shape((128, 512)),
            shape((128, 512), BF),
            shape((128, 2048)),
            shape((2, 2048)),
        ],
        (
            red, red_sums, gain_r, bias_r, squeeze_weight, fine_flat, coarse_flat, excite_weight,
            middle_kernel, expand_weight,
        ),
        scalars,
    )
    exp_sums = swap_sum(exp_sums, "dp")
    og, og_sums = run(
        functools.partial(out_back, row_total),
        [shape((128, 2048)), shape((2, 2048))],
        (expanded, exp_sums, gain_x, bias_x, wide, cotangent),
        (place,),
        clip=5,
    )
    og_sums = swap_sum(og_sums, "dp")
    hg, dexpand = run(
        functools.partial(expand_back, row_total),
        [shape((128, 512), BF), shape((512, 2048), BF)],
        (expanded, exp_sums, gain_x, og, og_sums, hpre, hidden, gated, expand_weight),
    )
    rg, rg_sums, dsqueeze, dfine, dcoarse, dexcite = run(
        functools.partial(gate_back, row_total),
        [
            shape((128, 512)),
            shape((2, 512)),
            shape((512, 32)),
            shape((288, 32)),
            shape((96, 32)),
            shape((32, 512)),
        ],
        (
            hg, red, red_sums, gain_r, bias_r, narrow, gate, fine_rows, coarse_rows, summed,
            squeeze_weight, fine_flat, coarse_flat, excite_weight, middle_kernel,
        ),
        scalars,
    )
    (dmiddle,) = run(middle_weight, [shape((9, 512, 512), BF)], (gated, hg))
    rg_sums = swap_sum(rg_sums, "dp")
    rs, rs_sums, dreduce = run(
        functools.partial(reduce_back, row_total, stem_total),
        [shape((512, 512)), shape((2, 512)), shape((2048, 512), BF)],
        (
            red, red_sums, gain_r, rg, rg_sums, wide, og, reduce_weight, v, stem_sums, gain_s,
            bias_s,
        ),
    )
    rs_sums = swap_sum(rs_sums, "dp")
    frame_grad, dstem, ddiff, stem_totals = run(
        functools.partial(stem_back, stem_total),
        [shape((8, 3, 8, 64)), shape((147, 64)), shape((54, 64)), shape((2, 512))],
        (v, stem_sums, gain_s, rs, rs_sums, win, win2, u, u2),
        scalars,
        [pltpu.VMEM((192, 128), F32)],
    )
    everyone = ("dp", "pipe")
    dmiddle = lax.psum(dmiddle, everyone).astype(F32)
    dexpand = lax.psum(dexpand, everyone).astype(F32)
    dreduce = lax.psum(dreduce, everyone).astype(F32)
    dstem, ddiff, dsqueeze, dfine, dcoarse, dexcite = lax.psum(
        (dstem, ddiff, dsqueeze, dfine, dcoarse, dexcite), everyone
    )
    og_all, rg_all, rs_all = lax.psum((og_sums, rg_sums, stem_totals), "pipe")
    dcoarse = jnp.pad(dcoarse, ((96, 96), (0, 0)))
    return (
        frame_grad[None],
        dstem,
        ddiff.reshape(9, 6, STEM),
        rs_all[1, :STEM],
        rs_all[0, :STEM],
        dreduce,
        rg_all[1],
        rg_all[0],
        dsqueeze,
        dfine.reshape(9, 32, 32),
        dcoarse.reshape(9, 32, 32),
        dexcite,
        dmiddle,
        dexpand,
        og_all[1],
        og_all[0],
    )


def solution(mesh):
    copied = P()
    by_group = P("dp")
    in_specs = (by_group,) * 3 + (copied,) * 15 + (by_group,)
    out_specs = (P(("dp", "pipe")),) + (copied,) * 15
    return jax.shard_map(body, mesh=mesh, in_specs=in_specs, out_specs=out_specs, check_vma=False)
```

```python
import functools

import jax
import jax.numpy as jnp
from jax import lax
from jax.experimental import pallas as pl
from jax.experimental.pallas import tpu as pltpu
from jax.sharding import PartitionSpec as P

FRAMES = 8
MICRO = 4
EPSILON = 1e-05
COST = 1_000_000
VMEM_BYTES = 32 * 1024 * 1024
BF = jnp.bfloat16
F32 = jnp.float32

STEM = 64
SLOT = 16


def dot(left, right):
    return jnp.dot(left, right, preferred_element_type=F32)


def dot_nt(left, right):
    return lax.dot_general(left, right, (((1,), (1,)), ((), ())), preferred_element_type=F32)


def dot_tn(left, right):
    return lax.dot_general(left, right, (((0,), (0,)), ((), ())), preferred_element_type=F32)


def dot_exact(left, right):
    return jnp.dot(left, right, preferred_element_type=F32, precision=lax.Precision.HIGHEST)


def iota(shape, dim):
    return lax.broadcasted_iota(jnp.int32, shape, dim)


def sigmoid(v):
    return 1.0 / (1.0 + jnp.exp(-v))


def swish_slope(v):
    s = sigmoid(v)
    return s * (1.0 + v * (1.0 - s))


def valid_scalars(place_ref, cut_ref, offset_ref):
    clip = place_ref[0]
    stop = offset_ref[clip]
    return [
        jnp.where(stop == t + 1, 0, cut_ref[clip, t]).astype(F32) for t in range(FRAMES - 1)
    ]


def keep_column(pack, lanes):
    rows = pack[192:208, :].astype(F32)
    return jnp.concatenate(
        [jnp.broadcast_to(rows[f : f + 1, :lanes], (8, lanes)) for f in range(FRAMES)], 0
    )


def gate_column(pack):
    keep = keep_column(pack, 64)
    both = jnp.concatenate([keep, keep], 1)
    return jnp.concatenate([jnp.zeros((8, 128), F32), both[:-8]], 0)


def pack_clip(place, cut, offset, frames, out):
    valid = valid_scalars(place, cut, offset)
    flat = frames[0].astype(F32).reshape(192, 64)
    rows = [jnp.full((1, 64), s, F32) for s in valid] + [jnp.zeros((9, 64), F32)]
    out[...] = jnp.concatenate([flat] + rows, 0).astype(BF)


def summed_up(pieces):
    value = pieces[0][...]
    for piece in pieces[1:]:
        value = value + piece[...]
    return value


def spread_sums(out, first, second):
    out[...] = jnp.concatenate([first, second], 0)


def norm_scale(sums, row_total):
    mean = sums[0:1] * (1.0 / row_total)
    variance = sums[1:2] * (1.0 / row_total) - mean * mean
    return mean, lax.rsqrt(variance + EPSILON)


def column_sums(out, first, second):
    spread_sums(out, jnp.sum(first, 0, keepdims=True), jnp.sum(second, 0, keepdims=True))


def fold_lanes(sums):
    for step in (64, 128, 256):
        sums = sums + pltpu.roll(sums, step, 1)
    return sums


def shift_rows(v, dy, dx):
    rows = v.shape[0]
    if dx:
        rolled = pltpu.roll(v, (-dx) % rows, 0)
        wb = lax.rem(iota(v.shape, 0), 8)
        v = jnp.where((wb + dx >= 0) & (wb + dx < 8), rolled, 0.0)
    half = rows // 2
    if dy == 1:
        v = jnp.concatenate([v[half:], jnp.zeros_like(v[half:])], 0)
    elif dy == -1:
        v = jnp.concatenate([jnp.zeros_like(v[:half]), v[:half]], 0)
    return v


def cell_sum(v):
    half = v.shape[0] // 2
    both = v[:half] + v[half:]
    even = lax.rem(iota(both.shape, 0), 2) == 0
    both = both + jnp.where(even, pltpu.roll(both, half - 1, 0), pltpu.roll(both, 1, 0))
    return jnp.concatenate([both, both], 0)


def taps(v):
    return [shift_rows(v, ky - 1, kx - 1) for ky in range(3) for kx in range(3)]


def back_taps(v):
    return [shift_rows(v, 1 - ky, 1 - kx) for ky in range(3) for kx in range(3)]


def coarse_taps(v):
    return [shift_rows(v, 0, 2 * (k - 1)) for k in range(3)]


def window_select(rows, cols, kind):
    place = iota((rows, cols), 0)
    col = iota((rows, cols), 1)
    lane = lax.rem(place, 128)
    tap_row = lax.div(place, 128)
    channel = lax.div(lane, SLOT)
    slot = lax.rem(lane, SLOT)
    if kind == "stem":
        hit = (col == (7 * tap_row + slot) * 3 + channel) & (slot < 7) & (channel < 3)
        return jnp.where(hit, 1.0, 0.0)
    cell = lax.div(slot - 1, 2)
    hit = (col == (3 * tap_row + cell) * 6 + channel) & (slot >= 1) & (slot < 7) & (channel < 6)
    return jnp.where(hit, 0.25, 0.0)


def spread_select():
    w = iota((64, 128), 0)
    lane = iota((64, 128), 1)
    return jnp.where(w == 8 * lax.div(lane, SLOT) + lax.rem(lane, SLOT) - 3, 1.0, 0.0)


def gather_select():
    row = iota((384, 128), 0)
    col = iota((384, 128), 1)
    return jnp.where(col == lax.div(row, 128) * SLOT + lax.rem(row, SLOT), 1.0, 0.0)


def own_block():
    row = iota((8, 128), 0)
    lane = iota((8, 128), 1)
    return jnp.where(lax.div(lane, SLOT) == row, 1.0, 0.0)


def stem_windows(pack, kernel, diff, win, win2, u, u2, spread, tiles):
    spread[...] = dot(pack[0:192, :], spread_select().astype(BF))
    mask = own_block()
    for f in range(8):
        for c in range(3):
            for h in range(8):
                line = f * 24 + c * 8 + h
                tiles[h * 64 + f * 8 : h * 64 + f * 8 + 8, c * 128 : c * 128 + 128] = (
                    jnp.broadcast_to(spread[line : line + 1, :], (8, 128)) * mask
                )
    pixels = dot(tiles[...].astype(BF), gather_select().astype(BF))
    rows = [pixels[64 * h : 64 * h + 64] for h in range(8)]
    gate = gate_column(pack)
    steps = []
    for h2 in range(4):
        both = rows[2 * h2] + rows[2 * h2 + 1]
        step = (both - jnp.concatenate([jnp.zeros((8, 128), F32), both[:-8]], 0)) * gate
        later = jnp.concatenate([step[8:], jnp.zeros((8, 128), F32)], 0)
        steps.append((step + pltpu.roll(later, 48, 1)).astype(BF))
    rows = [r.astype(BF) for r in rows]
    blank = jnp.zeros((64, 128), BF)
    for dy in range(7):
        for h in range(8):
            source = h + dy - 3
            win[64 * h : 64 * h + 64, 128 * dy : 128 * dy + 128] = (
                rows[source] if 0 <= source < 8 else blank
            )
    for dy in range(3):
        for h in range(4):
            source = h + dy - 1
            win2[64 * h : 64 * h + 64, 128 * dy : 128 * dy + 128] = (
                steps[source] if 0 <= source < 4 else blank
            )
    low_half = iota((896, 128), 1) < 64
    wide_kernel = jnp.concatenate([kernel[...], kernel[...]], 0)
    placed = dot_nt(window_select(896, 147, "stem").astype(BF), wide_kernel)
    wide_diff = jnp.concatenate([diff[...], diff[...]], 1)
    placed2 = dot(window_select(384, 54, "diff").astype(BF), wide_diff)
    for q in range(4):
        first = pltpu.roll(placed, 2 * q, 0) if q else placed
        second = pltpu.roll(placed, 2 * q + 1, 0)
        u[:, 128 * q : 128 * q + 128] = jnp.where(low_half, first, second).astype(BF)
        u2[:, 128 * q : 128 * q + 128] = (
            pltpu.roll(placed2, 2 * q, 0) if q else placed2
        ).astype(BF)


def stem_front(pack, kernel, diff, v_out, sums_out, win, win2, u, u2, spread, tiles):
    stem_windows(pack, kernel, diff, win, win2, u, u2, spread, tiles)
    v = dot(win[...], u[...])
    side = dot(win2[...], u2[...])
    first = jnp.zeros((1, 512), F32)
    second = jnp.zeros((1, 512), F32)
    for h in range(8):
        piece = v[64 * h : 64 * h + 64] + side[64 * (h // 2) : 64 * (h // 2) + 64]
        v_out[64 * h : 64 * h + 64, :] = piece
        first = first + jnp.sum(piece, 0, keepdims=True)
        second = second + jnp.sum(piece * piece, 0, keepdims=True)
    spread_sums(sums_out, first, second)


def stem_close(row_total, v, sums, gain, bias, weight, wide_out, red_out, sums_out):
    mean, scale = norm_scale(fold_lanes(summed_up(sums)), row_total)
    factor = scale * gain[...]
    for h in range(8):
        y = (v[64 * h : 64 * h + 64, :] - mean) * factor + bias[...]
        wide_out[
            64 * (h // 4) : 64 * (h // 4) + 64, 512 * (h % 4) : 512 * (h % 4) + 512
        ] = (y * sigmoid(y)).astype(BF)
    red = dot(wide_out[...], weight[...])
    red_out[...] = red
    column_sums(sums_out, red, red * red)


def gate_path(pack, narrow, squeeze, fine, coarse, excite):
    squeezed = dot_nt(narrow.astype(BF), squeeze[...])
    keep = keep_column(pack, 32)
    parts = []
    for hb in range(2):
        part = squeezed[64 * hb : 64 * hb + 64]
        later = jnp.concatenate([part[8:], part[:8]], 0)
        parts.append((later - part) * keep)
    change = jnp.concatenate(parts, 0)
    fine_rows = jnp.concatenate(taps(change), 1).astype(BF)
    pooled = 0.25 * cell_sum(change)
    coarse_rows = jnp.concatenate(coarse_taps(pooled), 1).astype(BF)
    summed = (dot(fine_rows, fine[...]) + dot(coarse_rows, coarse[96:192, :])).astype(BF)
    return fine_rows, coarse_rows, summed, sigmoid(dot(summed, excite[...]))


def gate_front(
    row_total, pack, red, sums, gain, bias, squeeze, fine, coarse, excite, middle, expand,
    hpre_out, both_out, exp_out, sums_out,
):
    mean, scale = norm_scale(summed_up(sums), row_total)
    y = (red[...] - mean) * scale * gain[...] + bias[...]
    narrow = y * sigmoid(y)
    gate = gate_path(pack, narrow, squeeze, fine, coarse, excite)[3]
    gated = narrow * (1.0 + gate)
    total = jnp.zeros((128, 512), F32)
    for k, piece in enumerate(taps(gated)):
        total = total + dot(piece.astype(BF), middle[k])
    hpre_out[...] = total
    hidden = (total * sigmoid(total)).astype(BF)
    for half in range(2):
        part = slice(256 * half, 256 * half + 256)
        both_out[:, 512 * half : 512 * half + 256] = gated[:, part].astype(BF)
        both_out[:, 512 * half + 256 : 512 * half + 512] = hidden[:, part]
    expanded = dot(hidden, expand[...])
    exp_out[...] = expanded
    column_sums(sums_out, expanded, expanded * expanded)


def out_back(row_total, expanded, sums, gain, bias, wide, cot, og_out, sums_out):
    mean, scale = norm_scale(summed_up(sums), row_total)
    first = jnp.zeros((1, 2048), F32)
    second = jnp.zeros((1, 2048), F32)
    for hb in range(2):
        part = slice(64 * hb, 64 * hb + 64)
        normal = (expanded[part, :] - mean) * scale
        y = normal * gain[...] + bias[...] + wide[part, :].astype(F32)
        weightless = cot[:, hb, :, :].astype(F32).reshape(64, 2048)
        og = weightless * swish_slope(y)
        og_out[part, :] = og
        first = first + jnp.sum(og, 0, keepdims=True)
        second = second + jnp.sum(og * normal, 0, keepdims=True)
    spread_sums(sums_out, first, second)


def norm_pull(grad, normal, scale, gain, grad_sums, row_total):
    return (
        gain
        * scale
        * (
            grad
            - grad_sums[0:1] * (1.0 / row_total)
            - normal * (grad_sums[1:2] * (1.0 / row_total))
        )
    )


def block_order(info, partner=False):
    block = 2 * info[1] + info[2]
    first = jnp.where((info[0] == 0) != partner, 2, 1)
    return [block, block ^ first, block ^ (3 - first), block ^ 3]


def lanes(start, width):
    return pl.ds(pl.multiple_of(start, 128), width)


def expand_back(
    row_total, info, expanded, sums, gain, og, grad_sums, hpre, expand, hg_out, *rest
):
    outs, (hg_scratch, dv_scratch) = rest[:4], rest[4:]
    mean, scale = norm_scale(summed_up(sums), row_total)
    normal = (expanded[...] - mean) * scale
    dv = norm_pull(og[...], normal, scale, gain[...], summed_up(grad_sums), row_total).astype(BF)
    dv_scratch[...] = dv
    dhid = dot_nt(dv, expand[...]).astype(BF).astype(F32)
    hg = (dhid * swish_slope(hpre[...])).astype(BF)
    hg_out[...] = hg
    hg_scratch[...] = hg
    for out, block in zip(outs, block_order(info)):
        out[:, :128] = hg_scratch[:, lanes(128 * block, 128)]
        out[:, 128:] = dv_scratch[:, lanes(512 * block, 512)]


def all_rows(refs):
    return jnp.concatenate([ref[...] for ref in refs], 0)


def depth_index(info, count):
    return sum(info[3 + b] << b for b in range(bit_count(count)))


def depth_parts(info, scratch, base, outs):
    rows = outs[0].shape[0]
    z = depth_index(info, len(outs))
    for m, out in enumerate(outs):
        out[...] = scratch[pl.ds(pl.multiple_of(base + (z ^ m) * rows, 16), rows), :]


def middle_weights(info, left_refs, right_refs, *rest):
    outs, (scratch,) = rest[:-1], rest[-1:]
    left = jnp.concatenate([ref[:, :256] for ref in left_refs], 0).T
    clips = [
        back_taps(ref[128 * k : 128 * k + 128, :128].astype(F32))
        for ref in right_refs
        for k in range(4)
    ]
    for k in range(9):
        right = jnp.concatenate([clip[k] for clip in clips], 0).astype(BF)
        scratch[256 * k : 256 * k + 256, :] = dot(left, right).astype(BF)
    if scratch.shape[0] > 2304:
        scratch[2304:, :] = jnp.zeros((scratch.shape[0] - 2304, 128), BF)
    depth_parts(info, scratch, 0, outs)


def outer_weights(info, left_refs, right_refs, wide, late, *rest):
    outs, (scratch,) = rest[:-1], rest[-1:]
    left = jnp.concatenate([ref[:, 256:] for ref in left_refs], 0)
    right = jnp.concatenate([ref[:, 128:] for ref in right_refs], 0)
    result = dot_tn(left, right).astype(BF)
    for q in range(4):
        scratch[256 * q : 256 * q + 256, :] = result[:, 128 * q : 128 * q + 128]
    right = jnp.concatenate([ref[:, :128] for ref in late], 0)
    scratch[1024:2048, :] = dot_tn(all_rows(wide), right).astype(BF)
    small = [late[0][128 * k : 128 * k + 128, 128:].astype(F32) for k in range(4)]
    scratch[2048:2176, :] = sum(small).astype(BF)
    if scratch.shape[0] > 2176:
        scratch[2176:, :] = jnp.zeros((scratch.shape[0] - 2176, 128), BF)
    depth_parts(info, scratch, 0, outs)


def stack_rows(*refs):
    out = refs[-1]
    start = 0
    for ref in refs[:-1]:
        out[start : start + ref.shape[0], :] = ref[...]
        start += ref.shape[0]


def stack_depth(info, *refs):
    out = refs[-1]
    rows = refs[0].shape[0]
    z = depth_index(info, len(refs) - 1)
    for m, ref in enumerate(refs[:-1]):
        out[pl.ds(pl.multiple_of((z ^ m) * rows, 16), rows), :] = ref[...]


def gate_back(
    row_total, pack, hg, red, sums, gain, bias, squeeze, fine, coarse, excite, middle,
    rg_out, sums_out, small_out,
):
    mean, scale = norm_scale(summed_up(sums), row_total)
    normal = (red[...] - mean) * scale
    y = normal * gain[...] + bias[...]
    narrow_v = y * sigmoid(y)
    fine_rows, coarse_rows, summed, gate_v = gate_path(
        pack, narrow_v, squeeze, fine, coarse, excite
    )
    total = jnp.zeros((128, 512), F32)
    for k, piece in enumerate(back_taps(hg[...].astype(F32))):
        total = total + dot_nt(piece.astype(BF), middle[k])
    gg = total.astype(BF).astype(F32)
    narrow_grad = gg * (1.0 + gate_v)
    excite_grad = (gg * narrow_v * gate_v * (1.0 - gate_v)).astype(BF)
    dexcite = dot_tn(summed, excite_grad)
    summed_low = dot_nt(excite_grad, excite[...]).astype(BF)
    summed_grad = summed_low.astype(F32)
    coarse_low = cell_sum(summed_grad).astype(BF)
    dfine = dot_tn(fine_rows, summed_low)
    dcoarse = 0.25 * dot_tn(coarse_rows, coarse_low)
    spread = dot_nt(summed_low, fine[...])
    change_grad = jnp.zeros((128, 32), F32)
    for k in range(9):
        change_grad = change_grad + shift_rows(
            spread[:, 32 * k : 32 * k + 32], 1 - k // 3, 1 - k % 3
        )
    spread = dot_nt(coarse_low, coarse[96:192, :])
    pooled_grad = jnp.zeros((128, 32), F32)
    for k in range(3):
        pooled_grad = pooled_grad + shift_rows(spread[:, 32 * k : 32 * k + 32], 0, 2 * (1 - k))
    change_grad = change_grad + 0.25 * pooled_grad
    keep = keep_column(pack, 32)
    parts = []
    for hb in range(2):
        step = change_grad[64 * hb : 64 * hb + 64] * keep
        earlier = jnp.concatenate([step[56:], step[:56]], 0)
        parts.append(earlier - step)
    squeezed_grad = jnp.concatenate(parts, 0).astype(BF)
    dsqueeze = dot_tn(squeezed_grad, narrow_v.astype(BF))
    narrow_grad = narrow_grad + dot(squeezed_grad, squeeze[...])
    rg = narrow_grad * swish_slope(y)
    rg_out[...] = rg
    column_sums(sums_out, rg, rg * normal)
    small_out[0:32, :] = dsqueeze[:, :256]
    small_out[32:64, :] = dsqueeze[:, 256:]
    small_out[64:96, :] = dexcite[:, :256]
    small_out[96:128, :] = dexcite[:, 256:]
    pieces = [dfine[32 * k : 32 * k + 32] for k in range(9)]
    pieces += [dcoarse[32 * k : 32 * k + 32] for k in range(3)]
    small_out[128:160, :] = jnp.concatenate(pieces[:8], 1)
    small_out[160:192, :] = jnp.concatenate(pieces[8:] + [jnp.zeros((32, 128), F32)], 1)
    small_out[192:256, :] = jnp.zeros((64, 256), F32)


def reduce_back(
    row_total, stem_total, info, small, red, sums, gain, rg, grad_sums, og, weight, v, stem_sums,
    stem_gain, stem_bias, rs_out, sums_out, dv0, dv1, dv2, dv3, dv_scratch,
):
    mean, scale = norm_scale(summed_up(sums), row_total)
    normal = (red[...] - mean) * scale
    dv = norm_pull(rg[...], normal, scale, gain[...], summed_up(grad_sums), row_total).astype(BF)
    dv_scratch[...] = dv
    for out, block in zip((dv0, dv1, dv2, dv3), block_order(info)):
        out[:, :128] = dv_scratch[:, lanes(128 * block, 128)]
        part = small[pl.ds(pl.multiple_of(64 * block, 64), 64), :].astype(BF)
        out[:64, 128:] = part[:, :128]
        out[64:, 128:] = part[:, 128:]
    wide_grad = dot_nt(dv, weight[...]) + og[...].astype(BF).astype(F32)
    wide_grad = wide_grad.astype(BF).astype(F32)
    mean, scale = norm_scale(fold_lanes(summed_up(stem_sums)), stem_total)
    first = jnp.zeros((1, 512), F32)
    second = jnp.zeros((1, 512), F32)
    for h in range(8):
        normal = (v[64 * h : 64 * h + 64, :] - mean) * scale
        y = normal * stem_gain[...] + stem_bias[...]
        rs = (
            wide_grad[64 * (h // 4) : 64 * (h // 4) + 64, 512 * (h % 4) : 512 * (h % 4) + 512]
            * swish_slope(y)
        )
        rs_out[64 * h : 64 * h + 64, :] = rs
        first = first + jnp.sum(rs, 0, keepdims=True)
        second = second + jnp.sum(rs * normal, 0, keepdims=True)
    spread_sums(sums_out, first, second)


def stem_back(
    stem_total, share, pack, kernel, diff, v, stem_sums, gain, rs, grad_sums, og_sums,
    rg_sums, frames_out, tail_out, win, win2, u, u2, lines, tiles,
):
    stem_windows(pack, kernel, diff, win, win2, u, u2, lines, tiles)
    mean, scale = norm_scale(fold_lanes(summed_up(stem_sums)), stem_total)
    totals = fold_lanes(summed_up(grad_sums))
    rows = []
    pairs = []
    for h in range(8):
        part = slice(64 * h, 64 * h + 64)
        normal = (v[part, :] - mean) * scale
        pre = norm_pull(rs[part, :], normal, scale, gain[...], totals, stem_total)
        rows.append(pre.astype(BF))
        if h % 2:
            pairs.append((before + pre).astype(BF))
        before = pre
    dv = jnp.concatenate(rows, 0)
    dside = jnp.concatenate(pairs, 0)

    low_half = iota((896, 128), 1) < 64
    du = dot_tn(win[...], dv)
    placed = jnp.zeros((896, 128), F32)
    for q in range(4):
        part = du[:, 128 * q : 128 * q + 128]
        first = pltpu.roll(part, 896 - 2 * q, 0) if q else part
        placed = placed + jnp.where(low_half, first, pltpu.roll(part, 896 - 2 * q - 1, 0))
    placed = placed + pltpu.roll(placed, 64, 1)
    tail_out[0:147, 0:64] = lax.dot_general(
        window_select(896, 147, "stem"), placed, (((0,), (0,)), ((), ())),
        preferred_element_type=F32, precision=lax.Precision.HIGHEST,
    )[:, :64]
    du2 = dot_tn(win2[...], dside)
    placed = jnp.zeros((384, 128), F32)
    for q in range(4):
        part = du2[:, 128 * q : 128 * q + 128]
        placed = placed + (pltpu.roll(part, 384 - 2 * q, 0) if q else part)
    placed = placed + pltpu.roll(placed, 64, 1)
    tail_out[0:54, 64:128] = lax.dot_general(
        window_select(384, 54, "diff"), placed, (((0,), (0,)), ((), ())),
        preferred_element_type=F32, precision=lax.Precision.HIGHEST,
    )[:, :64]

    dwin = dot_nt(dv, u[...])
    dwin2 = dot_nt(dside, u2[...])
    gate = gate_column(pack)
    steps = []
    for h2 in range(4):
        total = jnp.zeros((64, 128), F32)
        for dy in range(3):
            target = h2 + 1 - dy
            if 0 <= target < 4:
                total = total + dwin2[64 * target : 64 * target + 64, 128 * dy : 128 * dy + 128]
        later = pltpu.roll(total, 80, 1)
        later = jnp.concatenate([jnp.zeros((8, 128), F32), later[:-8]], 0)
        step = (total + later) * gate
        steps.append(step - jnp.concatenate([step[8:], jnp.zeros((8, 128), F32)], 0))
    pixels = []
    for h in range(8):
        total = steps[h // 2]
        for dy in range(7):
            target = h + 3 - dy
            if 0 <= target < 8:
                total = total + dwin[64 * target : 64 * target + 64, 128 * dy : 128 * dy + 128]
        pixels.append(total)
    pixels = jnp.concatenate(pixels, 0)
    back = lax.dot_general(
        pixels, gather_select(), (((1,), (1,)), ((), ())),
        preferred_element_type=F32, precision=lax.Precision.HIGHEST,
    )
    mask = own_block()
    for f in range(8):
        for c in range(3):
            for h in range(8):
                line = f * 24 + c * 8 + h
                block = back[h * 64 + f * 8 : h * 64 + f * 8 + 8, c * 128 : c * 128 + 128]
                lines[line : line + 1, :] = jnp.sum(block * mask, 0, keepdims=True)
    flat = lax.dot_general(
        lines[...], spread_select(), (((1,), (1,)), ((), ())),
        preferred_element_type=F32, precision=lax.Precision.HIGHEST,
    )
    frames_out[...] = flat.reshape(8, 3, 8, 64)
    og_all = summed_up(og_sums)
    rg_all = summed_up(rg_sums)
    for q in range(16):
        tail_out[152 + 2 * q : 154 + 2 * q, :] = og_all[:, 128 * q : 128 * q + 128] * share
    for q in range(4):
        tail_out[184 + 2 * q : 186 + 2 * q, :] = rg_all[:, 128 * q : 128 * q + 128] * share
    tail_out[192:194, :] = totals[:, :128] * share


def unpack_tail(
    pieces, stem_out, diff_out, gain_s, bias_s, gain_r, bias_r, gain_x, bias_x
):
    tail = sum(piece[...] for piece in pieces)
    stem_out[...] = tail[0:152].T[0:64, 0:147]
    for k in range(9):
        diff_out[k] = tail[6 * k : 6 * k + 6, 64:128]
    for q in range(16):
        bias_x[:, 128 * q : 128 * q + 128] = tail[152 + 2 * q : 153 + 2 * q, :]
        gain_x[:, 128 * q : 128 * q + 128] = tail[153 + 2 * q : 154 + 2 * q, :]
    for q in range(4):
        bias_r[:, 128 * q : 128 * q + 128] = tail[184 + 2 * q : 185 + 2 * q, :]
        gain_r[:, 128 * q : 128 * q + 128] = tail[185 + 2 * q : 186 + 2 * q, :]
    bias_s[...] = tail[192:193, :64]
    gain_s[...] = tail[193:194, :64]


def finish_blocks(place, own, other, out):
    bit = place[0]
    lead = (0,) * (len(out.shape) - 2)
    out[lead + (slice(None), pl.ds(pl.multiple_of(256 * bit, 128), 256))] = own[...].astype(F32)
    out[lead + (slice(None), pl.ds(pl.multiple_of(256 * (1 - bit), 128), 256))] = (
        other[...].astype(F32)
    )


def place_blocks(info, pieces, out, row, width, base, partner):
    rows = row.size if isinstance(row, pl.Slice) else out.shape[-2]
    for piece, block in zip(pieces, block_order(info, partner)):
        for q in range(width):
            tile = piece[base + rows * q : base + rows * q + rows, :]
            out[row, lanes(128 * (width * block + q), 128)] = tile.astype(F32)


def finish_middle(info, *refs):
    out = refs[-1]
    for pieces, bit, partner in ((refs[:4], info[0], False), (refs[4:8], 1 - info[0], True)):
        for tap in range(out.shape[0]):
            row = pl.ds(pl.multiple_of(256 * bit, 128), 256)
            place_blocks(info, pieces, out.at[tap], row, 1, 256 * tap, partner)


def finish_half(width, info, *refs):
    out = refs[-1]
    mine = pl.program_id(0) == info[0]

    @pl.when(mine)
    def _():
        place_blocks(info, refs[:4], out, slice(None), width, 0, False)

    @pl.when(jnp.logical_not(mine))
    def _():
        place_blocks(info, refs[4:8], out, slice(None), width, 0, True)


def finish_small(info, *refs):
    dsqueeze, dexcite, dfine, dcoarse, scratch = refs[8:]
    for pieces, partner in ((refs[:4], False), (refs[4:8], True)):
        for piece, block in zip(pieces, block_order(info, partner)):
            rows = pl.ds(pl.multiple_of(64 * block, 64), 64)
            here = jnp.concatenate([piece[0:64, :], piece[64:128, :]], 1).astype(F32)
            scratch[rows, :] = scratch[rows, :] + here if partner else here
    rows = scratch[...]
    dsqueeze[:, :256] = rows[0:32]
    dsqueeze[:, 256:] = rows[32:64]
    dexcite[:, :256] = rows[64:96]
    dexcite[:, 256:] = rows[96:128]
    for k in range(8):
        dfine[k] = rows[128:160, 32 * k : 32 * k + 32]
    dfine[8] = rows[160:192, 0:32]
    for k in range(9):
        dcoarse[k] = (
            rows[160:192, 32 * (k - 2) : 32 * (k - 2) + 32]
            if 3 <= k < 6
            else jnp.zeros((32, 32), F32)
        )


def shape(dims, dtype=F32):
    return jax.ShapeDtypeStruct(dims, dtype)


def whole(dims):
    count = len(dims)
    return pl.BlockSpec(dims, lambda i, *scalars: (0,) * count)


def run(kernel, outs, arrays, scalars=(), scratch=(), clip=None, halved=(), cost=COST):
    flat = jax.tree.leaves(tuple(arrays))
    tree = jax.tree.structure(tuple(arrays))
    in_specs = []
    for position, array in enumerate(flat):
        if position == clip:
            rest = len(array.shape) - 1
            in_specs.append(
                pl.BlockSpec(
                    (1,) + array.shape[1:], lambda i, place, *more: (place[0],) + (0,) * rest
                )
            )
        elif array.shape[1] // 2 in halved:
            in_specs.append(
                pl.BlockSpec((array.shape[0], array.shape[1] // 2), lambda i, info: (0, info[0]))
            )
        else:
            in_specs.append(whole(array.shape))

    def regrouped(*refs):
        first = len(scalars)
        last = first + len(flat)
        kernel(*refs[:first], *jax.tree.unflatten(tree, refs[first:last]), *refs[last:])

    return pl.pallas_call(
        regrouped,
        grid_spec=pltpu.PrefetchScalarGridSpec(
            num_scalar_prefetch=len(scalars),
            grid=(1,),
            in_specs=in_specs,
            out_specs=[whole(o.shape) for o in outs],
            scratch_shapes=scratch,
        ),
        out_shape=outs,
        compiler_params=pltpu.CompilerParams(vmem_limit_bytes=VMEM_BYTES),
        cost_estimate=pl.CostEstimate(flops=cost, bytes_accessed=cost, transcendentals=0),
    )(*scalars, *flat)


ALL = ("z", "y", "x", "c")


def exchange(value, partner):
    count = lax.axis_size(ALL)
    return lax.ppermute(value, ALL, [(i, partner(i)) for i in range(count)])


def by_mask(value, mask):
    return exchange(value, lambda i: i ^ mask)


def bit_count(n):
    count = n.bit_length() - 1
    assert n == 1 << count
    return count


def swap_bits(i, first, second):
    if (i >> first & 1) != (i >> second & 1):
        i ^= (1 << first) | (1 << second)
    return i


def after(value, *others):
    return lax.optimization_barrier((value,) + others)[0]


def finish(kernel, info, pieces, block, index_map, grid, out, out_block, out_map):
    return pl.pallas_call(
        kernel,
        grid_spec=pltpu.PrefetchScalarGridSpec(
            num_scalar_prefetch=1,
            grid=grid,
            in_specs=[pl.BlockSpec(block, index_map)] * len(pieces),
            out_specs=pl.BlockSpec(out_block, out_map),
        ),
        out_shape=out,
        compiler_params=pltpu.CompilerParams(vmem_limit_bytes=VMEM_BYTES),
    )(info, *pieces)


class Order:
    def __init__(self):
        self.last = None

    def __call__(self, step, *values):
        if self.last is not None:
            flat, tree = jax.tree.flatten(values)
            held = lax.optimization_barrier(tuple(flat) + (self.last,))
            values = jax.tree.unflatten(tree, held[:-1])
        result = step(*values)
        self.last = jax.tree.leaves(result)[0]
        return result


def body(
    frames,
    cut_mask,
    offsets,
    stem_kernel,
    diff_kernel,
    stem_gain,
    stem_bias,
    reduce_weight,
    reduce_gain,
    reduce_bias,
    squeeze_weight,
    fine_kernel,
    coarse_kernel,
    excite_weight,
    middle_kernel,
    expand_weight,
    expand_gain,
    expand_bias,
    cotangent,
):
    depth = lax.axis_size("z")
    groups = 2 * depth
    assert frames.shape[0] == MICRO
    bits = bit_count(depth) + 3
    index = lax.axis_index(ALL)
    stem_total = float(4096 * groups)
    row_total = float(128 * groups)
    clip = lax.rem(index, 4).astype(jnp.int32)
    place = clip.reshape(1)
    info = jnp.stack([lax.rem(lax.div(index, 1 << b), 2) for b in range(bits)]).astype(jnp.int32)
    plane = [(1, 2), (2, 1)]
    plane_mask = 6
    diff_flat = diff_kernel.reshape(54, STEM)
    fine_flat = fine_kernel.reshape(288, 32)
    coarse_flat = coarse_kernel.reshape(288, 32)
    gain_s = jnp.tile(stem_gain, 8)[None]
    bias_s = jnp.tile(stem_bias, 8)[None]
    gain_r = reduce_gain[None]
    bias_r = reduce_bias[None]
    gain_x = expand_gain[None]
    bias_x = expand_bias[None]

    def swapped(value):
        return exchange(value, lambda i: swap_bits(i, 0, 2))

    def along(value, choice):
        return exchange(value, lambda i: i ^ (1 << choice[i & 1]))

    def pooled_sum(value):
        value = value + by_mask(value, 1)
        if depth > 4:
            return (lax.psum(value, "z"),)
        return (value,) + tuple(by_mask(value, m << 3) for m in range(1, depth))

    def sums_shape(width):
        return shape((2, width))

    def to_plane(pieces):
        own, first, second, both = pieces
        return own, along(first, plane[0]), along(second, plane[1]), by_mask(both, plane_mask)

    def depth_sum(parts):
        got = [parts[0]] + [by_mask(parts[m], m << 3) for m in range(1, depth)]
        return got

    def total_of(parts):
        return sum(part.astype(F32) for part in parts).astype(BF)

    def padded(rows):
        unit = 16 * depth
        return -(-rows // unit) * unit

    (pack,) = run(
        pack_clip, [shape((208, 64), BF)], (frames,), (place, cut_mask, offsets), clip=0
    )
    pack = swapped(pack)
    stem_scratch = [
        pltpu.VMEM((512, 896), BF),
        pltpu.VMEM((256, 384), BF),
        pltpu.VMEM((896, 512), BF),
        pltpu.VMEM((384, 512), BF),
        pltpu.VMEM((192, 128), F32),
        pltpu.VMEM((512, 384), F32),
    ]
    v, stem_sums = run(
        stem_front,
        [shape((512, 512)), sums_shape(512)],
        (pack, stem_kernel.T, diff_flat),
        scratch=stem_scratch,
    )
    stem_sums = pooled_sum(stem_sums)
    wide, red, red_sums = run(
        functools.partial(stem_close, stem_total),
        [shape((128, 2048), BF), shape((128, 512)), sums_shape(512)],
        (v, stem_sums, gain_s, bias_s, reduce_weight),
    )
    wide_got = along(wide, plane[0])
    red_sums = pooled_sum(red_sums)
    cot = swapped(lax.dynamic_index_in_dim(after(cotangent, red), clip, 0, keepdims=False))
    hpre, both, expanded, exp_sums = run(
        functools.partial(gate_front, row_total),
        [shape((128, 512)), shape((128, 1024), BF), shape((128, 2048)), sums_shape(2048)],
        (
            pack, red, red_sums, gain_r, bias_r, squeeze_weight.T, fine_flat, coarse_flat,
            excite_weight, middle_kernel, expand_weight,
        ),
    )
    both_got = along(both, plane[0])
    exp_sums = pooled_sum(exp_sums)
    og, og_sums = run(
        functools.partial(out_back, row_total),
        [shape((128, 2048)), sums_shape(2048)],
        (expanded, exp_sums, gain_x, bias_x, wide, cot),
    )
    wide_near = jnp.concatenate([wide, after(wide_got, exp_sums[0])], 0)
    wide_far = along(wide_near, plane[1])
    both_near = jnp.concatenate([both, after(both_got, og_sums)], 0)
    both_far = along(both_near, plane[1])
    og_sums = pooled_sum(og_sums)
    hg, *blocks = run(
        functools.partial(expand_back, row_total),
        [shape((128, 512), BF)] + [shape((128, 640), BF)] * 4,
        (expanded, exp_sums, gain_x, og, og_sums, hpre, expand_weight),
        (info,),
        [pltpu.VMEM((128, 512), BF), pltpu.VMEM((128, 2048), BF)],
    )
    order = Order()
    order.last = hg
    blocks = to_plane(blocks)

    def four(pieces):
        rows, width = pieces[0].shape
        return run(stack_rows, [shape((4 * rows, width), BF)], pieces)[0]

    rg, rg_sums, small = order(
        lambda *arrays: run(
            functools.partial(gate_back, row_total),
            [shape((128, 512)), sums_shape(512), shape((256, 256))],
            arrays,
        ),
        pack, hg, red, red_sums, gain_r, bias_r, squeeze_weight.T, fine_flat, coarse_flat,
        excite_weight, middle_kernel,
    )
    both_far = after(both_far, rg)
    both_all = (both_near, both_far, by_mask(both_near, 1), by_mask(both_far, 1))
    rg_sums = order(pooled_sum, rg_sums)
    order.last = rg_sums[0]
    blocks = order(four, blocks)
    blocks_pair = by_mask(blocks, 1)
    rs, rs_sums, *late = order(
        lambda *arrays: run(
            functools.partial(reduce_back, row_total, stem_total),
            [shape((512, 512)), sums_shape(512)] + [shape((128, 256), BF)] * 4,
            arrays,
            (info,),
            [pltpu.VMEM((128, 512), BF)],
        ),
        small, red, red_sums, gain_r, rg, rg_sums, og, reduce_weight, v, stem_sums, gain_s, bias_s,
    )
    late = to_plane(late)
    wide_far = after(wide_far, rs)
    wide_all = (wide_near, wide_far, by_mask(wide_near, 1), by_mask(wide_far, 1))
    middle_rows = padded(2304)
    middle_parts = order(
        lambda left, right: run(
            middle_weights,
            [shape((middle_rows // depth, 128), BF)] * depth,
            (left, right),
            (info,),
            [pltpu.VMEM((middle_rows, 128), BF)],
            halved=(512,),
        ),
        both_all, (blocks, blocks_pair),
    )
    middle_parts = depth_sum(middle_parts)
    late = order(four, late)
    late_pair = by_mask(late, 1)
    outer_rows = padded(2176)
    outer_parts = order(
        lambda left, right, wide, late: run(
            outer_weights,
            [shape((outer_rows // depth, 128), BF)] * depth,
            (left, right, wide, late),
            (info,),
            [pltpu.VMEM((outer_rows, 128), BF)],
            halved=(512, 1024),
        ),
        both_all, (blocks, blocks_pair), wide_all, (late, late_pair),
    )
    outer_parts = depth_sum(outer_parts)
    rs_sums = order(pooled_sum, rs_sums)
    order.last = rs_sums[0]

    def depth_spread(value):
        return (value,) + tuple(by_mask(value, m << 3) for m in range(1, depth))

    def depth_stack(*parts):
        rows, width = parts[0].shape
        return run(stack_depth, [shape((depth * rows, width), BF)], parts, (info,))[0]

    middle = depth_spread(order(total_of, middle_parts))
    frame_grad, tail = order(
        lambda *arrays: run(
            functools.partial(stem_back, stem_total, 1.0 / groups),
            [shape((8, 3, 8, 64)), shape((200, 128))],
            arrays,
            scratch=stem_scratch,
        ),
        pack, stem_kernel.T, diff_flat, v, stem_sums, gain_s, rs, rs_sums, og_sums, rg_sums,
    )
    frame_grad = swapped(frame_grad)
    outer = depth_spread(order(total_of, outer_parts))
    tail = order(lambda a, b: a + b, tail, by_mask(tail, 1))
    tail_parts = depth_sum([tail] * depth)

    def plane_spread(value):
        return along(value, plane[0]), along(value, plane[1])

    middle = order(depth_stack, *middle)
    middle_first, middle_second = plane_spread(middle)
    tail = order(lambda *parts: sum(parts), *tail_parts)
    tail_parts = (tail,) + tuple(by_mask(tail, mask) for mask in (2, 4, 6))
    outer = order(depth_stack, *outer)
    outer_first, outer_second = plane_spread(outer)
    dstem, ddiff, gain_s, bias_s, gain_r, bias_r, gain_x, bias_x = order(
        lambda *parts: run(
            unpack_tail,
            [shape((64, 147)), shape((9, 6, 64))]
            + [shape((1, n)) for n in (64, 64, 512, 512, 2048, 2048)],
            (parts,),
        ),
        *tail_parts,
    )

    def with_pair(pieces):
        return tuple(pieces) + tuple(by_mask(piece, 1) for piece in pieces)

    middle_both = along(middle_second, plane[0])
    outer_both = along(outer_second, plane[0])
    middle = with_pair((middle, middle_first, middle_second, middle_both))
    dmiddle = order(
        lambda *pieces: finish(
            finish_middle, info, pieces, (768, 128), lambda i, info: (i, 0), (3,),
            shape((9, 512, 512)), (3, 512, 512), lambda i, info: (i, 0, 0),
        ),
        *middle,
    )
    outer = with_pair((outer, outer_first, outer_second, outer_both))
    dexpand = order(
        lambda *pieces: finish(
            functools.partial(finish_half, 4), info, pieces, (1024, 128),
            lambda h, info: (0, 0), (2,), shape((512, 2048)), (256, 2048),
            lambda h, info: (h, 0),
        ),
        *outer,
    )
    dreduce = order(
        lambda *pieces: finish(
            functools.partial(finish_half, 1), info, pieces, (1024, 128),
            lambda h, info: (1, 0), (2,), shape((2048, 512)), (1024, 512),
            lambda h, info: (h, 0),
        ),
        *outer,
    )
    small_shapes = ((32, 512), (32, 512), (9, 32, 32), (9, 32, 32))
    dsqueeze, dexcite, dfine, dcoarse = pl.pallas_call(
        finish_small,
        grid_spec=pltpu.PrefetchScalarGridSpec(
            num_scalar_prefetch=1,
            grid=(1,),
            in_specs=[pl.BlockSpec((128, 128), lambda i, info: (16, 0))] * 8,
            out_specs=[whole(d) for d in small_shapes],
            scratch_shapes=[pltpu.VMEM((256, 256), F32)],
        ),
        out_shape=[shape(d) for d in small_shapes],
        compiler_params=pltpu.CompilerParams(vmem_limit_bytes=VMEM_BYTES),
    )(info, *outer)
    return (
        frame_grad[None],
        dstem.T,
        ddiff,
        gain_s[0],
        bias_s[0],
        dreduce,
        gain_r[0],
        bias_r[0],
        dsqueeze.T,
        dfine,
        dcoarse,
        dexcite,
        dmiddle,
        dexpand,
        gain_x[0],
        bias_x[0],
    )


def solution(mesh):
    split = jax.sharding.Mesh(mesh.devices.reshape(-1, 2, 2, 2), ALL)
    copied = P()
    by_group = P(("z", "y"))
    in_specs = (by_group,) * 3 + (copied,) * 15 + (by_group,)
    out_specs = (P(ALL),) + (copied,) * 15
    return jax.shard_map(body, mesh=split, in_specs=in_specs, out_specs=out_specs, check_vma=False)
```

```python
import functools

import jax
import jax.numpy as jnp
from jax import lax
from jax.experimental import pallas as pl
from jax.experimental.pallas import tpu as pltpu
from jax.sharding import PartitionSpec as P

FRAMES = 8
MICRO = 4
EPSILON = 1e-05
COST = 1_000_000
FINISH_BYTES = 16 * 1024 * 1024
VMEM_BYTES = 32 * 1024 * 1024
BF = jnp.bfloat16
F32 = jnp.float32

STEM = 64
SLOT = 16


def dot(left, right):
    return jnp.dot(left, right, preferred_element_type=F32)


def dot_nt(left, right):
    return lax.dot_general(left, right, (((1,), (1,)), ((), ())), preferred_element_type=F32)


def dot_tn(left, right):
    return lax.dot_general(left, right, (((0,), (0,)), ((), ())), preferred_element_type=F32)


def dot_exact(left, right):
    return jnp.dot(left, right, preferred_element_type=F32, precision=lax.Precision.HIGHEST)


def iota(shape, dim):
    return lax.broadcasted_iota(jnp.int32, shape, dim)


def sigmoid(v):
    return 1.0 / (1.0 + jnp.exp(-v))


def swish_slope(v):
    s = sigmoid(v)
    return s * (1.0 + v * (1.0 - s))


def keep_column(pack, lanes):
    rows = pack[192:208, :].astype(F32)
    return jnp.concatenate(
        [jnp.broadcast_to(rows[f : f + 1, :lanes], (8, lanes)) for f in range(FRAMES)], 0
    )


def gate_column(pack):
    keep = keep_column(pack, 64)
    both = jnp.concatenate([keep, keep], 1)
    return jnp.concatenate([jnp.zeros((8, 128), F32), both[:-8]], 0)


def pack_clip(place, cut, offset, frames, out):
    clip = place[0]
    row = cut[pl.ds(clip, 1), :]
    own = iota((1, MICRO), 1) == clip
    stop = jnp.sum(jnp.where(own, offset[...], 0), 1, keepdims=True)
    step = iota(row.shape, 1)
    valid = jnp.where(step + 1 == stop, 0, row).astype(F32)
    spread = iota((16, FRAMES - 1), 0) == iota((16, FRAMES - 1), 1)
    column = jnp.sum(jnp.where(spread, valid, 0.0), 1, keepdims=True)
    out[0:192, :] = frames[...].astype(F32).reshape(192, 64).astype(BF)
    out[192:208, :] = jnp.broadcast_to(column, (16, 64)).astype(BF)


def summed_up(pieces):
    value = pieces[0][...]
    for piece in pieces[1:]:
        value = value + piece[...]
    return value


def spread_sums(out, first, second):
    out[...] = jnp.concatenate([first, second], 0)


def norm_scale(sums, row_total):
    mean = sums[0:1] * (1.0 / row_total)
    variance = sums[1:2] * (1.0 / row_total) - mean * mean
    return mean, lax.rsqrt(variance + EPSILON)


def column_sums(out, first, second):
    spread_sums(out, jnp.sum(first, 0, keepdims=True), jnp.sum(second, 0, keepdims=True))


def fold_lanes(sums):
    for step in (64, 128, 256):
        sums = sums + pltpu.roll(sums, step, 1)
    return sums


def shift_rows(v, dy, dx):
    rows = v.shape[0]
    if dx:
        rolled = pltpu.roll(v, (-dx) % rows, 0)
        wb = lax.rem(iota(v.shape, 0), 8)
        v = jnp.where((wb + dx >= 0) & (wb + dx < 8), rolled, 0.0)
    half = rows // 2
    if dy == 1:
        v = jnp.concatenate([v[half:], jnp.zeros_like(v[half:])], 0)
    elif dy == -1:
        v = jnp.concatenate([jnp.zeros_like(v[:half]), v[:half]], 0)
    return v


def cell_sum(v):
    half = v.shape[0] // 2
    both = v[:half] + v[half:]
    even = lax.rem(iota(both.shape, 0), 2) == 0
    both = both + jnp.where(even, pltpu.roll(both, half - 1, 0), pltpu.roll(both, 1, 0))
    return jnp.concatenate([both, both], 0)


def taps(v):
    return [shift_rows(v, ky - 1, kx - 1) for ky in range(3) for kx in range(3)]


def back_taps(v):
    return [shift_rows(v, 1 - ky, 1 - kx) for ky in range(3) for kx in range(3)]


def coarse_taps(v):
    return [shift_rows(v, 0, 2 * (k - 1)) for k in range(3)]


def window_select(rows, cols, kind):
    place = iota((rows, cols), 0)
    col = iota((rows, cols), 1)
    lane = lax.rem(place, 128)
    tap_row = lax.div(place, 128)
    channel = lax.div(lane, SLOT)
    slot = lax.rem(lane, SLOT)
    if kind == "stem":
        hit = (col == (7 * tap_row + slot) * 3 + channel) & (slot < 7) & (channel < 3)
        return jnp.where(hit, 1.0, 0.0)
    cell = lax.div(slot - 1, 2)
    hit = (col == (3 * tap_row + cell) * 6 + channel) & (slot >= 1) & (slot < 7) & (channel < 6)
    return jnp.where(hit, 0.25, 0.0)


def spread_select():
    w = iota((64, 128), 0)
    lane = iota((64, 128), 1)
    return jnp.where(w == 8 * lax.div(lane, SLOT) + lax.rem(lane, SLOT) - 3, 1.0, 0.0)


def gather_select():
    row = iota((384, 128), 0)
    col = iota((384, 128), 1)
    return jnp.where(col == lax.div(row, 128) * SLOT + lax.rem(row, SLOT), 1.0, 0.0)


def own_block():
    row = iota((8, 128), 0)
    lane = iota((8, 128), 1)
    return jnp.where(lax.div(lane, SLOT) == row, 1.0, 0.0)


def stem_windows(pack, kernel, diff, win, win2, u, u2, spread, tiles):
    spread[...] = dot(pack[0:192, :], spread_select().astype(BF))
    mask = own_block()
    for f in range(8):
        for c in range(3):
            for h in range(8):
                line = f * 24 + c * 8 + h
                tiles[h * 64 + f * 8 : h * 64 + f * 8 + 8, c * 128 : c * 128 + 128] = (
                    jnp.broadcast_to(spread[line : line + 1, :], (8, 128)) * mask
                )
    pixels = dot(tiles[...].astype(BF), gather_select().astype(BF))
    rows = [pixels[64 * h : 64 * h + 64] for h in range(8)]
    gate = gate_column(pack)
    steps = []
    for h2 in range(4):
        both = rows[2 * h2] + rows[2 * h2 + 1]
        step = (both - jnp.concatenate([jnp.zeros((8, 128), F32), both[:-8]], 0)) * gate
        later = jnp.concatenate([step[8:], jnp.zeros((8, 128), F32)], 0)
        steps.append((step + pltpu.roll(later, 48, 1)).astype(BF))
    rows = [r.astype(BF) for r in rows]
    blank = jnp.zeros((64, 128), BF)
    for dy in range(7):
        for h in range(8):
            source = h + dy - 3
            win[64 * h : 64 * h + 64, 128 * dy : 128 * dy + 128] = (
                rows[source] if 0 <= source < 8 else blank
            )
    for dy in range(3):
        for h in range(4):
            source = h + dy - 1
            win2[64 * h : 64 * h + 64, 128 * dy : 128 * dy + 128] = (
                steps[source] if 0 <= source < 4 else blank
            )
    low_half = iota((896, 128), 1) < 64
    wide_kernel = jnp.concatenate([kernel[...], kernel[...]], 0)
    placed = dot_nt(window_select(896, 147, "stem").astype(BF), wide_kernel)
    wide_diff = jnp.concatenate([diff[...], diff[...]], 1)
    placed2 = dot(window_select(384, 54, "diff").astype(BF), wide_diff)
    for q in range(4):
        first = pltpu.roll(placed, 2 * q, 0) if q else placed
        second = pltpu.roll(placed, 2 * q + 1, 0)
        u[:, 128 * q : 128 * q + 128] = jnp.where(low_half, first, second).astype(BF)
        u2[:, 128 * q : 128 * q + 128] = (
            pltpu.roll(placed2, 2 * q, 0) if q else placed2
        ).astype(BF)


def stem_front(pack, kernel, diff, v_out, sums_out, win, win2, u, u2, spread, tiles):
    stem_windows(pack, kernel, diff, win, win2, u, u2, spread, tiles)
    v = dot(win[...], u[...])
    side = dot(win2[...], u2[...])
    first = jnp.zeros((1, 512), F32)
    second = jnp.zeros((1, 512), F32)
    for h in range(8):
        piece = v[64 * h : 64 * h + 64] + side[64 * (h // 2) : 64 * (h // 2) + 64]
        v_out[64 * h : 64 * h + 64, :] = piece
        first = first + jnp.sum(piece, 0, keepdims=True)
        second = second + jnp.sum(piece * piece, 0, keepdims=True)
    spread_sums(sums_out, first, second)


def stem_close(
    row_total, info, v, sums, gain, bias, weight, wide_out, keep_out, send_out, red_out, sums_out,
    save,
):
    mean, scale = norm_scale(fold_lanes(summed_up(sums)), row_total)
    save[512:513, :] = scale
    for h in range(8):
        normal = (v[64 * h : 64 * h + 64, :] - mean) * scale
        save[64 * h : 64 * h + 64, :] = normal
        y = normal * gain[...] + bias[...]
        wide_out[
            64 * (h // 4) : 64 * (h // 4) + 64, 512 * (h % 4) : 512 * (h % 4) + 512
        ] = (y * sigmoid(y)).astype(BF)
    save.flush()
    wide_out.flush()
    keep_out[...] = wide_out[:, lanes(1024 * info[0], 1024)]
    send_out[...] = wide_out[:, lanes(1024 * (1 - info[0]), 1024)]
    red = dot(wide_out[...], weight[...])
    red_out[...] = red
    column_sums(sums_out, red, red * red)


def gate_path(pack, narrow, squeeze, fine, coarse, excite):
    squeezed = dot_nt(narrow.astype(BF), squeeze[...])
    keep = keep_column(pack, 32)
    parts = []
    for hb in range(2):
        part = squeezed[64 * hb : 64 * hb + 64]
        later = jnp.concatenate([part[8:], part[:8]], 0)
        parts.append((later - part) * keep)
    change = jnp.concatenate(parts, 0)
    fine_rows = jnp.concatenate(taps(change), 1).astype(BF)
    pooled = 0.25 * cell_sum(change)
    coarse_rows = jnp.concatenate(coarse_taps(pooled), 1).astype(BF)
    summed = (dot(fine_rows, fine[...]) + dot(coarse_rows, coarse[96:192, :])).astype(BF)
    return fine_rows, coarse_rows, summed, sigmoid(dot(summed, excite[...]))


def gate_front(
    row_total, info, red, sums, pack, gain, bias, squeeze, fine, coarse, excite, middle, expand,
    keep_out, send_out, exp_out, sums_out, save, both,
):
    mean, scale = norm_scale(summed_up(sums), row_total)
    normal = (red[...] - mean) * scale
    save[0:128, :] = normal
    save[128:129, :] = scale
    save.flush()
    y = normal * gain[...] + bias[...]
    narrow = y * sigmoid(y)
    gate = gate_path(pack, narrow, squeeze, fine, coarse, excite)[3]
    gated = narrow * (1.0 + gate)
    total = jnp.zeros((128, 512), F32)
    for k, piece in enumerate(taps(gated)):
        total = total + dot(piece.astype(BF), middle[k])
    save[136:264, :] = total
    save.flush()
    hidden = (total * sigmoid(total)).astype(BF)
    for half in range(2):
        part = slice(256 * half, 256 * half + 256)
        both[:, 512 * half : 512 * half + 256] = gated[:, part].astype(BF)
        both[:, 512 * half + 256 : 512 * half + 512] = hidden[:, part]
    keep_out[...] = both[:, lanes(512 * info[0], 512)]
    send_out[...] = both[:, lanes(512 * (1 - info[0]), 512)]
    expanded = dot(hidden, expand[...])
    exp_out[...] = expanded
    column_sums(sums_out, expanded, expanded * expanded)


def out_back(row_total, expanded, sums, gain, bias, wide, cot, sums_out, save):
    mean, scale = norm_scale(summed_up(sums), row_total)
    save[256:257, :] = scale
    first = jnp.zeros((1, 2048), F32)
    second = jnp.zeros((1, 2048), F32)
    for hb in range(2):
        part = slice(64 * hb, 64 * hb + 64)
        if hb:
            save.flush()
            save.flush()
        normal = (expanded[part, :] - mean) * scale
        y = normal * gain[...] + bias[...] + wide[part, :].astype(F32)
        weightless = cot[:, hb, :, :].astype(F32).reshape(64, 2048)
        og = weightless * swish_slope(y)
        save[part, :] = og
        save[128 + 64 * hb : 192 + 64 * hb, :] = normal
        first = first + jnp.sum(og, 0, keepdims=True)
        second = second + jnp.sum(og * normal, 0, keepdims=True)
    spread_sums(sums_out, first, second)


def norm_pull(grad, normal, scale, gain, grad_sums, row_total):
    return (
        gain
        * scale
        * (
            grad
            - grad_sums[0:1] * (1.0 / row_total)
            - normal * (grad_sums[1:2] * (1.0 / row_total))
        )
    )


def block_order(info, partner=False):
    block = 2 * info[1] + info[2]
    first = jnp.where((info[0] == 0) != partner, 2, 1)
    return [block, block ^ first, block ^ (3 - first), block ^ 3]


def lanes(start, width):
    return pl.ds(pl.multiple_of(start, 128), width)


def expand_back(
    row_total, info, grad_sums, saved, hpre, gain, expand, hg_out, total_out, *rest
):
    outs, (hg_scratch, dv_scratch) = rest[:4], rest[4:]
    sums = summed_up(grad_sums)
    total_out[0:2, :] = sums
    total_out.flush()
    dv = norm_pull(
        saved[0:128, :], saved[128:256, :], saved[256:257, :], gain[...], sums, row_total
    ).astype(BF)
    dv_scratch[...] = dv
    dhid = dot_nt(dv, expand[...]).astype(BF).astype(F32)
    hg = (dhid * swish_slope(hpre[...])).astype(BF)
    hg_out[...] = hg
    hg_scratch[...] = hg
    for out, block in zip(outs, block_order(info)):
        out[:, :128] = hg_scratch[:, lanes(128 * block, 128)]
        out[:, 128:] = dv_scratch[:, lanes(512 * block, 512)]


def all_rows(refs):
    return jnp.concatenate([ref[...] for ref in refs], 0)


def clip_rows(mine, pair, columns):
    rows = []
    for k, other in enumerate((0, 2, 1, 3)):
        rows.append(mine[128 * k : 128 * k + 128, columns])
        rows.append(pair[128 * other : 128 * other + 128, columns])
    return rows


def depth_halves(info, bit, scratch, keep_out, send_out):
    rows = keep_out.shape[0]
    mine = info[bit]
    keep_out[...] = scratch[pl.ds(pl.multiple_of(mine * rows, 16), rows), :]
    send_out[...] = scratch[pl.ds(pl.multiple_of((1 - mine) * rows, 16), rows), :]


def add_halves(bit, info, keep, got, keep_out, send_out, scratch):
    scratch[...] = (keep[...].astype(F32) + got[...].astype(F32)).astype(BF)
    depth_halves(info, bit, scratch, keep_out, send_out)


def add_rows(keep, got, out):
    out[...] = (keep[...].astype(F32) + got[...].astype(F32)).astype(BF)


def join_halves(bit, info, own, got, out):
    rows = own.shape[0]
    mine = info[bit]
    out[pl.ds(pl.multiple_of(mine * rows, 16), rows), :] = own[...]
    out[pl.ds(pl.multiple_of((1 - mine) * rows, 16), rows), :] = got[...]


def middle_weights(info, left_refs, right_refs, *rest):
    outs, (scratch,) = rest[:-1], rest[-1:]
    left = jnp.concatenate([ref[:, :256] for ref in left_refs], 0).T
    clips = [
        back_taps(rows.astype(F32)) for rows in clip_rows(*right_refs, slice(0, 128))
    ]
    for k in range(9):
        right = jnp.concatenate([clip[k] for clip in clips], 0).astype(BF)
        scratch[256 * k : 256 * k + 256, :] = dot(left, right).astype(BF)
    if scratch.shape[0] > 2304:
        scratch[2304:, :] = jnp.zeros((scratch.shape[0] - 2304, 128), BF)
    depth_halves(info, 3, scratch, *outs)


def outer_weights(info, left_refs, right_refs, wide, late, *rest):
    outs, (scratch,) = rest[:-1], rest[-1:]
    left = jnp.concatenate([ref[:, 256:] for ref in left_refs], 0)
    right = jnp.concatenate(clip_rows(*right_refs, slice(128, 640)), 0)
    result = dot_tn(left, right).astype(BF)
    for q in range(4):
        scratch[256 * q : 256 * q + 256, :] = result[:, 128 * q : 128 * q + 128]
    right = jnp.concatenate(clip_rows(*late, slice(0, 128)), 0)
    scratch[1024:2048, :] = dot_tn(all_rows(wide), right).astype(BF)
    small = [late[0][128 * k : 128 * k + 128, 128:].astype(F32) for k in range(4)]
    scratch[2048:2176, :] = sum(small).astype(BF)
    if scratch.shape[0] > 2176:
        scratch[2176:, :] = jnp.zeros((scratch.shape[0] - 2176, 128), BF)
    depth_halves(info, 3, scratch, *outs)


def copy_rows(source, out):
    out[...] = source[...]


def add_floats(first, second, out):
    out[...] = first[...] + second[...]


def stack_rows(*refs):
    out = refs[-1]
    start = 0
    for ref in refs[:-1]:
        out[start : start + ref.shape[0], :] = ref[...]
        start += ref.shape[0]


def gate_back(
    pack, hg, normal, gain, bias, squeeze, fine, coarse, excite, middle,
    rg_out, sums_out, small_out,
):
    y = normal[...] * gain[...] + bias[...]
    narrow_v = y * sigmoid(y)
    fine_rows, coarse_rows, summed, gate_v = gate_path(
        pack, narrow_v, squeeze, fine, coarse, excite
    )
    total = jnp.zeros((128, 512), F32)
    for k, piece in enumerate(back_taps(hg[...].astype(F32))):
        total = total + dot_nt(piece.astype(BF), middle[k])
    gg = total.astype(BF).astype(F32)
    narrow_grad = gg * (1.0 + gate_v)
    excite_grad = (gg * narrow_v * gate_v * (1.0 - gate_v)).astype(BF)
    dexcite = dot_tn(summed, excite_grad)
    summed_low = dot_nt(excite_grad, excite[...]).astype(BF)
    summed_grad = summed_low.astype(F32)
    coarse_low = cell_sum(summed_grad).astype(BF)
    dfine = dot_tn(fine_rows, summed_low)
    dcoarse = 0.25 * dot_tn(coarse_rows, coarse_low)
    spread = dot_nt(summed_low, fine[...])
    change_grad = jnp.zeros((128, 32), F32)
    for k in range(9):
        change_grad = change_grad + shift_rows(
            spread[:, 32 * k : 32 * k + 32], 1 - k // 3, 1 - k % 3
        )
    spread = dot_nt(coarse_low, coarse[96:192, :])
    pooled_grad = jnp.zeros((128, 32), F32)
    for k in range(3):
        pooled_grad = pooled_grad + shift_rows(spread[:, 32 * k : 32 * k + 32], 0, 2 * (1 - k))
    change_grad = change_grad + 0.25 * pooled_grad
    keep = keep_column(pack, 32)
    parts = []
    for hb in range(2):
        step = change_grad[64 * hb : 64 * hb + 64] * keep
        earlier = jnp.concatenate([step[56:], step[:56]], 0)
        parts.append(earlier - step)
    squeezed_grad = jnp.concatenate(parts, 0).astype(BF)
    dsqueeze = dot_tn(squeezed_grad, narrow_v.astype(BF))
    narrow_grad = narrow_grad + dot(squeezed_grad, squeeze[...])
    rg = narrow_grad * swish_slope(y)
    rg_out[...] = rg
    column_sums(sums_out, rg, rg * normal[...])
    small_out[0:32, :] = dsqueeze[:, :256]
    small_out[32:64, :] = dsqueeze[:, 256:]
    small_out[64:96, :] = dexcite[:, :256]
    small_out[96:128, :] = dexcite[:, 256:]
    pieces = [dfine[32 * k : 32 * k + 32] for k in range(9)]
    pieces += [dcoarse[32 * k : 32 * k + 32] for k in range(3)]
    small_out[128:160, :] = jnp.concatenate(pieces[:8], 1)
    small_out[160:192, :] = jnp.concatenate(pieces[8:] + [jnp.zeros((32, 128), F32)], 1)
    small_out[192:256, :] = jnp.zeros((64, 256), F32)


def reduce_back(
    row_total, info, small, rg, grad_sums, saved, gain, og, weight, stem_saved, stem_gain,
    stem_bias, rs_out, sums_out, total_out, dv0, dv1, dv2, dv3, dv_scratch,
):
    sums = summed_up(grad_sums)
    total_out[0:2, :] = sums
    total_out.flush()
    dv = norm_pull(
        rg[...], saved[0:128, :], saved[128:129, :], gain[...], sums, row_total
    ).astype(BF)
    dv_scratch[...] = dv
    for out, block in zip((dv0, dv1, dv2, dv3), block_order(info)):
        out[:, :128] = dv_scratch[:, lanes(128 * block, 128)]
        part = small[pl.ds(pl.multiple_of(64 * block, 64), 64), :].astype(BF)
        out[:64, 128:] = part[:, :128]
        out[64:, 128:] = part[:, 128:]
    wide_grad = dot_nt(dv, weight[...]) + og[...].astype(BF).astype(F32)
    wide_grad = wide_grad.astype(BF).astype(F32)
    first = jnp.zeros((1, 512), F32)
    second = jnp.zeros((1, 512), F32)
    for h in range(8):
        normal = stem_saved[64 * h : 64 * h + 64, :]
        y = normal * stem_gain[...] + stem_bias[...]
        rs = (
            wide_grad[64 * (h // 4) : 64 * (h // 4) + 64, 512 * (h % 4) : 512 * (h % 4) + 512]
            * swish_slope(y)
        )
        rs_out[64 * h : 64 * h + 64, :] = rs
        first = first + jnp.sum(rs, 0, keepdims=True)
        second = second + jnp.sum(rs * normal, 0, keepdims=True)
    spread_sums(sums_out, first, second)


def stem_back(
    stem_total, share, pack, kernel, diff, saved, gain, rs, grad_sums, og_total,
    rg_total, frames_out, tail_out, win, win2, u, u2, lines, tiles,
):
    stem_windows(pack, kernel, diff, win, win2, u, u2, lines, tiles)
    scale = saved[512:513, :]
    totals = fold_lanes(summed_up(grad_sums))
    rows = []
    pairs = []
    for h in range(8):
        part = slice(64 * h, 64 * h + 64)
        normal = saved[part, :]
        pre = norm_pull(rs[part, :], normal, scale, gain[...], totals, stem_total)
        rows.append(pre.astype(BF))
        if h % 2:
            pairs.append((before + pre).astype(BF))
        before = pre
    dv = jnp.concatenate(rows, 0)
    dside = jnp.concatenate(pairs, 0)

    low_half = iota((896, 128), 1) < 64
    du = dot_tn(win[...], dv)
    placed = jnp.zeros((896, 128), F32)
    for q in range(4):
        part = du[:, 128 * q : 128 * q + 128]
        first = pltpu.roll(part, 896 - 2 * q, 0) if q else part
        placed = placed + jnp.where(low_half, first, pltpu.roll(part, 896 - 2 * q - 1, 0))
    placed = placed + pltpu.roll(placed, 64, 1)
    tail_out[0:147, 0:64] = lax.dot_general(
        window_select(896, 147, "stem"), placed, (((0,), (0,)), ((), ())),
        preferred_element_type=F32, precision=lax.Precision.HIGHEST,
    )[:, :64]
    du2 = dot_tn(win2[...], dside)
    placed = jnp.zeros((384, 128), F32)
    for q in range(4):
        part = du2[:, 128 * q : 128 * q + 128]
        placed = placed + (pltpu.roll(part, 384 - 2 * q, 0) if q else part)
    placed = placed + pltpu.roll(placed, 64, 1)
    tail_out[0:54, 64:128] = lax.dot_general(
        window_select(384, 54, "diff"), placed, (((0,), (0,)), ((), ())),
        preferred_element_type=F32, precision=lax.Precision.HIGHEST,
    )[:, :64]

    dwin = dot_nt(dv, u[...])
    dwin2 = dot_nt(dside, u2[...])
    gate = gate_column(pack)
    steps = []
    for h2 in range(4):
        total = jnp.zeros((64, 128), F32)
        for dy in range(3):
            target = h2 + 1 - dy
            if 0 <= target < 4:
                total = total + dwin2[64 * target : 64 * target + 64, 128 * dy : 128 * dy + 128]
        later = pltpu.roll(total, 80, 1)
        later = jnp.concatenate([jnp.zeros((8, 128), F32), later[:-8]], 0)
        step = (total + later) * gate
        steps.append(step - jnp.concatenate([step[8:], jnp.zeros((8, 128), F32)], 0))
    pixels = []
    for h in range(8):
        total = steps[h // 2]
        for dy in range(7):
            target = h + 3 - dy
            if 0 <= target < 8:
                total = total + dwin[64 * target : 64 * target + 64, 128 * dy : 128 * dy + 128]
        pixels.append(total)
    pixels = jnp.concatenate(pixels, 0)
    back = lax.dot_general(
        pixels, gather_select(), (((1,), (1,)), ((), ())),
        preferred_element_type=F32, precision=lax.Precision.HIGHEST,
    )
    mask = own_block()
    for f in range(8):
        for c in range(3):
            for h in range(8):
                line = f * 24 + c * 8 + h
                block = back[h * 64 + f * 8 : h * 64 + f * 8 + 8, c * 128 : c * 128 + 128]
                lines[line : line + 1, :] = jnp.sum(block * mask, 0, keepdims=True)
    flat = lax.dot_general(
        lines[...], spread_select(), (((1,), (1,)), ((), ())),
        preferred_element_type=F32, precision=lax.Precision.HIGHEST,
    )
    frames_out[...] = flat.reshape(8, 3, 8, 64)
    og_all = og_total[0:2, :]
    rg_all = rg_total[0:2, :]
    for q in range(16):
        tail_out[152 + 2 * q : 154 + 2 * q, :] = og_all[:, 128 * q : 128 * q + 128] * share
    for q in range(4):
        tail_out[184 + 2 * q : 186 + 2 * q, :] = rg_all[:, 128 * q : 128 * q + 128] * share
    tail_out[192:194, :] = totals[:, :128] * share


def plane_pieces(near, far):
    return near.at[0], far.at[0], near.at[1], far.at[1]


def finish_middle(info, near, far, near2, far2, out):
    sides = ((near, far, info[0], False), (near2, far2, 1 - info[0], True))
    for one, two, bit, partner in sides:
        row = pl.ds(pl.multiple_of(256 * bit, 128), 256)
        for piece, block in zip(plane_pieces(one, two), block_order(info, partner)):
            for tap in range(out.shape[0]):
                tile = piece[256 * tap : 256 * tap + 256, :]
                out[tap, row, lanes(128 * block, 128)] = tile.astype(F32)


def finish_outer(info, *refs):
    expand_refs, reduce_refs = refs[:4], refs[4:8]
    expand_out, reduce_out = refs[8:]
    step = pl.program_id(0)

    def place(near, far, partner, out, width):
        rows = out.shape[0]
        for piece, block in zip(plane_pieces(near, far), block_order(info, partner)):
            for q in range(width):
                tile = piece[rows * q : rows * q + rows, :]
                out[:, lanes(128 * (width * block + q), 128)] = tile.astype(F32)

    for half in range(2):
        for base, sources, out, width in (
            (0, expand_refs, expand_out, 4),
            (2, reduce_refs, reduce_out, 1),
        ):
            here = step == base + half
            pl.when(here & (info[0] == half))(
                functools.partial(place, *sources[:2], False, out, width)
            )
            pl.when(here & (info[0] != half))(
                functools.partial(place, *sources[2:], True, out, width)
            )


def finish_small(
    info, near, far, near2, far2, tail_mine, tail_got, token,
    dsqueeze, dexcite, dfine, dcoarse, stem_out, diff_out, gain_s, bias_s, gain_r, bias_r,
    gain_x, bias_x, scratch, tail,
):
    for one, two, partner in ((near, far, False), (near2, far2, True)):
        for piece, block in zip(plane_pieces(one, two), block_order(info, partner)):
            rows = pl.ds(pl.multiple_of(64 * block, 64), 64)
            here = jnp.concatenate([piece[0:64, :], piece[64:128, :]], 1).astype(F32)
            scratch[rows, :] = scratch[rows, :] + here if partner else here
    tail[...] = tail_mine[...] + tail_got[...]
    rows = scratch[...]
    dsqueeze[:, :256] = rows[0:32]
    dsqueeze[:, 256:] = rows[32:64]
    dexcite[:, :256] = rows[64:96]
    dexcite[:, 256:] = rows[96:128]
    for k in range(8):
        dfine[k] = rows[128:160, 32 * k : 32 * k + 32]
    dfine[8] = rows[160:192, 0:32]
    for k in range(9):
        dcoarse[k] = (
            rows[160:192, 32 * (k - 2) : 32 * (k - 2) + 32]
            if 3 <= k < 6
            else jnp.zeros((32, 32), F32)
        )
    stem_out[...] = tail[0:152, :].T[0:64, 0:147]
    for k in range(9):
        diff_out[k] = tail[6 * k : 6 * k + 6, 64:128]
    for q in range(16):
        bias_x[:, 128 * q : 128 * q + 128] = tail[152 + 2 * q : 153 + 2 * q, :]
        gain_x[:, 128 * q : 128 * q + 128] = tail[153 + 2 * q : 154 + 2 * q, :]
    for q in range(4):
        bias_r[:, 128 * q : 128 * q + 128] = tail[184 + 2 * q : 185 + 2 * q, :]
        gain_r[:, 128 * q : 128 * q + 128] = tail[185 + 2 * q : 186 + 2 * q, :]
    bias_s[...] = tail[192:193, :64]
    gain_s[...] = tail[193:194, :64]


def shape(dims, dtype=F32):
    return jax.ShapeDtypeStruct(dims, dtype)


def whole(dims):
    count = len(dims)
    return pl.BlockSpec(dims, lambda i, *scalars: (0,) * count)


class Far:
    def __init__(self, array, start=0, rows=None, clip=False, other=None):
        self.array, self.start, self.rows, self.clip = array, start, rows, clip
        self.other = other

    def arrays(self):
        return [self.array] if self.other is None else [self.array, self.other]

    def buffer(self):
        dims = self.array.shape
        if self.clip:
            dims = dims[1:]
        elif self.rows is not None:
            dims = (self.rows,) + dims[1:]
        return pltpu.VMEM(dims, self.array.dtype)

    def source(self, ref, scalars):
        if self.clip:
            return ref.at[scalars[0][0]]
        if self.rows is not None:
            return ref.at[pl.ds(self.start, self.rows)]
        return ref


jax.tree_util.register_pytree_node(
    Far,
    lambda far: ((far.array, far.other), (far.start, far.rows, far.clip)),
    lambda rest, children: Far(children[0], *rest, children[1]),
)


class FarRef:
    def __init__(self, sources, buffer, semaphore, info):
        self.copy = pltpu.make_async_copy(sources[0], buffer, semaphore)
        if len(sources) == 1:
            self.copy.start()
        else:
            other = pltpu.make_async_copy(sources[1], buffer, semaphore)
            pl.when(info[info.shape[0] - 1] == 1)(self.copy.start)
            pl.when(info[info.shape[0] - 1] == 0)(other.start)
        self.buffer, self.pending = buffer, True
        self.shape = buffer.shape

    def wait(self):
        if self.pending:
            self.copy.wait()
            self.pending = False

    def __getitem__(self, place):
        self.wait()
        return self.buffer[place]


class FarOut:
    def __init__(self, out, parts=None):
        self.out = out
        self.parts = parts or [(0, out.shape[0])]


class FarOutRef:
    def __init__(self, buffer, home, semaphores, parts):
        self.buffer, self.shape = buffer, buffer.shape
        self.copies = [
            pltpu.make_async_copy(
                buffer.at[pl.ds(start, rows)], home.at[pl.ds(start, rows)], semaphore
            )
            for (start, rows), semaphore in zip(parts, semaphores)
        ]
        self.started = 0

    def __getitem__(self, place):
        return self.buffer[place]

    def __setitem__(self, place, value):
        self.buffer[place] = value

    def flush(self):
        self.copies[self.started].start()
        self.started += 1

    def finish(self):
        while self.started < len(self.copies):
            self.flush()
        for copy in self.copies:
            copy.wait()


def run(
    kernel, outs, arrays, scalars=(), scratch=(), choose=None, deps=(), cost=COST
):
    flat, tree = jax.tree.flatten(tuple(arrays), is_leaf=lambda x: isinstance(x, Far))
    operands, in_specs, places = [], [], []
    for array in flat:
        places.append(len(operands))
        if isinstance(array, Far):
            for piece in array.arrays():
                operands.append(pltpu.with_memory_space_constraint(piece, pltpu.HBM))
                in_specs.append(pl.BlockSpec(memory_space=pltpu.HBM))
            continue
        operands.append(array)
        in_specs.append(whole(array.shape))
    read = len(operands)
    for array in deps:
        operands.append(array)
        in_specs.append(pl.BlockSpec(memory_space=pl.ANY))
    out_specs, out_shape = [], []
    for out in outs:
        if isinstance(out, FarOut):
            out_specs.append(pl.BlockSpec(memory_space=pltpu.HBM))
            out_shape.append(pltpu.HBM(out.out.shape, out.out.dtype))
        else:
            out_specs.append(whole(out.shape))
            out_shape.append(out)
    far_in = [p for p, array in enumerate(flat) if isinstance(array, Far)]
    far_out = [p for p, out in enumerate(outs) if isinstance(out, FarOut)]
    buffers = [flat[p].buffer() for p in far_in]
    buffers += [pltpu.VMEM(outs[p].out.shape, outs[p].out.dtype) for p in far_out]
    moves = len(buffers)
    semaphore_count = len(far_in) + sum(len(outs[p].parts) for p in far_out)
    prefetched = tuple(scalars) if choose is None else tuple(scalars) + (choose,)

    def regrouped(*refs):
        first = len(prefetched)
        last = first + len(operands)
        end = last + len(outs)
        near, results = refs[first : first + read], list(refs[last:end])
        kept = refs[end : end + moves]
        semaphores = refs[end + moves] if moves else None
        rest = refs[end + moves + 1 :] if moves else refs[end:]
        ins = [near[place] for place in places]
        for k, p in enumerate(far_in):
            far = flat[p]
            sources = [
                far.source(near[places[p] + j], refs[:first]) for j in range(len(far.arrays()))
            ]
            ins[p] = FarRef(sources, kept[k], semaphores.at[k], refs[first - 1])
        used = len(far_in)
        for k, p in enumerate(far_out):
            parts = outs[p].parts
            own = [semaphores.at[used + n] for n in range(len(parts))]
            used += len(parts)
            results[p] = FarOutRef(kept[len(far_in) + k], results[p], own, parts)
        kernel(*refs[: len(scalars)], *jax.tree.unflatten(tree, ins), *results, *rest)
        for p in far_in:
            ins[p].wait()
        for p in far_out:
            results[p].finish()

    return pl.pallas_call(
        regrouped,
        grid_spec=pltpu.PrefetchScalarGridSpec(
            num_scalar_prefetch=len(prefetched),
            grid=(1,),
            in_specs=in_specs,
            out_specs=out_specs,
            scratch_shapes=buffers
            + ([pltpu.SemaphoreType.DMA((semaphore_count,))] if moves else [])
            + list(scratch),
        ),
        out_shape=out_shape,
        compiler_params=pltpu.CompilerParams(vmem_limit_bytes=VMEM_BYTES),
        cost_estimate=pl.CostEstimate(flops=cost, bytes_accessed=cost, transcendentals=0),
    )(*prefetched, *operands)


ALL = ("z", "y", "x", "c")


def exchange(value, partner, whole_route=False):
    count = lax.axis_size(ALL)
    route = [(i, partner(i)) for i in range(count) if whole_route or partner(i) != i]
    return lax.ppermute(value, ALL, route)


def by_mask(value, mask):
    return exchange(value, lambda i: i ^ mask)


def bit_count(n):
    count = n.bit_length() - 1
    assert n == 1 << count
    return count


def swap_bits(i, first, second):
    if (i >> first & 1) != (i >> second & 1):
        i ^= (1 << first) | (1 << second)
    return i


def finish(
    kernel, info, pieces, block, index_map, grid, out, out_block, out_map, far=False, deps=()
):
    if far:
        pieces = [pltpu.with_memory_space_constraint(piece, pltpu.HBM) for piece in pieces]

    def with_token(*refs):
        refs[-1][...] = jnp.zeros((8, 128), F32)
        kernel(*refs[: 1 + len(pieces)], refs[-2])

    return pl.pallas_call(
        with_token,
        grid_spec=pltpu.PrefetchScalarGridSpec(
            num_scalar_prefetch=1,
            grid=grid,
            in_specs=[pl.BlockSpec(block, index_map)] * len(pieces)
            + [pl.BlockSpec(memory_space=pl.ANY)] * len(deps),
            out_specs=[
                pl.BlockSpec(out_block, out_map),
                pl.BlockSpec((8, 128), lambda *place: (0, 0)),
            ],
        ),
        out_shape=[out, shape((8, 128))],
        compiler_params=pltpu.CompilerParams(vmem_limit_bytes=FINISH_BYTES),
    )(info, *pieces, *deps)


def body(
    frames,
    cut_mask,
    offsets,
    stem_kernel,
    diff_kernel,
    stem_gain,
    stem_bias,
    reduce_weight,
    reduce_gain,
    reduce_bias,
    squeeze_weight,
    fine_kernel,
    coarse_kernel,
    excite_weight,
    middle_kernel,
    expand_weight,
    expand_gain,
    expand_bias,
    cotangent,
):
    depth = lax.axis_size("z")
    groups = 2 * depth
    assert frames.shape[0] == MICRO
    bits = bit_count(depth) + 3
    index = lax.axis_index(ALL)
    stem_total = float(4096 * groups)
    row_total = float(128 * groups)
    clip = lax.rem(index, 4).astype(jnp.int32)
    place = clip.reshape(1)
    bit_list = [lax.rem(lax.div(index, 1 << b), 2) for b in range(bits)]
    stays = jnp.where(bit_list[0] == bit_list[2], 1, 0)
    info = jnp.stack(bit_list + [stays]).astype(jnp.int32)
    plane = [(1, 2), (2, 1)]
    plane_mask = 6
    diff_flat = diff_kernel.reshape(54, STEM)
    fine_flat = fine_kernel.reshape(288, 32)
    coarse_flat = coarse_kernel.reshape(288, 32)
    gain_s = jnp.tile(stem_gain, 8)[None]
    bias_s = jnp.tile(stem_bias, 8)[None]
    gain_r = reduce_gain[None]
    bias_r = reduce_bias[None]
    gain_x = expand_gain[None]
    bias_x = expand_bias[None]

    def swapped(value, whole_route=False):
        return exchange(value, lambda i: swap_bits(i, 0, 2), whole_route)

    def along(value, choice):
        return exchange(value, lambda i: i ^ (1 << choice[i & 1]))

    def pooled_sum(value):
        return depth_pieces(value + by_mask(value, 1))

    def depth_pieces(value):
        if depth > 4:
            return (lax.psum(value, "z"),)
        return (value,) + tuple(by_mask(value, m << 3) for m in range(1, depth))

    def sums_shape(width):
        return shape((2, width))

    def to_plane(pieces):
        own, first, second, both = pieces
        return own, along(first, plane[0]), along(second, plane[1]), by_mask(both, plane_mask)

    def padded(rows):
        unit = 16 * depth
        return -(-rows // unit) * unit

    def far(*arrays):
        return tuple(Far(array) for array in arrays)

    def stack(*pieces, deps=()):
        rows = sum(piece.shape[0] for piece in pieces)
        return run(stack_rows, [shape((rows, pieces[0].shape[1]), BF)], pieces, deps=deps)[0]

    def add(first, second, deps=()):
        return run(add_floats, [shape(first.shape)], (first, second), deps=deps)[0]

    def halves(kernel, rows, arrays, deps=()):
        return run(
            kernel, [shape((rows // 2, 128), BF)] * 2, arrays, (info,),
            [pltpu.VMEM((rows, 128), BF)], deps=deps,
        )

    (pack,) = run(
        pack_clip,
        [shape((208, 64), BF)],
        (*far(cut_mask, offsets[None]), Far(frames, clip=True)),
        (place,),
    )
    pack = (pack, swapped(pack))

    def far_pack():
        return Far(pack[0], other=pack[1])

    stem_scratch = [
        pltpu.VMEM((512, 896), BF),
        pltpu.VMEM((256, 384), BF),
        pltpu.VMEM((896, 512), BF),
        pltpu.VMEM((384, 512), BF),
        pltpu.VMEM((192, 128), F32),
        pltpu.VMEM((512, 384), F32),
    ]
    stem_weights = far(stem_kernel.T, diff_flat)
    v, stem_sums = run(
        stem_front,
        [shape((512, 512)), sums_shape(512)],
        (far_pack(), *stem_weights),
        scratch=stem_scratch,
        choose=info,
    )
    stem_sums = pooled_sum(stem_sums)
    (cot,) = run(
        lambda place, *refs: copy_rows(*refs),
        [FarOut(shape(cotangent.shape[1:], BF))],
        (Far(cotangent, clip=True),),
        (place,),
        deps=(stem_sums[0],),
    )
    cot_got = swapped(cot)
    stem_norm = far(gain_s, bias_s)
    wide, wide_keep, send, red, red_sums, stem_saved = run(
        functools.partial(stem_close, stem_total),
        [
            FarOut(shape((128, 2048), BF)),
            shape((128, 1024), BF),
            shape((128, 1024), BF),
            shape((128, 512)),
            sums_shape(512),
            FarOut(shape((520, 512))),
        ],
        (v, stem_sums, *stem_norm, Far(reduce_weight)),
        (info,),
    )
    wide_pair = by_mask(send, 1)
    red_sums = pooled_sum(red_sums)
    wide_chip = stack(wide_keep, wide_pair, deps=(red_sums[0], cot_got))
    wide_got = along(wide_chip, plane[0])
    gate_weights = far(squeeze_weight.T, fine_flat, coarse_flat, excite_weight, middle_kernel)
    both_keep, send, expanded, exp_sums, saved = run(
        functools.partial(gate_front, row_total),
        [
            shape((128, 512), BF),
            shape((128, 512), BF),
            shape((128, 2048)),
            sums_shape(2048),
            FarOut(shape((264, 512)), [(0, 136), (136, 128)]),
        ],
        (
            red, red_sums, far_pack(), *far(gain_r, bias_r), *gate_weights, Far(expand_weight),
        ),
        (info,),
        [pltpu.VMEM((128, 1024), BF)],
        choose=info,
        deps=(wide_chip,),
    )
    both_pair = by_mask(send, 1)
    exp_sums = pooled_sum(exp_sums)
    both_chip = stack(both_keep, both_pair, deps=(exp_sums[0],))
    both_got = along(both_chip, plane[0])
    wide_near = stack(wide_chip, wide_got, deps=(both_chip,))
    wide_far = along(wide_near, plane[1])
    og_sums, out_saved = run(
        functools.partial(out_back, row_total),
        [
            sums_shape(2048),
            FarOut(shape((264, 2048)), [(0, 64), (128, 64), (64, 64), (192, 72)]),
        ],
        (expanded, exp_sums, *far(gain_x, bias_x, wide), Far(cot, other=cot_got)),
        choose=info,
        deps=(wide_near,),
    )
    og_sums = pooled_sum(og_sums)
    both_near = stack(both_chip, both_got, deps=(og_sums[0],))
    both_far = along(both_near, plane[1])
    hg, og_total, *blocks = run(
        functools.partial(expand_back, row_total),
        [shape((128, 512), BF), FarOut(shape((8, 2048)))] + [shape((128, 640), BF)] * 4,
        (og_sums, Far(out_saved), Far(saved, 136, 128), *far(gain_x, expand_weight)),
        (info,),
        [pltpu.VMEM((128, 512), BF), pltpu.VMEM((128, 2048), BF)],
        deps=(both_near,),
    )
    blocks = to_plane(blocks)
    rg, rg_sums, small = run(
        gate_back,
        [shape((128, 512)), sums_shape(512), shape((256, 256))],
        (far_pack(), hg, Far(saved, 0, 128), *far(gain_r, bias_r), *gate_weights),
        choose=info,
        deps=(wide_far, both_far),
    )
    rg_sums = pooled_sum(rg_sums)
    blocks = stack(*blocks, deps=(rg_sums[0],))
    blocks_pair = by_mask(blocks, 1)

    def depth_chain(keep, got):
        deps = yield
        for bit in range(4, bits):
            keep, send = halves(
                functools.partial(add_halves, bit), keep.shape[0], (keep, got), deps
            )
            got = by_mask(send, 1 << bit)
            deps = yield keep, None
        (value,) = run(add_rows, [shape(keep.shape, BF)], (keep, got), deps=deps)
        for bit in reversed(range(3, bits)):
            got = by_mask(value, 1 << bit)
            deps = yield value, None
            rows, width = value.shape
            (value,) = run(
                functools.partial(join_halves, bit),
                [shape((2 * rows, width), BF)],
                (value, got),
                (info,),
                deps=deps,
            )
        yield value, value

    def finish_chain(chain, deps):
        result = None
        while result is None:
            _, result = chain.send(deps)
        return result

    middle_rows = padded(2304)
    outer_rows = padded(2176)
    keep, send = halves(
        middle_weights, middle_rows, ((both_near, both_far), (blocks, blocks_pair)), rg_sums[1:]
    )
    middle_chain = depth_chain(keep, by_mask(send, 8))
    next(middle_chain)
    rs, rs_sums, rg_total, *late = run(
        functools.partial(reduce_back, row_total),
        [shape((512, 512)), sums_shape(512), FarOut(shape((8, 512)))]
        + [shape((128, 256), BF)] * 4,
        (
            small, rg, rg_sums, Far(saved, 0, 136), Far(gain_r), Far(out_saved, 0, 128),
            *far(reduce_weight, stem_saved), *stem_norm,
        ),
        (info,),
        [pltpu.VMEM((128, 512), BF)],
        deps=(keep,),
    )
    late = to_plane(late)
    last, _ = middle_chain.send((rs,))
    rs_here = add(rs_sums, by_mask(rs_sums, 1), (last,))
    late = stack(*late, deps=(rs_here,))
    keep, send = halves(
        outer_weights,
        outer_rows,
        (
            (both_near, both_far), (blocks, blocks_pair), (wide_near, wide_far),
            (late, by_mask(late, 1)),
        ),
    )
    outer_chain = depth_chain(keep, by_mask(send, 8))
    next(outer_chain)
    last, _ = middle_chain.send((keep,))
    last, _ = outer_chain.send((last,))
    last, _ = middle_chain.send((last,))
    last, _ = outer_chain.send((last,))
    middle = finish_chain(middle_chain, (last,))
    middle_got = along(middle, plane[1])
    last, _ = outer_chain.send((middle,))
    middle_near = stack(middle, middle_got, deps=(last,))
    middle_far = along(middle_near, plane[0])
    rs_sums = depth_pieces(rs_here)
    frame_grad, tail = run(
        functools.partial(stem_back, stem_total, 1.0 / groups),
        [shape((8, 3, 8, 64)), shape((200, 128))],
        (
            far_pack(), *stem_weights, Far(stem_saved), stem_norm[0], rs, rs_sums, Far(og_total),
            Far(rg_total),
        ),
        scratch=stem_scratch,
        choose=info,
        deps=(middle_near,),
    )
    outer = finish_chain(outer_chain, (tail,))
    outer_got = along(outer, plane[1])
    middle_far = stack(middle_far, deps=(outer,))

    def with_pair(near, far, rows):
        pieces = (near, far, by_mask(near, 1), by_mask(far, 1))
        return tuple(piece.reshape(2, rows, 128) for piece in pieces)

    tail = add(tail, by_mask(tail, 1), (outer,))
    tail = add(tail, by_mask(tail, 2))
    outer_near = stack(outer, outer_got, deps=(tail,))
    outer_far = along(outer_near, plane[0])
    dmiddle, token = finish(
        finish_middle, info, with_pair(middle_near, middle_far, middle_rows), (2, 768, 128),
        lambda i, info: (0, i, 0), (3,), shape((9, 512, 512)), (3, 512, 512),
        lambda i, info: (i, 0, 0), far=True, deps=(outer_near,),
    )
    tail = add(tail, by_mask(tail, 4), (token,))
    depth_bits = list(range(3, bits))
    for bit in depth_bits[:-1]:
        tail = add(tail, by_mask(tail, 1 << bit))
    tail_got = by_mask(tail, 1 << depth_bits[-1])
    frame_grad = swapped(frame_grad, True)
    outer_far = stack(outer_far, deps=(tail,))
    outer = with_pair(outer_near, outer_far, outer_rows)
    dexpand, dreduce, token = pl.pallas_call(
        lambda info, *refs: finish_outer(info, *refs[:-1]),
        grid_spec=pltpu.PrefetchScalarGridSpec(
            num_scalar_prefetch=1,
            grid=(4,),
            in_specs=[pl.BlockSpec((2, 1024, 128), lambda i, info: (0, 0, 0))] * 4
            + [pl.BlockSpec((2, 1024, 128), lambda i, info: (0, 1, 0))] * 4,
            out_specs=[
                pl.BlockSpec((256, 2048), lambda i, info: (jnp.minimum(i, 1), 0)),
                pl.BlockSpec((1024, 512), lambda i, info: (jnp.maximum(i - 2, 0), 0)),
                pl.BlockSpec((8, 128), lambda i, info: (0, 0)),
            ],
        ),
        out_shape=[shape((512, 2048)), shape((2048, 512)), shape((8, 128))],
        compiler_params=pltpu.CompilerParams(vmem_limit_bytes=FINISH_BYTES),
    )(info, *outer, *outer)
    small_shapes = ((32, 512), (32, 512), (9, 32, 32), (9, 32, 32), (64, 147), (9, 6, 64))
    small_shapes += tuple((1, n) for n in (64, 64, 512, 512, 2048, 2048))
    (
        dsqueeze, dexcite, dfine, dcoarse, dstem, ddiff, gain_s, bias_s, gain_r, bias_r, gain_x,
        bias_x,
    ) = pl.pallas_call(
        finish_small,
        grid_spec=pltpu.PrefetchScalarGridSpec(
            num_scalar_prefetch=1,
            grid=(1,),
            in_specs=[pl.BlockSpec((2, 128, 128), lambda i, info: (0, 16, 0))] * 4
            + [whole((200, 128))] * 2
            + [pl.BlockSpec(memory_space=pl.ANY)],
            out_specs=[whole(d) for d in small_shapes],
            scratch_shapes=[pltpu.VMEM((256, 256), F32), pltpu.VMEM((200, 128), F32)],
        ),
        out_shape=[shape(d) for d in small_shapes],
        compiler_params=pltpu.CompilerParams(vmem_limit_bytes=FINISH_BYTES),
    )(info, *outer, tail, tail_got, token)
    return (
        frame_grad[None],
        dstem.T,
        ddiff,
        gain_s[0],
        bias_s[0],
        dreduce,
        gain_r[0],
        bias_r[0],
        dsqueeze.T,
        dfine,
        dcoarse,
        dexcite,
        dmiddle,
        dexpand,
        gain_x[0],
        bias_x[0],
    )


def solution(mesh):
    split = jax.sharding.Mesh(mesh.devices.reshape(-1, 2, 2, 2), ALL)
    copied = P()
    by_group = P(("z", "y"))
    in_specs = (by_group,) * 3 + (copied,) * 15 + (by_group,)
    out_specs = (P(ALL),) + (copied,) * 15
    return jax.shard_map(body, mesh=split, in_specs=in_specs, out_specs=out_specs, check_vma=False)
```

```python
import functools

import jax
import jax.numpy as jnp
from jax import lax
from jax.experimental import pallas as pl
from jax.experimental.pallas import tpu as pltpu
from jax.sharding import PartitionSpec as P

FRAMES = 8
MICRO = 4
EPSILON = 1e-05
COST = 1_000_000
ORDER = (
    ("K", "R", "Ma", "St", "Rs", "Mb", "O", "Mc", "Oa", "Z", "Md", "B", "Ob", "Mn", "Oc", "Od")
    + ("T0", "T3", "Mf", "On", "T4", "F", "G")
)
FINISH_BYTES = 16 * 1024 * 1024
VMEM_BYTES = 32 * 1024 * 1024
BF = jnp.bfloat16
F32 = jnp.float32

STEM = 64
SLOT = 16


def dot(left, right):
    return jnp.dot(left, right, preferred_element_type=F32)


def dot_nt(left, right):
    return lax.dot_general(left, right, (((1,), (1,)), ((), ())), preferred_element_type=F32)


def dot_tn(left, right):
    return lax.dot_general(left, right, (((0,), (0,)), ((), ())), preferred_element_type=F32)


def dot_exact(left, right):
    return jnp.dot(left, right, preferred_element_type=F32, precision=lax.Precision.HIGHEST)


def iota(shape, dim):
    return lax.broadcasted_iota(jnp.int32, shape, dim)


def sigmoid(v):
    return 1.0 / (1.0 + jnp.exp(-v))


def swish_slope(v):
    s = sigmoid(v)
    return s * (1.0 + v * (1.0 - s))


def keep_column(pack, lanes):
    rows = pack[192:208, :].astype(F32)
    return jnp.concatenate(
        [jnp.broadcast_to(rows[f : f + 1, :lanes], (8, lanes)) for f in range(FRAMES)], 0
    )


def gate_column(pack):
    keep = keep_column(pack, 64)
    both = jnp.concatenate([keep, keep], 1)
    return jnp.concatenate([jnp.zeros((8, 128), F32), both[:-8]], 0)


def pack_clip(place, cut, offset, frames, out):
    clip = place[0]
    row = cut[pl.ds(clip, 1), :]
    own = iota((1, MICRO), 1) == clip
    stop = jnp.sum(jnp.where(own, offset[...], 0), 1, keepdims=True)
    step = iota(row.shape, 1)
    valid = jnp.where(step + 1 == stop, 0, row).astype(F32)
    spread = iota((16, FRAMES - 1), 0) == iota((16, FRAMES - 1), 1)
    column = jnp.sum(jnp.where(spread, valid, 0.0), 1, keepdims=True)
    out[0:192, :] = frames[...].astype(F32).reshape(192, 64).astype(BF)
    out[192:208, :] = jnp.broadcast_to(column, (16, 64)).astype(BF)


def summed_up(pieces):
    value = pieces[0][...]
    for piece in pieces[1:]:
        value = value + piece[...]
    return value


def spread_sums(out, first, second):
    out[...] = jnp.concatenate([first, second], 0)


def norm_scale(sums, row_total):
    mean = sums[0:1] * (1.0 / row_total)
    variance = sums[1:2] * (1.0 / row_total) - mean * mean
    return mean, lax.rsqrt(variance + EPSILON)


def column_sums(out, first, second):
    spread_sums(out, jnp.sum(first, 0, keepdims=True), jnp.sum(second, 0, keepdims=True))


def fold_lanes(sums):
    for step in (64, 128, 256):
        sums = sums + pltpu.roll(sums, step, 1)
    return sums


def shift_rows(v, dy, dx):
    rows = v.shape[0]
    if dx:
        rolled = pltpu.roll(v, (-dx) % rows, 0)
        wb = lax.rem(iota(v.shape, 0), 8)
        v = jnp.where((wb + dx >= 0) & (wb + dx < 8), rolled, 0.0)
    half = rows // 2
    if dy == 1:
        v = jnp.concatenate([v[half:], jnp.zeros_like(v[half:])], 0)
    elif dy == -1:
        v = jnp.concatenate([jnp.zeros_like(v[:half]), v[:half]], 0)
    return v


def cell_sum(v):
    half = v.shape[0] // 2
    both = v[:half] + v[half:]
    even = lax.rem(iota(both.shape, 0), 2) == 0
    both = both + jnp.where(even, pltpu.roll(both, half - 1, 0), pltpu.roll(both, 1, 0))
    return jnp.concatenate([both, both], 0)


def taps(v):
    return [shift_rows(v, ky - 1, kx - 1) for ky in range(3) for kx in range(3)]


def back_taps(v):
    return [shift_rows(v, 1 - ky, 1 - kx) for ky in range(3) for kx in range(3)]


def coarse_taps(v):
    return [shift_rows(v, 0, 2 * (k - 1)) for k in range(3)]


def window_select(rows, cols, kind):
    place = iota((rows, cols), 0)
    col = iota((rows, cols), 1)
    lane = lax.rem(place, 128)
    tap_row = lax.div(place, 128)
    channel = lax.div(lane, SLOT)
    slot = lax.rem(lane, SLOT)
    if kind == "stem":
        hit = (col == (7 * tap_row + slot) * 3 + channel) & (slot < 7) & (channel < 3)
        return jnp.where(hit, 1.0, 0.0)
    cell = lax.div(slot - 1, 2)
    hit = (col == (3 * tap_row + cell) * 6 + channel) & (slot >= 1) & (slot < 7) & (channel < 6)
    return jnp.where(hit, 0.25, 0.0)


def spread_select():
    w = iota((64, 128), 0)
    lane = iota((64, 128), 1)
    return jnp.where(w == 8 * lax.div(lane, SLOT) + lax.rem(lane, SLOT) - 3, 1.0, 0.0)


def gather_select():
    row = iota((384, 128), 0)
    col = iota((384, 128), 1)
    return jnp.where(col == lax.div(row, 128) * SLOT + lax.rem(row, SLOT), 1.0, 0.0)


def own_block():
    row = iota((8, 128), 0)
    lane = iota((8, 128), 1)
    return jnp.where(lax.div(lane, SLOT) == row, 1.0, 0.0)


def stem_windows(pack, kernel, diff, win, win2, u, u2, spread, tiles):
    spread[...] = dot(pack[0:192, :], spread_select().astype(BF))
    mask = own_block()
    for f in range(8):
        for c in range(3):
            for h in range(8):
                line = f * 24 + c * 8 + h
                tiles[h * 64 + f * 8 : h * 64 + f * 8 + 8, c * 128 : c * 128 + 128] = (
                    jnp.broadcast_to(spread[line : line + 1, :], (8, 128)) * mask
                )
    pixels = dot(tiles[...].astype(BF), gather_select().astype(BF))
    rows = [pixels[64 * h : 64 * h + 64] for h in range(8)]
    gate = gate_column(pack)
    steps = []
    for h2 in range(4):
        both = rows[2 * h2] + rows[2 * h2 + 1]
        step = (both - jnp.concatenate([jnp.zeros((8, 128), F32), both[:-8]], 0)) * gate
        later = jnp.concatenate([step[8:], jnp.zeros((8, 128), F32)], 0)
        steps.append((step + pltpu.roll(later, 48, 1)).astype(BF))
    rows = [r.astype(BF) for r in rows]
    blank = jnp.zeros((64, 128), BF)
    for dy in range(7):
        for h in range(8):
            source = h + dy - 3
            win[64 * h : 64 * h + 64, 128 * dy : 128 * dy + 128] = (
                rows[source] if 0 <= source < 8 else blank
            )
    for dy in range(3):
        for h in range(4):
            source = h + dy - 1
            win2[64 * h : 64 * h + 64, 128 * dy : 128 * dy + 128] = (
                steps[source] if 0 <= source < 4 else blank
            )
    low_half = iota((896, 128), 1) < 64
    wide_kernel = jnp.concatenate([kernel[...], kernel[...]], 0)
    placed = dot_nt(window_select(896, 147, "stem").astype(BF), wide_kernel)
    taps = diff[...].astype(F32)
    rows = jnp.concatenate([taps[k] for k in range(9)], 0)
    wide_diff = jnp.concatenate([rows, rows], 1).astype(BF)
    placed2 = dot(window_select(384, 54, "diff").astype(BF), wide_diff)
    for q in range(4):
        first = pltpu.roll(placed, 2 * q, 0) if q else placed
        second = pltpu.roll(placed, 2 * q + 1, 0)
        u[:, 128 * q : 128 * q + 128] = jnp.where(low_half, first, second).astype(BF)
        u2[:, 128 * q : 128 * q + 128] = (
            pltpu.roll(placed2, 2 * q, 0) if q else placed2
        ).astype(BF)


class Pick:
    def __init__(self, info, own, other):
        self.stays = info[info.shape[0] - 1] == 1
        self.own, self.other = own, other

    def __getitem__(self, place):
        return jnp.where(self.stays, self.own[place], self.other[place])


def stem_front(
    info, pack, kernel, diff, v_out, sums_out, win, win2, u, u2, spread, tiles
):
    stem_windows(Pick(info, *pack), kernel, diff, win, win2, u, u2, spread, tiles)
    v = dot(win[...], u[...])
    side = dot(win2[...], u2[...])
    first = jnp.zeros((1, 512), F32)
    second = jnp.zeros((1, 512), F32)
    for h in range(8):
        piece = v[64 * h : 64 * h + 64] + side[64 * (h // 2) : 64 * (h // 2) + 64]
        v_out[64 * h : 64 * h + 64, :] = piece
        first = first + jnp.sum(piece, 0, keepdims=True)
        second = second + jnp.sum(piece * piece, 0, keepdims=True)
    spread_sums(sums_out, first, second)


def stem_close(
    row_total, info, v, sums, gain, bias, weight, wide_out, keep_out, send_out, red_out, sums_out,
    save,
):
    mean, scale = norm_scale(fold_lanes(summed_up(sums)), row_total)
    save[512:513, :] = scale
    for h in range(8):
        normal = (v[64 * h : 64 * h + 64, :] - mean) * scale
        save[64 * h : 64 * h + 64, :] = normal
        y = normal * gain[...] + bias[...]
        wide_out[
            64 * (h // 4) : 64 * (h // 4) + 64, 512 * (h % 4) : 512 * (h % 4) + 512
        ] = (y * sigmoid(y)).astype(BF)
    save.flush()
    wide_out.flush()
    keep_out[...] = wide_out[:, lanes(1024 * info[0], 1024)]
    send_out[...] = wide_out[:, lanes(1024 * (1 - info[0]), 1024)]
    red = dot(wide_out[...], weight[...])
    red_out[...] = red
    column_sums(sums_out, red, red * red)


def gate_path(pack, narrow, squeeze, fine, coarse, excite):
    squeezed = dot_nt(narrow.astype(BF), squeeze[...])
    keep = keep_column(pack, 32)
    parts = []
    for hb in range(2):
        part = squeezed[64 * hb : 64 * hb + 64]
        later = jnp.concatenate([part[8:], part[:8]], 0)
        parts.append((later - part) * keep)
    change = jnp.concatenate(parts, 0)
    fine_rows = jnp.concatenate(taps(change), 1).astype(BF)
    pooled = 0.25 * cell_sum(change)
    coarse_rows = jnp.concatenate(coarse_taps(pooled), 1).astype(BF)
    summed = (dot(fine_rows, fine[...]) + dot(coarse_rows, coarse[96:192, :])).astype(BF)
    return fine_rows, coarse_rows, summed, sigmoid(dot(summed, excite[...]))


def gate_front(
    row_total, info, red, sums, pack, gain, bias, squeeze, fine, coarse, excite, middle, expand,
    keep_out, send_out, exp_out, sums_out, save, both,
):
    mean, scale = norm_scale(summed_up(sums), row_total)
    normal = (red[...] - mean) * scale
    save[0:128, :] = normal
    save[128:129, :] = scale
    save.flush()
    y = normal * gain[...] + bias[...]
    narrow = y * sigmoid(y)
    gate = gate_path(pack, narrow, squeeze, fine, coarse, excite)[3]
    gated = narrow * (1.0 + gate)
    total = jnp.zeros((128, 512), F32)
    for k, piece in enumerate(taps(gated)):
        total = total + dot(piece.astype(BF), middle[k])
    save[136:264, :] = total
    save.flush()
    hidden = (total * sigmoid(total)).astype(BF)
    for half in range(2):
        part = slice(256 * half, 256 * half + 256)
        both[:, 512 * half : 512 * half + 256] = gated[:, part].astype(BF)
        both[:, 512 * half + 256 : 512 * half + 512] = hidden[:, part]
    keep_out[...] = both[:, lanes(512 * info[0], 512)]
    send_out[...] = both[:, lanes(512 * (1 - info[0]), 512)]
    expanded = dot(hidden, expand[...])
    exp_out[...] = expanded
    column_sums(sums_out, expanded, expanded * expanded)


def out_back(row_total, expanded, sums, gain, bias, wide, cot, sums_out, save):
    mean, scale = norm_scale(summed_up(sums), row_total)
    save[256:257, :] = scale
    first = jnp.zeros((1, 2048), F32)
    second = jnp.zeros((1, 2048), F32)
    for hb in range(2):
        part = slice(64 * hb, 64 * hb + 64)
        if hb:
            save.flush()
            save.flush()
        normal = (expanded[part, :] - mean) * scale
        y = normal * gain[...] + bias[...] + wide[part, :].astype(F32)
        weightless = cot[:, hb, :, :].astype(F32).reshape(64, 2048)
        og = weightless * swish_slope(y)
        save[part, :] = og
        save[128 + 64 * hb : 192 + 64 * hb, :] = normal
        first = first + jnp.sum(og, 0, keepdims=True)
        second = second + jnp.sum(og * normal, 0, keepdims=True)
    spread_sums(sums_out, first, second)


def norm_pull(grad, normal, scale, gain, grad_sums, row_total):
    return (
        gain
        * scale
        * (
            grad
            - grad_sums[0:1] * (1.0 / row_total)
            - normal * (grad_sums[1:2] * (1.0 / row_total))
        )
    )


def block_order(info, partner=False):
    block = 2 * info[1] + info[2]
    first = jnp.where((info[0] == 0) != partner, 2, 1)
    return [block, block ^ first, block ^ (3 - first), block ^ 3]


def lanes(start, width):
    return pl.ds(pl.multiple_of(start, 128), width)


def expand_back(
    row_total, info, grad_sums, saved, hpre, gain, expand, hg_out, total_out, *rest
):
    outs, (hg_scratch, dv_scratch) = rest[:4], rest[4:]
    sums = summed_up(grad_sums)
    total_out[0:2, :] = sums
    total_out.flush()
    dv = norm_pull(
        saved[0:128, :], saved[128:256, :], saved[256:257, :], gain[...], sums, row_total
    ).astype(BF)
    dv_scratch[...] = dv
    dhid = dot_nt(dv, expand[...]).astype(BF).astype(F32)
    hg = (dhid * swish_slope(hpre[...])).astype(BF)
    hg_out[...] = hg
    hg_scratch[...] = hg
    for out, block in zip(outs, block_order(info)):
        out[:, :128] = hg_scratch[:, lanes(128 * block, 128)]
        out[:, 128:] = dv_scratch[:, lanes(512 * block, 512)]


def all_rows(refs):
    return jnp.concatenate([ref[...] for ref in refs], 0)


def clip_rows(mine, pair, columns):
    rows = []
    for k, other in enumerate((0, 2, 1, 3)):
        rows.append(mine[128 * k : 128 * k + 128, columns])
        rows.append(pair[128 * other : 128 * other + 128, columns])
    return rows


def depth_halves(info, bit, scratch, keep_out, send_out):
    rows = keep_out.shape[0]
    mine = info[bit]
    keep_out[...] = scratch[pl.ds(pl.multiple_of(mine * rows, 16), rows), :]
    send_out[...] = scratch[pl.ds(pl.multiple_of((1 - mine) * rows, 16), rows), :]


def add_halves(bit, info, keep, got, keep_out, send_out, scratch):
    scratch[...] = (keep[...].astype(F32) + got[...].astype(F32)).astype(BF)
    depth_halves(info, bit, scratch, keep_out, send_out)


def add_rows(keep, got, out):
    out[...] = (keep[...].astype(F32) + got[...].astype(F32)).astype(BF)


def join_halves(bit, info, own, got, out):
    rows = own.shape[0]
    mine = info[bit]
    out[pl.ds(pl.multiple_of(mine * rows, 16), rows), :] = own[...]
    out[pl.ds(pl.multiple_of((1 - mine) * rows, 16), rows), :] = got[...]


def middle_weights(info, left_refs, right_refs, *rest):
    outs, (scratch,) = rest[:-1], rest[-1:]
    left = jnp.concatenate([ref[:, :256] for ref in left_refs], 0).T
    clips = [
        back_taps(rows.astype(F32)) for rows in clip_rows(*right_refs, slice(0, 128))
    ]
    for k in range(9):
        right = jnp.concatenate([clip[k] for clip in clips], 0).astype(BF)
        scratch[256 * k : 256 * k + 256, :] = dot(left, right).astype(BF)
    if scratch.shape[0] > 2304:
        scratch[2304:, :] = jnp.zeros((scratch.shape[0] - 2304, 128), BF)
    depth_halves(info, 3, scratch, *outs)


def outer_weights(info, left_refs, right_refs, wide, late, *rest):
    outs, (scratch,) = rest[:-1], rest[-1:]
    left = jnp.concatenate([ref[:, 256:] for ref in left_refs], 0)
    right = jnp.concatenate(clip_rows(*right_refs, slice(128, 640)), 0)
    result = dot_tn(left, right).astype(BF)
    for q in range(4):
        scratch[256 * q : 256 * q + 256, :] = result[:, 128 * q : 128 * q + 128]
    right = jnp.concatenate(clip_rows(*late, slice(0, 128)), 0)
    scratch[1024:2048, :] = dot_tn(all_rows(wide), right).astype(BF)
    small = [late[0][128 * k : 128 * k + 128, 128:].astype(F32) for k in range(4)]
    scratch[2048:2176, :] = sum(small).astype(BF)
    if scratch.shape[0] > 2176:
        scratch[2176:, :] = jnp.zeros((scratch.shape[0] - 2176, 128), BF)
    depth_halves(info, 3, scratch, *outs)


def copy_rows(source, out):
    out[...] = source[...]


def add_floats(first, second, out):
    out[...] = first[...] + second[...]


def stack_rows(*refs):
    out = refs[-1]
    start = 0
    for ref in refs[:-1]:
        out[start : start + ref.shape[0], :] = ref[...]
        start += ref.shape[0]


def gate_back(
    pack, hg, normal, gain, bias, squeeze, fine, coarse, excite, middle,
    rg_out, sums_out, small_out,
):
    y = normal[...] * gain[...] + bias[...]
    narrow_v = y * sigmoid(y)
    fine_rows, coarse_rows, summed, gate_v = gate_path(
        pack, narrow_v, squeeze, fine, coarse, excite
    )
    total = jnp.zeros((128, 512), F32)
    for k, piece in enumerate(back_taps(hg[...].astype(F32))):
        total = total + dot_nt(piece.astype(BF), middle[k])
    gg = total.astype(BF).astype(F32)
    narrow_grad = gg * (1.0 + gate_v)
    excite_grad = (gg * narrow_v * gate_v * (1.0 - gate_v)).astype(BF)
    dexcite = dot_tn(summed, excite_grad)
    summed_low = dot_nt(excite_grad, excite[...]).astype(BF)
    summed_grad = summed_low.astype(F32)
    coarse_low = cell_sum(summed_grad).astype(BF)
    dfine = dot_tn(fine_rows, summed_low)
    dcoarse = 0.25 * dot_tn(coarse_rows, coarse_low)
    spread = dot_nt(summed_low, fine[...])
    change_grad = jnp.zeros((128, 32), F32)
    for k in range(9):
        change_grad = change_grad + shift_rows(
            spread[:, 32 * k : 32 * k + 32], 1 - k // 3, 1 - k % 3
        )
    spread = dot_nt(coarse_low, coarse[96:192, :])
    pooled_grad = jnp.zeros((128, 32), F32)
    for k in range(3):
        pooled_grad = pooled_grad + shift_rows(spread[:, 32 * k : 32 * k + 32], 0, 2 * (1 - k))
    change_grad = change_grad + 0.25 * pooled_grad
    keep = keep_column(pack, 32)
    parts = []
    for hb in range(2):
        step = change_grad[64 * hb : 64 * hb + 64] * keep
        earlier = jnp.concatenate([step[56:], step[:56]], 0)
        parts.append(earlier - step)
    squeezed_grad = jnp.concatenate(parts, 0).astype(BF)
    dsqueeze = dot_tn(squeezed_grad, narrow_v.astype(BF))
    narrow_grad = narrow_grad + dot(squeezed_grad, squeeze[...])
    rg = narrow_grad * swish_slope(y)
    rg_out[...] = rg
    column_sums(sums_out, rg, rg * normal[...])
    small_out[0:32, :] = dsqueeze[:, :256]
    small_out[32:64, :] = dsqueeze[:, 256:]
    small_out[64:96, :] = dexcite[:, :256]
    small_out[96:128, :] = dexcite[:, 256:]
    pieces = [dfine[32 * k : 32 * k + 32] for k in range(9)]
    pieces += [dcoarse[32 * k : 32 * k + 32] for k in range(3)]
    small_out[128:160, :] = jnp.concatenate(pieces[:8], 1)
    small_out[160:192, :] = jnp.concatenate(pieces[8:] + [jnp.zeros((32, 128), F32)], 1)
    small_out[192:256, :] = jnp.zeros((64, 256), F32)


def reduce_back(
    row_total, info, small, rg, grad_sums, saved, gain, og, weight, stem_saved, stem_gain,
    stem_bias, rs_out, sums_out, total_out, dv0, dv1, dv2, dv3, dv_scratch,
):
    sums = summed_up(grad_sums)
    total_out[0:2, :] = sums
    total_out.flush()
    dv = norm_pull(
        rg[...], saved[0:128, :], saved[128:129, :], gain[...], sums, row_total
    ).astype(BF)
    dv_scratch[...] = dv
    for out, block in zip((dv0, dv1, dv2, dv3), block_order(info)):
        out[:, :128] = dv_scratch[:, lanes(128 * block, 128)]
        part = small[pl.ds(pl.multiple_of(64 * block, 64), 64), :].astype(BF)
        out[:64, 128:] = part[:, :128]
        out[64:, 128:] = part[:, 128:]
    wide_grad = dot_nt(dv, weight[...]) + og[...].astype(BF).astype(F32)
    wide_grad = wide_grad.astype(BF).astype(F32)
    first = jnp.zeros((1, 512), F32)
    second = jnp.zeros((1, 512), F32)
    for h in range(8):
        normal = stem_saved[64 * h : 64 * h + 64, :]
        y = normal * stem_gain[...] + stem_bias[...]
        rs = (
            wide_grad[64 * (h // 4) : 64 * (h // 4) + 64, 512 * (h % 4) : 512 * (h % 4) + 512]
            * swish_slope(y)
        )
        rs_out[64 * h : 64 * h + 64, :] = rs
        first = first + jnp.sum(rs, 0, keepdims=True)
        second = second + jnp.sum(rs * normal, 0, keepdims=True)
    spread_sums(sums_out, first, second)


def stem_back(
    stem_total, share, pack, kernel, diff, saved, gain, rs, grad_sums, og_total,
    rg_total, frames_out, tail_out, win, win2, u, u2, lines, tiles,
):
    stem_windows(pack, kernel, diff, win, win2, u, u2, lines, tiles)
    scale = saved[512:513, :]
    totals = fold_lanes(summed_up(grad_sums))
    rows = []
    pairs = []
    for h in range(8):
        part = slice(64 * h, 64 * h + 64)
        normal = saved[part, :]
        pre = norm_pull(rs[part, :], normal, scale, gain[...], totals, stem_total)
        rows.append(pre.astype(BF))
        if h % 2:
            pairs.append((before + pre).astype(BF))
        before = pre
    dv = jnp.concatenate(rows, 0)
    dside = jnp.concatenate(pairs, 0)

    low_half = iota((896, 128), 1) < 64
    du = dot_tn(win[...], dv)
    placed = jnp.zeros((896, 128), F32)
    for q in range(4):
        part = du[:, 128 * q : 128 * q + 128]
        first = pltpu.roll(part, 896 - 2 * q, 0) if q else part
        placed = placed + jnp.where(low_half, first, pltpu.roll(part, 896 - 2 * q - 1, 0))
    placed = placed + pltpu.roll(placed, 64, 1)
    tail_out[0:147, 0:64] = lax.dot_general(
        window_select(896, 147, "stem"), placed, (((0,), (0,)), ((), ())),
        preferred_element_type=F32, precision=lax.Precision.HIGHEST,
    )[:, :64]
    du2 = dot_tn(win2[...], dside)
    placed = jnp.zeros((384, 128), F32)
    for q in range(4):
        part = du2[:, 128 * q : 128 * q + 128]
        placed = placed + (pltpu.roll(part, 384 - 2 * q, 0) if q else part)
    placed = placed + pltpu.roll(placed, 64, 1)
    tail_out[0:54, 64:128] = lax.dot_general(
        window_select(384, 54, "diff"), placed, (((0,), (0,)), ((), ())),
        preferred_element_type=F32, precision=lax.Precision.HIGHEST,
    )[:, :64]

    dwin = dot_nt(dv, u[...])
    dwin2 = dot_nt(dside, u2[...])
    gate = gate_column(pack)
    steps = []
    for h2 in range(4):
        total = jnp.zeros((64, 128), F32)
        for dy in range(3):
            target = h2 + 1 - dy
            if 0 <= target < 4:
                total = total + dwin2[64 * target : 64 * target + 64, 128 * dy : 128 * dy + 128]
        later = pltpu.roll(total, 80, 1)
        later = jnp.concatenate([jnp.zeros((8, 128), F32), later[:-8]], 0)
        step = (total + later) * gate
        steps.append(step - jnp.concatenate([step[8:], jnp.zeros((8, 128), F32)], 0))
    pixels = []
    for h in range(8):
        total = steps[h // 2]
        for dy in range(7):
            target = h + 3 - dy
            if 0 <= target < 8:
                total = total + dwin[64 * target : 64 * target + 64, 128 * dy : 128 * dy + 128]
        pixels.append(total)
    pixels = jnp.concatenate(pixels, 0)
    back = lax.dot_general(
        pixels, gather_select(), (((1,), (1,)), ((), ())),
        preferred_element_type=F32, precision=lax.Precision.HIGHEST,
    )
    mask = own_block()
    for f in range(8):
        for c in range(3):
            for h in range(8):
                line = f * 24 + c * 8 + h
                block = back[h * 64 + f * 8 : h * 64 + f * 8 + 8, c * 128 : c * 128 + 128]
                lines[line : line + 1, :] = jnp.sum(block * mask, 0, keepdims=True)
    flat = lax.dot_general(
        lines[...], spread_select(), (((1,), (1,)), ((), ())),
        preferred_element_type=F32, precision=lax.Precision.HIGHEST,
    )
    frames_out[...] = flat.reshape(8, 3, 8, 64)
    og_all = og_total[0:2, :]
    rg_all = rg_total[0:2, :]
    for q in range(16):
        tail_out[152 + 2 * q : 154 + 2 * q, :] = og_all[:, 128 * q : 128 * q + 128] * share
    for q in range(4):
        tail_out[184 + 2 * q : 186 + 2 * q, :] = rg_all[:, 128 * q : 128 * q + 128] * share
    tail_out[192:194, :] = totals[:, :128] * share


def plane_pieces(near, far):
    return near.at[0], far.at[0], near.at[1], far.at[1]


def send_tiles(tiles, buffer, semaphores):
    copies = []
    for k, (fill, target) in enumerate(tiles):
        fill(buffer.at[k])
        copies.append(pltpu.make_async_copy(buffer.at[k], target, semaphores.at[k]))
        copies[-1].start()
    return copies


def finish_middle(info, near, far, near2, far2, *rest):
    out, token, buffer, semaphores = rest[-4:]
    token[...] = jnp.zeros(token.shape, F32)
    tiles = []
    for one, two, bit, partner in (
        (near, far, info[0], False), (near2, far2, 1 - info[0], True)
    ):
        row = pl.ds(pl.multiple_of(256 * bit, 128), 256)
        for piece, block in zip(plane_pieces(one, two), block_order(info, partner)):

            def fill(target, piece=piece):
                for tap in range(9):
                    target[tap] = piece[256 * tap : 256 * tap + 256, :].astype(F32)

            tiles.append((fill, out.at[:, row, lanes(128 * block, 128)]))
    for copy in send_tiles(tiles, buffer, semaphores):
        copy.wait()


def start_outer(
    first, info, mine, pair, expand_out, reduce_out,
    expand_buffer, reduce_buffer, expand_semaphores, reduce_semaphores,
):
    expand_tiles, reduce_tiles = [], []
    for pieces, bit, partner in ((mine, info[0], False), (pair, 1 - info[0], True)):
        order = block_order(info, partner)
        expand_row = pl.ds(pl.multiple_of(256 * bit, 128), 256)
        reduce_row = pl.ds(pl.multiple_of(1024 * bit, 128), 1024)
        for k, block in enumerate((order[1], order[3]) if first else (order[0], order[2])):

            def fill_expand(target, piece=pieces.at[k]):
                for q in range(4):
                    tile = piece[256 * q : 256 * q + 256, :].astype(F32)
                    target[:, 128 * q : 128 * q + 128] = tile

            def fill_reduce(target, piece=pieces.at[k]):
                target[...] = piece[1024:2048, :].astype(F32)

            expand_tiles.append((fill_expand, expand_out.at[expand_row, lanes(512 * block, 512)]))
            reduce_tiles.append((fill_reduce, reduce_out.at[reduce_row, lanes(128 * block, 128)]))
    copies = send_tiles(expand_tiles, expand_buffer, expand_semaphores)
    return copies + send_tiles(reduce_tiles, reduce_buffer, reduce_semaphores)


def finish_outer(first, info, mine, pair, *rest):
    expand_out, reduce_out, token = rest[-7:-4]
    token[...] = jnp.zeros(token.shape, F32)
    for copy in start_outer(first, info, mine, pair, expand_out, reduce_out, *rest[-4:]):
        copy.wait()


def finish_small(
    info, near, far, near2, far2, tail0, tail1, tail2, tail3,
    dsqueeze, dexcite, dfine, dcoarse, stem_out, diff_out, gain_s, bias_s, gain_r, bias_r,
    gain_x, bias_x, scratch, tail,
):
    for one, two, partner in ((near, far, False), (near2, far2, True)):
        for piece, block in zip(plane_pieces(one, two), block_order(info, partner)):
            rows = pl.ds(pl.multiple_of(64 * block, 64), 64)
            here = jnp.concatenate([piece[0:64, :], piece[64:128, :]], 1).astype(F32)
            scratch[rows, :] = scratch[rows, :] + here if partner else here
    tail[...] = tail0[...] + tail1[...] + tail2[...] + tail3[...]
    rows = scratch[...]
    dsqueeze[:, :256] = rows[0:32]
    dsqueeze[:, 256:] = rows[32:64]
    dexcite[:, :256] = rows[64:96]
    dexcite[:, 256:] = rows[96:128]
    for k in range(8):
        dfine[k] = rows[128:160, 32 * k : 32 * k + 32]
    dfine[8] = rows[160:192, 0:32]
    for k in range(9):
        dcoarse[k] = (
            rows[160:192, 32 * (k - 2) : 32 * (k - 2) + 32]
            if 3 <= k < 6
            else jnp.zeros((32, 32), F32)
        )
    stem_out[...] = tail[0:152, :].T[0:64, 0:147]
    for k in range(9):
        diff_out[k] = tail[6 * k : 6 * k + 6, 64:128]
    for q in range(16):
        bias_x[:, 128 * q : 128 * q + 128] = tail[152 + 2 * q : 153 + 2 * q, :]
        gain_x[:, 128 * q : 128 * q + 128] = tail[153 + 2 * q : 154 + 2 * q, :]
    for q in range(4):
        bias_r[:, 128 * q : 128 * q + 128] = tail[184 + 2 * q : 185 + 2 * q, :]
        gain_r[:, 128 * q : 128 * q + 128] = tail[185 + 2 * q : 186 + 2 * q, :]
    bias_s[...] = tail[192:193, :64]
    gain_s[...] = tail[193:194, :64]


def finish_rest(info, near, far, near2, far2, tail0, tail1, tail2, tail3, frames, *rest):
    rest[1][0] = frames[...]
    finish_small(info, near, far, near2, far2, tail0, tail1, tail2, tail3, *rest[2:])


def shape(dims, dtype=F32):
    return jax.ShapeDtypeStruct(dims, dtype)


def whole(dims):
    count = len(dims)
    return pl.BlockSpec(dims, lambda i, *scalars: (0,) * count)


class Far:
    def __init__(self, array, start=0, rows=None, clip=False, other=None):
        self.array, self.start, self.rows, self.clip = array, start, rows, clip
        self.other = other

    def arrays(self):
        return [self.array] if self.other is None else [self.array, self.other]

    def buffer(self):
        dims = self.array.shape
        if self.clip:
            dims = dims[1:]
        elif self.rows is not None:
            dims = (self.rows,) + dims[1:]
        return pltpu.VMEM(dims, self.array.dtype)

    def source(self, ref, scalars):
        if self.clip:
            return ref.at[scalars[0][0]]
        if self.rows is not None:
            return ref.at[pl.ds(self.start, self.rows)]
        return ref


jax.tree_util.register_pytree_node(
    Far,
    lambda far: ((far.array, far.other), (far.start, far.rows, far.clip)),
    lambda rest, children: Far(children[0], *rest, children[1]),
)


class FarRef:
    def __init__(self, sources, buffer, semaphore, info):
        self.copy = pltpu.make_async_copy(sources[0], buffer, semaphore)
        if len(sources) == 1:
            self.copy.start()
        else:
            other = pltpu.make_async_copy(sources[1], buffer, semaphore)
            pl.when(info[info.shape[0] - 1] == 1)(self.copy.start)
            pl.when(info[info.shape[0] - 1] == 0)(other.start)
        self.buffer, self.pending = buffer, True
        self.shape = buffer.shape

    def wait(self):
        if self.pending:
            self.copy.wait()
            self.pending = False

    def __getitem__(self, place):
        self.wait()
        return self.buffer[place]


class FarOut:
    def __init__(self, out, parts=None):
        self.out = out
        self.parts = parts or [(0, out.shape[0])]


class FarOutRef:
    def __init__(self, buffer, home, semaphores, parts):
        self.buffer, self.shape = buffer, buffer.shape
        self.copies = [
            pltpu.make_async_copy(
                buffer.at[pl.ds(start, rows)], home.at[pl.ds(start, rows)], semaphore
            )
            for (start, rows), semaphore in zip(parts, semaphores)
        ]
        self.started = 0

    def __getitem__(self, place):
        return self.buffer[place]

    def __setitem__(self, place, value):
        self.buffer[place] = value

    def flush(self):
        self.copies[self.started].start()
        self.started += 1

    def finish(self):
        while self.started < len(self.copies):
            self.flush()
        for copy in self.copies:
            copy.wait()


def run(
    kernel, outs, arrays, scalars=(), scratch=(), choose=None, deps=(), cost=COST
):
    flat, tree = jax.tree.flatten(tuple(arrays), is_leaf=lambda x: isinstance(x, Far))
    operands, in_specs, places = [], [], []
    for array in flat:
        places.append(len(operands))
        if isinstance(array, Far):
            for piece in array.arrays():
                operands.append(pltpu.with_memory_space_constraint(piece, pltpu.HBM))
                in_specs.append(pl.BlockSpec(memory_space=pltpu.HBM))
            continue
        operands.append(array)
        in_specs.append(whole(array.shape))
    read = len(operands)
    for array in deps:
        operands.append(array)
        in_specs.append(pl.BlockSpec(memory_space=pl.ANY))
    out_specs, out_shape = [], []
    for out in outs:
        if isinstance(out, FarOut):
            out_specs.append(pl.BlockSpec(memory_space=pltpu.HBM))
            out_shape.append(pltpu.HBM(out.out.shape, out.out.dtype))
        else:
            out_specs.append(whole(out.shape))
            out_shape.append(out)
    far_in = [p for p, array in enumerate(flat) if isinstance(array, Far)]
    far_out = [p for p, out in enumerate(outs) if isinstance(out, FarOut)]
    buffers = [flat[p].buffer() for p in far_in]
    buffers += [pltpu.VMEM(outs[p].out.shape, outs[p].out.dtype) for p in far_out]
    moves = len(buffers)
    semaphore_count = len(far_in) + sum(len(outs[p].parts) for p in far_out)
    prefetched = tuple(scalars) if choose is None else tuple(scalars) + (choose,)

    def regrouped(*refs):
        first = len(prefetched)
        last = first + len(operands)
        end = last + len(outs)
        near, results = refs[first : first + read], list(refs[last:end])
        kept = refs[end : end + moves]
        semaphores = refs[end + moves] if moves else None
        rest = refs[end + moves + 1 :] if moves else refs[end:]
        ins = [near[place] for place in places]
        for k, p in enumerate(far_in):
            far = flat[p]
            sources = [
                far.source(near[places[p] + j], refs[:first]) for j in range(len(far.arrays()))
            ]
            ins[p] = FarRef(sources, kept[k], semaphores.at[k], refs[first - 1])
        used = len(far_in)
        for k, p in enumerate(far_out):
            parts = outs[p].parts
            own = [semaphores.at[used + n] for n in range(len(parts))]
            used += len(parts)
            results[p] = FarOutRef(kept[len(far_in) + k], results[p], own, parts)
        kernel(*refs[: len(scalars)], *jax.tree.unflatten(tree, ins), *results, *rest)
        for p in far_in:
            ins[p].wait()
        for p in far_out:
            results[p].finish()

    return pl.pallas_call(
        regrouped,
        grid_spec=pltpu.PrefetchScalarGridSpec(
            num_scalar_prefetch=len(prefetched),
            grid=(1,),
            in_specs=in_specs,
            out_specs=out_specs,
            scratch_shapes=buffers
            + ([pltpu.SemaphoreType.DMA((semaphore_count,))] if moves else [])
            + list(scratch),
        ),
        out_shape=out_shape,
        compiler_params=pltpu.CompilerParams(vmem_limit_bytes=VMEM_BYTES),
        cost_estimate=pl.CostEstimate(flops=cost, bytes_accessed=cost, transcendentals=0),
    )(*prefetched, *operands)


ALL = ("z", "y", "x", "c")


def exchange(value, partner, whole_route=False):
    count = lax.axis_size(ALL)
    route = [(i, partner(i)) for i in range(count) if whole_route or partner(i) != i]
    return lax.ppermute(value, ALL, route)


def by_mask(value, mask):
    return exchange(value, lambda i: i ^ mask)


def bit_count(n):
    count = n.bit_length() - 1
    assert n == 1 << count
    return count


def swap_bits(i, first, second):
    if (i >> first & 1) != (i >> second & 1):
        i ^= (1 << first) | (1 << second)
    return i


def finish(kernel, info, pieces, outs, scratch, into=(), deps=()):
    far = [pl.BlockSpec(memory_space=pltpu.HBM)]
    first = 1 + len(pieces) + len(deps)
    return pl.pallas_call(
        kernel,
        grid_spec=pltpu.PrefetchScalarGridSpec(
            num_scalar_prefetch=1,
            grid=(1,),
            in_specs=[whole(piece.shape) for piece in pieces]
            + [pl.BlockSpec(memory_space=pl.ANY)] * len(deps)
            + far * len(into),
            out_specs=far * len(outs) + [whole((8, 128))],
            scratch_shapes=scratch,
        ),
        out_shape=[pltpu.HBM(out.shape, out.dtype) for out in outs] + [shape((8, 128))],
        input_output_aliases={first + k: k for k in range(len(into))},
        compiler_params=pltpu.CompilerParams(vmem_limit_bytes=VMEM_BYTES),
    )(info, *pieces, *deps, *(pltpu.with_memory_space_constraint(a, pltpu.HBM) for a in into))


def body(
    frames,
    cut_mask,
    offsets,
    stem_kernel,
    diff_kernel,
    stem_gain,
    stem_bias,
    reduce_weight,
    reduce_gain,
    reduce_bias,
    squeeze_weight,
    fine_kernel,
    coarse_kernel,
    excite_weight,
    middle_kernel,
    expand_weight,
    expand_gain,
    expand_bias,
    cotangent,
):
    depth = lax.axis_size("z")
    groups = 2 * depth
    assert frames.shape[0] == MICRO
    bits = bit_count(depth) + 3
    index = lax.axis_index(ALL)
    stem_total = float(4096 * groups)
    row_total = float(128 * groups)
    clip = lax.rem(index, 4).astype(jnp.int32)
    place = clip.reshape(1)
    bit_list = [lax.rem(lax.div(index, 1 << b), 2) for b in range(bits)]
    stays = jnp.where(bit_list[0] == bit_list[2], 1, 0)
    info = jnp.stack(bit_list + [stays]).astype(jnp.int32)
    plane = [(1, 2), (2, 1)]
    plane_mask = 6
    fine_flat = fine_kernel.reshape(288, 32)
    coarse_flat = coarse_kernel.reshape(288, 32)
    gain_s = jnp.tile(stem_gain, 8)[None]
    bias_s = jnp.tile(stem_bias, 8)[None]
    gain_r = reduce_gain[None]
    bias_r = reduce_bias[None]
    gain_x = expand_gain[None]
    bias_x = expand_bias[None]

    def swapped(value, whole_route=False):
        return exchange(value, lambda i: swap_bits(i, 0, 2), whole_route)

    def along(value, choice):
        return exchange(value, lambda i: i ^ (1 << choice[i & 1]))

    def pooled_sum(value):
        return depth_pieces(value + by_mask(value, 1))

    def depth_pieces(value):
        if depth > 4:
            return (lax.psum(value, "z"),)
        return (value,) + tuple(by_mask(value, m << 3) for m in reversed(range(1, depth)))

    def sums_shape(width):
        return shape((2, width))

    def to_plane(pieces):
        own, first, second, both = pieces
        return own, along(first, plane[0]), along(second, plane[1]), by_mask(both, plane_mask)

    def padded(rows):
        unit = 16 * depth
        return -(-rows // unit) * unit

    def far(*arrays):
        return tuple(Far(array) for array in arrays)

    def stack(*pieces, deps=()):
        rows = sum(piece.shape[0] for piece in pieces)
        return run(stack_rows, [shape((rows, pieces[0].shape[1]), BF)], pieces, deps=deps)[0]

    def add(first, second, deps=()):
        return run(add_floats, [shape(first.shape)], (first, second), deps=deps)[0]

    def halves(kernel, rows, arrays, deps=()):
        return run(
            kernel, [shape((rows // 2, 128), BF)] * 2, arrays, (info,),
            [pltpu.VMEM((rows, 128), BF)], deps=deps,
        )

    (pack,) = run(
        pack_clip,
        [shape((208, 64), BF)],
        (*far(cut_mask, offsets[None]), Far(frames, clip=True)),
        (place,),
    )
    pack = (pack, swapped(pack))

    def far_pack():
        return Far(pack[0], other=pack[1])

    stem_scratch = [
        pltpu.VMEM((512, 896), BF),
        pltpu.VMEM((256, 384), BF),
        pltpu.VMEM((896, 512), BF),
        pltpu.VMEM((384, 512), BF),
        pltpu.VMEM((192, 128), F32),
        pltpu.VMEM((512, 384), F32),
    ]
    stem_weights = far(stem_kernel.T, diff_kernel)
    v, stem_sums = run(
        stem_front,
        [shape((512, 512)), sums_shape(512)],
        (pack, *stem_weights),
        (info,),
        stem_scratch,
    )
    stem_sums = pooled_sum(stem_sums)
    (cot,) = run(
        lambda place, *refs: copy_rows(*refs),
        [FarOut(shape(cotangent.shape[1:], BF))],
        (Far(cotangent, clip=True),),
        (place,),
        deps=(stem_sums[0],),
    )
    cot_got = swapped(cot)
    stem_norm = far(gain_s, bias_s)
    wide, wide_keep, send, red, red_sums, stem_saved = run(
        functools.partial(stem_close, stem_total),
        [
            FarOut(shape((128, 2048), BF)),
            shape((128, 1024), BF),
            shape((128, 1024), BF),
            shape((128, 512)),
            sums_shape(512),
            FarOut(shape((520, 512))),
        ],
        (v, stem_sums, *stem_norm, Far(reduce_weight)),
        (info,),
    )
    wide_pair = by_mask(send, 1)
    red_sums = pooled_sum(red_sums)
    wide_chip = stack(wide_keep, wide_pair, deps=(red_sums[0], cot_got))
    wide_got = along(wide_chip, plane[0])
    gate_weights = far(squeeze_weight.T, fine_flat, coarse_flat, excite_weight, middle_kernel)
    both_keep, send, expanded, exp_sums, saved = run(
        functools.partial(gate_front, row_total),
        [
            shape((128, 512), BF),
            shape((128, 512), BF),
            shape((128, 2048)),
            sums_shape(2048),
            FarOut(shape((264, 512)), [(0, 136), (136, 128)]),
        ],
        (
            red, red_sums, far_pack(), *far(gain_r, bias_r), *gate_weights, Far(expand_weight),
        ),
        (info,),
        [pltpu.VMEM((128, 1024), BF)],
        choose=info,
        deps=(wide_chip,),
    )
    both_pair = by_mask(send, 1)
    exp_sums = pooled_sum(exp_sums)
    both_chip = stack(both_keep, both_pair, deps=(exp_sums[0],))
    both_got = along(both_chip, plane[0])
    wide_near = stack(wide_chip, wide_got, deps=(both_chip,))
    wide_far = along(wide_near, plane[1])
    og_sums, out_saved = run(
        functools.partial(out_back, row_total),
        [
            sums_shape(2048),
            FarOut(shape((264, 2048)), [(0, 64), (128, 64), (64, 64), (192, 72)]),
        ],
        (expanded, exp_sums, *far(gain_x, bias_x, wide), Far(cot, other=cot_got)),
        choose=info,
        deps=(wide_near,),
    )
    og_sums = pooled_sum(og_sums)
    both_near = stack(both_chip, both_got, deps=(og_sums[0],))
    both_far = along(both_near, plane[1])
    hg, og_total, *blocks = run(
        functools.partial(expand_back, row_total),
        [shape((128, 512), BF), FarOut(shape((8, 2048)))] + [shape((128, 640), BF)] * 4,
        (og_sums, Far(out_saved), Far(saved, 136, 128), *far(gain_x, expand_weight)),
        (info,),
        [pltpu.VMEM((128, 512), BF), pltpu.VMEM((128, 2048), BF)],
        deps=(both_near,),
    )
    blocks = to_plane(blocks)
    rg, rg_sums, small = run(
        gate_back,
        [shape((128, 512)), sums_shape(512), shape((256, 256))],
        (far_pack(), hg, Far(saved, 0, 128), *far(gain_r, bias_r), *gate_weights),
        choose=info,
        deps=(wide_far, both_far),
    )
    rg_sums = pooled_sum(rg_sums)
    blocks = stack(*blocks, deps=(rg_sums[0],))
    blocks_pair = by_mask(blocks, 1)

    middle_rows = padded(2304)
    outer_rows = padded(2176)
    depth_bits = list(range(3, bits))
    have = {}
    held = [tuple(rg_sums[1:])]

    def waits():
        deps, held[0] = held[0], ()
        return deps

    def paired(value, rows):
        return value.reshape(2, rows, 128), by_mask(value, 1).reshape(2, rows, 128)

    def halve(name):
        deps = waits()
        for bit in depth_bits[1:]:
            keep, got = have[name]
            keep, send = halves(
                functools.partial(add_halves, bit), keep.shape[0], (keep, got), deps
            )
            have[name] = keep, by_mask(send, 1 << bit)
            deps = ()
        return keep

    def sum_up(name):
        keep, got = have[name]
        (value,) = run(add_rows, [shape(keep.shape, BF)], (keep, got), deps=waits())
        have[name] = value, by_mask(value, 1 << depth_bits[-1])
        return value

    def join(name, depth_range):
        deps = waits()
        for bit in depth_range:
            value, got = have[name]
            rows, width = value.shape
            (value,) = run(
                functools.partial(join_halves, bit),
                [shape((2 * rows, width), BF)],
                (value, got),
                (info,),
                deps=deps,
            )
            if bit > 3:
                have[name] = value, by_mask(value, 1 << (bit - 1))
            deps = ()
        if depth_range[-1] == 3:
            have[name] = value, along(value, plane[1])
        return value

    def near(name, rows):
        value = stack(*have[name], deps=waits())
        have[name + " far"] = along(value, plane[0])
        have[name + " near"] = paired(value, rows)
        return value

    def middle_kernel_sum():
        keep, send = halves(
            middle_weights, middle_rows, ((both_near, both_far), (blocks, blocks_pair)), waits()
        )
        have["middle"] = keep, by_mask(send, 8)
        return keep

    def reduction_back():
        rs, rs_sums, rg_total, *late = run(
            functools.partial(reduce_back, row_total),
            [shape((512, 512)), sums_shape(512), FarOut(shape((8, 512)))]
            + [shape((128, 256), BF)] * 4,
            (
                small, rg, rg_sums, Far(saved, 0, 136), Far(gain_r), Far(out_saved, 0, 128),
                *far(reduce_weight, stem_saved), *stem_norm,
            ),
            (info,),
            [pltpu.VMEM((128, 512), BF)],
            deps=waits(),
        )
        have["rs"] = rs, rs_sums, rg_total
        have["late"] = to_plane(late)
        return rs

    def stem_sum():
        rs_sums = have["rs"][1]
        have["rs here"] = add(rs_sums, by_mask(rs_sums, 1), waits())
        return have["rs here"]

    def late_rows():
        have["late"] = stack(*have["late"], deps=waits())
        have["late pair"] = by_mask(have["late"], 1)
        return have["late"]

    def outer_kernel_sum():
        keep, send = halves(
            outer_weights,
            outer_rows,
            (
                (both_near, both_far), (blocks, blocks_pair), (wide_near, wide_far),
                (have["late"], have["late pair"]),
            ),
            waits(),
        )
        have["outer"] = keep, by_mask(send, 8)
        return keep

    def stem_pieces():
        have["rs pieces"] = depth_pieces(have["rs here"])
        return held[0] + have["rs pieces"]

    def stem_gradient():
        rs, _, rg_total = have["rs"]
        have["frame"], have["tail"] = run(
            functools.partial(stem_back, stem_total, 1.0 / groups),
            [shape((8, 3, 8, 64)), shape((200, 128))],
            (
                far_pack(), *stem_weights, Far(stem_saved), stem_norm[0], rs, have["rs pieces"],
                Far(og_total), Far(rg_total),
            ),
            scratch=stem_scratch,
            choose=info,
            deps=waits(),
        )
        return have["tail"]

    def tail_add(bits_here):
        deps = waits()
        for bit in bits_here:
            have["tail"] = add(have["tail"], by_mask(have["tail"], 1 << bit), deps)
            deps = ()
        return have["tail"]

    def middle_far_rows():
        value = stack(have["middle far"], deps=waits())
        have["middle far"] = paired(value, middle_rows)
        return value

    outer_scratch = [
        pltpu.VMEM((4, 256, 512), F32),
        pltpu.VMEM((4, 1024, 128), F32),
        pltpu.SemaphoreType.DMA((4,)),
        pltpu.SemaphoreType.DMA((4,)),
    ]

    def middle_finish():
        one, two = have["middle near"], have["middle far"]
        have["dmiddle"], token = finish(
            finish_middle,
            info,
            (one[0], two[0], one[1], two[1]),
            [shape((9, 512, 512))],
            [pltpu.VMEM((8, 9, 256, 128), F32), pltpu.SemaphoreType.DMA((8,))],
            deps=waits(),
        )
        return token

    def outer_finish():
        dexpand, dreduce, token = finish(
            functools.partial(finish_outer, False),
            info,
            have["outer near"],
            [shape((512, 2048)), shape((2048, 512))],
            outer_scratch,
            deps=waits(),
        )
        have["outer out"] = dexpand, dreduce
        return token

    steps = {
        "K": middle_kernel_sum,
        "R": reduction_back,
        "Ma": lambda: halve("middle"),
        "Mb": lambda: sum_up("middle"),
        "Mc": lambda: join("middle", depth_bits[:0:-1]),
        "Md": lambda: join("middle", depth_bits[:1]),
        "Mn": lambda: near("middle", middle_rows),
        "Mf": middle_far_rows,
        "Rs": stem_sum,
        "St": late_rows,
        "O": outer_kernel_sum,
        "Oa": lambda: halve("outer"),
        "Ob": lambda: sum_up("outer"),
        "Oc": lambda: join("outer", depth_bits[:0:-1]),
        "Od": lambda: join("outer", depth_bits[:1]),
        "On": lambda: near("outer", outer_rows),
        "Z": stem_pieces,
        "B": stem_gradient,
        "T0": lambda: tail_add([0]),
        "T3": lambda: tail_add(depth_bits[:-1]),
        "T4": lambda: tail_add(depth_bits[-1:]),
        "F": middle_finish,
        "G": outer_finish,
    }
    for name in ORDER:
        result = steps[name]()
        held[0] = result if isinstance(result, tuple) else (result,)
    frame_grad, tail = have["frame"], have["tail"]
    dmiddle = have["dmiddle"]
    dexpand, dreduce = have["outer out"]
    outer_near = have["outer near"]
    token = held[0][0]
    outer_far = have["outer far"]
    frame_grad = swapped(frame_grad, True)
    outer_far = stack(outer_far, deps=(token,))
    outer_far = paired(outer_far, outer_rows)
    tail = (tail,) + tuple(by_mask(tail, mask) for mask in (2, 4, 6))
    dexpand, dreduce, token = finish(
        functools.partial(finish_outer, True),
        info,
        outer_far,
        [shape((512, 2048)), shape((2048, 512))],
        outer_scratch,
        (dexpand, dreduce),
    )
    outer = (outer_near[0], outer_far[0], outer_near[1], outer_far[1])
    small_shapes = ((1, 8, 3, 8, 64), (32, 512), (32, 512), (9, 32, 32), (9, 32, 32), (64, 147))
    small_shapes += ((9, 6, 64),) + tuple((1, n) for n in (64, 64, 512, 512, 2048, 2048))
    (
        frame_grad, dsqueeze, dexcite, dfine, dcoarse, dstem, ddiff, gain_s, bias_s, gain_r,
        bias_r, gain_x, bias_x,
    ) = pl.pallas_call(
        finish_rest,
        grid_spec=pltpu.PrefetchScalarGridSpec(
            num_scalar_prefetch=1,
            grid=(1,),
            in_specs=[pl.BlockSpec((2, 128, 128), lambda i, info: (0, 16, 0))] * 4
            + [whole((200, 128))] * 4
            + [whole((8, 3, 8, 64)), pl.BlockSpec(memory_space=pl.ANY)],
            out_specs=[whole(d) for d in small_shapes],
            scratch_shapes=[pltpu.VMEM((256, 256), F32), pltpu.VMEM((200, 128), F32)],
        ),
        out_shape=[shape(d) for d in small_shapes],
        compiler_params=pltpu.CompilerParams(vmem_limit_bytes=FINISH_BYTES),
    )(info, *outer, *tail, frame_grad, token)
    return (
        frame_grad,
        dstem.T,
        ddiff,
        gain_s[0],
        bias_s[0],
        dreduce,
        gain_r[0],
        bias_r[0],
        dsqueeze.T,
        dfine,
        dcoarse,
        dexcite,
        dmiddle,
        dexpand,
        gain_x[0],
        bias_x[0],
    )


def solution(mesh):
    split = jax.sharding.Mesh(mesh.devices.reshape(-1, 2, 2, 2), ALL)
    copied = P()
    by_group = P(("z", "y"))
    in_specs = (by_group,) * 3 + (copied,) * 15 + (by_group,)
    out_specs = (P(ALL),) + (copied,) * 15
    return jax.shard_map(body, mesh=split, in_specs=in_specs, out_specs=out_specs, check_vma=False)
```

```python
import functools

import jax
import jax.numpy as jnp
from jax import lax
from jax.experimental import pallas as pl
from jax.experimental.pallas import tpu as pltpu
from jax.sharding import PartitionSpec as P

FRAMES = 8
MICRO = 4
EPSILON = 1e-05
COST = 1_000_000
ORDER = (
    ("K", "R", "Ma", "St", "Rs", "Mb", "O", "Mc", "Oa", "Z", "Md", "B", "Ob", "Mn", "Oc", "Od")
    + ("T0", "Mf", "T3", "On", "F", "T4", "G")
)
FINISH_BYTES = 16 * 1024 * 1024
VMEM_BYTES = 32 * 1024 * 1024
BF = jnp.bfloat16
F32 = jnp.float32

STEM = 64
SLOT = 16


def dot(left, right):
    return jnp.dot(left, right, preferred_element_type=F32)


def dot_nt(left, right):
    return lax.dot_general(left, right, (((1,), (1,)), ((), ())), preferred_element_type=F32)


def dot_tn(left, right):
    return lax.dot_general(left, right, (((0,), (0,)), ((), ())), preferred_element_type=F32)


def dot_exact(left, right):
    return jnp.dot(left, right, preferred_element_type=F32, precision=lax.Precision.HIGHEST)


def iota(shape, dim):
    return lax.broadcasted_iota(jnp.int32, shape, dim)


def sigmoid(v):
    return 1.0 / (1.0 + jnp.exp(-v))


def swish_slope(v):
    s = sigmoid(v)
    return s * (1.0 + v * (1.0 - s))


def keep_column(pack, lanes):
    rows = pack[192:208, :].astype(F32)
    return jnp.concatenate(
        [jnp.broadcast_to(rows[f : f + 1, :lanes], (8, lanes)) for f in range(FRAMES)], 0
    )


def gate_column(pack):
    keep = keep_column(pack, 64)
    both = jnp.concatenate([keep, keep], 1)
    return jnp.concatenate([jnp.zeros((8, 128), F32), both[:-8]], 0)


def pack_clip(place, cut, offset, frames, out):
    clip = place[0]
    row = cut[pl.ds(clip, 1), :]
    own = iota((1, MICRO), 1) == clip
    stop = jnp.sum(jnp.where(own, offset[...], 0), 1, keepdims=True)
    step = iota(row.shape, 1)
    valid = jnp.where(step + 1 == stop, 0, row).astype(F32)
    spread = iota((16, FRAMES - 1), 0) == iota((16, FRAMES - 1), 1)
    column = jnp.sum(jnp.where(spread, valid, 0.0), 1, keepdims=True)
    out[0:192, :] = frames[...].astype(F32).reshape(192, 64).astype(BF)
    out[192:208, :] = jnp.broadcast_to(column, (16, 64)).astype(BF)


def summed_up(pieces):
    value = pieces[0][...]
    for piece in pieces[1:]:
        value = value + piece[...]
    return value


def spread_sums(out, first, second):
    out[...] = jnp.concatenate([first, second], 0)


def norm_scale(sums, row_total):
    mean = sums[0:1] * (1.0 / row_total)
    variance = sums[1:2] * (1.0 / row_total) - mean * mean
    return mean, lax.rsqrt(variance + EPSILON)


def column_sums(out, first, second):
    spread_sums(out, jnp.sum(first, 0, keepdims=True), jnp.sum(second, 0, keepdims=True))


def fold_lanes(sums):
    for step in (64, 128, 256):
        sums = sums + pltpu.roll(sums, step, 1)
    return sums


def shift_rows(v, dy, dx):
    rows = v.shape[0]
    if dx:
        rolled = pltpu.roll(v, (-dx) % rows, 0)
        wb = lax.rem(iota(v.shape, 0), 8)
        v = jnp.where((wb + dx >= 0) & (wb + dx < 8), rolled, 0.0)
    half = rows // 2
    if dy == 1:
        v = jnp.concatenate([v[half:], jnp.zeros_like(v[half:])], 0)
    elif dy == -1:
        v = jnp.concatenate([jnp.zeros_like(v[:half]), v[:half]], 0)
    return v


def cell_sum(v):
    half = v.shape[0] // 2
    both = v[:half] + v[half:]
    even = lax.rem(iota(both.shape, 0), 2) == 0
    both = both + jnp.where(even, pltpu.roll(both, half - 1, 0), pltpu.roll(both, 1, 0))
    return jnp.concatenate([both, both], 0)


def taps(v):
    return [shift_rows(v, ky - 1, kx - 1) for ky in range(3) for kx in range(3)]


def back_taps(v):
    return [shift_rows(v, 1 - ky, 1 - kx) for ky in range(3) for kx in range(3)]


def coarse_taps(v):
    return [shift_rows(v, 0, 2 * (k - 1)) for k in range(3)]


def window_select(rows, cols, kind):
    place = iota((rows, cols), 0)
    col = iota((rows, cols), 1)
    lane = lax.rem(place, 128)
    tap_row = lax.div(place, 128)
    channel = lax.div(lane, SLOT)
    slot = lax.rem(lane, SLOT)
    if kind == "stem":
        hit = (col == (7 * tap_row + slot) * 3 + channel) & (slot < 7) & (channel < 3)
        return jnp.where(hit, 1.0, 0.0)
    cell = lax.div(slot - 1, 2)
    hit = (col == (3 * tap_row + cell) * 6 + channel) & (slot >= 1) & (slot < 7) & (channel < 6)
    return jnp.where(hit, 0.25, 0.0)


def spread_select():
    w = iota((64, 128), 0)
    lane = iota((64, 128), 1)
    return jnp.where(w == 8 * lax.div(lane, SLOT) + lax.rem(lane, SLOT) - 3, 1.0, 0.0)


def gather_select():
    row = iota((384, 128), 0)
    col = iota((384, 128), 1)
    return jnp.where(col == lax.div(row, 128) * SLOT + lax.rem(row, SLOT), 1.0, 0.0)


def own_block():
    row = iota((8, 128), 0)
    lane = iota((8, 128), 1)
    return jnp.where(lax.div(lane, SLOT) == row, 1.0, 0.0)


def stem_windows(pack, kernel, diff, win, win2, u, u2, spread, tiles):
    spread[...] = dot(pack[0:192, :], spread_select().astype(BF))
    mask = own_block()
    for f in range(8):
        for c in range(3):
            for h in range(8):
                line = f * 24 + c * 8 + h
                tiles[h * 64 + f * 8 : h * 64 + f * 8 + 8, c * 128 : c * 128 + 128] = (
                    jnp.broadcast_to(spread[line : line + 1, :], (8, 128)) * mask
                )
    pixels = dot(tiles[...].astype(BF), gather_select().astype(BF))
    rows = [pixels[64 * h : 64 * h + 64] for h in range(8)]
    gate = gate_column(pack)
    steps = []
    for h2 in range(4):
        both = rows[2 * h2] + rows[2 * h2 + 1]
        step = (both - jnp.concatenate([jnp.zeros((8, 128), F32), both[:-8]], 0)) * gate
        later = jnp.concatenate([step[8:], jnp.zeros((8, 128), F32)], 0)
        steps.append((step + pltpu.roll(later, 48, 1)).astype(BF))
    rows = [r.astype(BF) for r in rows]
    blank = jnp.zeros((64, 128), BF)
    for dy in range(7):
        for h in range(8):
            source = h + dy - 3
            win[64 * h : 64 * h + 64, 128 * dy : 128 * dy + 128] = (
                rows[source] if 0 <= source < 8 else blank
            )
    for dy in range(3):
        for h in range(4):
            source = h + dy - 1
            win2[64 * h : 64 * h + 64, 128 * dy : 128 * dy + 128] = (
                steps[source] if 0 <= source < 4 else blank
            )
    low_half = iota((896, 128), 1) < 64
    wide_kernel = jnp.concatenate([kernel[...], kernel[...]], 0)
    placed = dot_nt(window_select(896, 147, "stem").astype(BF), wide_kernel)
    taps = diff[...].astype(F32)
    rows = jnp.concatenate([taps[k] for k in range(9)], 0)
    wide_diff = jnp.concatenate([rows, rows], 1).astype(BF)
    placed2 = dot(window_select(384, 54, "diff").astype(BF), wide_diff)
    for q in range(4):
        first = pltpu.roll(placed, 2 * q, 0) if q else placed
        second = pltpu.roll(placed, 2 * q + 1, 0)
        u[:, 128 * q : 128 * q + 128] = jnp.where(low_half, first, second).astype(BF)
        u2[:, 128 * q : 128 * q + 128] = (
            pltpu.roll(placed2, 2 * q, 0) if q else placed2
        ).astype(BF)


class Pick:
    def __init__(self, info, own, other):
        self.stays = info[info.shape[0] - 1] == 1
        self.own, self.other = own, other

    def __getitem__(self, place):
        return jnp.where(self.stays, self.own[place], self.other[place])


def stem_front(
    info, pack, kernel, diff, v_out, sums_out, win, win2, u, u2, spread, tiles
):
    stem_windows(Pick(info, *pack), kernel, diff, win, win2, u, u2, spread, tiles)
    v = dot(win[...], u[...])
    side = dot(win2[...], u2[...])
    first = jnp.zeros((1, 512), F32)
    second = jnp.zeros((1, 512), F32)
    for h in range(8):
        piece = v[64 * h : 64 * h + 64] + side[64 * (h // 2) : 64 * (h // 2) + 64]
        v_out[64 * h : 64 * h + 64, :] = piece
        first = first + jnp.sum(piece, 0, keepdims=True)
        second = second + jnp.sum(piece * piece, 0, keepdims=True)
    spread_sums(sums_out, first, second)


def stem_close(
    row_total, info, v, sums, gain, bias, weight, wide_out, keep_out, send_out, red_out, sums_out,
    save,
):
    mean, scale = norm_scale(fold_lanes(summed_up(sums)), row_total)
    save[512:513, :] = scale
    for h in range(8):
        normal = (v[64 * h : 64 * h + 64, :] - mean) * scale
        save[64 * h : 64 * h + 64, :] = normal
        y = normal * gain[...] + bias[...]
        wide_out[
            64 * (h // 4) : 64 * (h // 4) + 64, 512 * (h % 4) : 512 * (h % 4) + 512
        ] = (y * sigmoid(y)).astype(BF)
    save.flush()
    wide_out.flush()
    keep_out[...] = wide_out[:, lanes(1024 * info[0], 1024)]
    send_out[...] = wide_out[:, lanes(1024 * (1 - info[0]), 1024)]
    red = dot(wide_out[...], weight[...])
    red_out[...] = red
    column_sums(sums_out, red, red * red)


def gate_path(pack, narrow, squeeze, fine, coarse, excite):
    squeezed = dot_nt(narrow.astype(BF), squeeze[...])
    keep = keep_column(pack, 32)
    parts = []
    for hb in range(2):
        part = squeezed[64 * hb : 64 * hb + 64]
        later = jnp.concatenate([part[8:], part[:8]], 0)
        parts.append((later - part) * keep)
    change = jnp.concatenate(parts, 0)
    fine_rows = jnp.concatenate(taps(change), 1).astype(BF)
    pooled = 0.25 * cell_sum(change)
    coarse_rows = jnp.concatenate(coarse_taps(pooled), 1).astype(BF)
    summed = (dot(fine_rows, fine[...]) + dot(coarse_rows, coarse[96:192, :])).astype(BF)
    return fine_rows, coarse_rows, summed, sigmoid(dot(summed, excite[...]))


def gate_front(
    row_total, info, red, sums, pack, gain, bias, squeeze, fine, coarse, excite, middle, expand,
    keep_out, send_out, exp_out, sums_out, save, both,
):
    mean, scale = norm_scale(summed_up(sums), row_total)
    normal = (red[...] - mean) * scale
    save[0:128, :] = normal
    save[128:129, :] = scale
    save.flush()
    y = normal * gain[...] + bias[...]
    narrow = y * sigmoid(y)
    gate = gate_path(pack, narrow, squeeze, fine, coarse, excite)[3]
    gated = narrow * (1.0 + gate)
    total = jnp.zeros((128, 512), F32)
    for k, piece in enumerate(taps(gated)):
        total = total + dot(piece.astype(BF), middle[k])
    save[136:264, :] = total
    save.flush()
    hidden = (total * sigmoid(total)).astype(BF)
    for half in range(2):
        part = slice(256 * half, 256 * half + 256)
        both[:, 512 * half : 512 * half + 256] = gated[:, part].astype(BF)
        both[:, 512 * half + 256 : 512 * half + 512] = hidden[:, part]
    keep_out[...] = both[:, lanes(512 * info[0], 512)]
    send_out[...] = both[:, lanes(512 * (1 - info[0]), 512)]
    expanded = dot(hidden, expand[...])
    exp_out[...] = expanded
    column_sums(sums_out, expanded, expanded * expanded)


def out_back(row_total, expanded, sums, gain, bias, wide, cot, sums_out, save):
    mean, scale = norm_scale(summed_up(sums), row_total)
    save[256:257, :] = scale
    first = jnp.zeros((1, 2048), F32)
    second = jnp.zeros((1, 2048), F32)
    for hb in range(2):
        part = slice(64 * hb, 64 * hb + 64)
        if hb:
            save.flush()
            save.flush()
        normal = (expanded[part, :] - mean) * scale
        y = normal * gain[...] + bias[...] + wide[part, :].astype(F32)
        weightless = cot[:, hb, :, :].astype(F32).reshape(64, 2048)
        og = weightless * swish_slope(y)
        save[part, :] = og
        save[128 + 64 * hb : 192 + 64 * hb, :] = normal
        first = first + jnp.sum(og, 0, keepdims=True)
        second = second + jnp.sum(og * normal, 0, keepdims=True)
    spread_sums(sums_out, first, second)


def norm_pull(grad, normal, scale, gain, grad_sums, row_total):
    return (
        gain
        * scale
        * (
            grad
            - grad_sums[0:1] * (1.0 / row_total)
            - normal * (grad_sums[1:2] * (1.0 / row_total))
        )
    )


def block_order(info, partner=False):
    block = 2 * info[1] + info[2]
    first = jnp.where((info[0] == 0) != partner, 2, 1)
    return [block, block ^ first, block ^ (3 - first), block ^ 3]


def lanes(start, width):
    return pl.ds(pl.multiple_of(start, 128), width)


def expand_back(
    row_total, info, grad_sums, saved, hpre, gain, expand, hg_out, total_out, *rest
):
    outs, (hg_scratch, dv_scratch) = rest[:4], rest[4:]
    sums = summed_up(grad_sums)
    total_out[0:2, :] = sums
    total_out.flush()
    dv = norm_pull(
        saved[0:128, :], saved[128:256, :], saved[256:257, :], gain[...], sums, row_total
    ).astype(BF)
    dv_scratch[...] = dv
    dhid = dot_nt(dv, expand[...]).astype(BF).astype(F32)
    hg = (dhid * swish_slope(hpre[...])).astype(BF)
    hg_out[...] = hg
    hg_scratch[...] = hg
    for out, block in zip(outs, block_order(info)):
        out[:, :128] = hg_scratch[:, lanes(128 * block, 128)]
        out[:, 128:] = dv_scratch[:, lanes(512 * block, 512)]


def all_rows(refs):
    return jnp.concatenate([ref[...] for ref in refs], 0)


def clip_rows(mine, pair, columns):
    rows = []
    for k, other in enumerate((0, 2, 1, 3)):
        rows.append(mine[128 * k : 128 * k + 128, columns])
        rows.append(pair[128 * other : 128 * other + 128, columns])
    return rows


def depth_halves(info, bit, scratch, keep_out, send_out):
    rows = keep_out.shape[0]
    mine = info[bit]
    keep_out[...] = scratch[pl.ds(pl.multiple_of(mine * rows, 16), rows), :]
    send_out[...] = scratch[pl.ds(pl.multiple_of((1 - mine) * rows, 16), rows), :]


def add_halves(bit, info, keep, got, keep_out, send_out, scratch):
    scratch[...] = (keep[...].astype(F32) + got[...].astype(F32)).astype(BF)
    depth_halves(info, bit, scratch, keep_out, send_out)


def add_rows(keep, got, out):
    out[...] = (keep[...].astype(F32) + got[...].astype(F32)).astype(BF)


def join_halves(bit, info, own, got, out):
    rows = own.shape[0]
    mine = info[bit]
    out[pl.ds(pl.multiple_of(mine * rows, 16), rows), :] = own[...]
    out[pl.ds(pl.multiple_of((1 - mine) * rows, 16), rows), :] = got[...]


def middle_weights(info, left_refs, right_refs, *rest):
    outs, (scratch,) = rest[:-1], rest[-1:]
    left = jnp.concatenate([ref[:, :256] for ref in left_refs], 0).T
    clips = [
        back_taps(rows.astype(F32)) for rows in clip_rows(*right_refs, slice(0, 128))
    ]
    for k in range(9):
        right = jnp.concatenate([clip[k] for clip in clips], 0).astype(BF)
        scratch[256 * k : 256 * k + 256, :] = dot(left, right).astype(BF)
    if scratch.shape[0] > 2304:
        scratch[2304:, :] = jnp.zeros((scratch.shape[0] - 2304, 128), BF)
    depth_halves(info, 3, scratch, *outs)


def outer_weights(info, left_refs, right_refs, wide, late, *rest):
    outs, (scratch,) = rest[:-1], rest[-1:]
    left = jnp.concatenate([ref[:, 256:] for ref in left_refs], 0)
    right = jnp.concatenate(clip_rows(*right_refs, slice(128, 640)), 0)
    result = dot_tn(left, right).astype(BF)
    for q in range(4):
        scratch[256 * q : 256 * q + 256, :] = result[:, 128 * q : 128 * q + 128]
    right = jnp.concatenate(clip_rows(*late, slice(0, 128)), 0)
    scratch[1024:2048, :] = dot_tn(all_rows(wide), right).astype(BF)
    small = [late[0][128 * k : 128 * k + 128, 128:].astype(F32) for k in range(4)]
    scratch[2048:2176, :] = sum(small).astype(BF)
    if scratch.shape[0] > 2176:
        scratch[2176:, :] = jnp.zeros((scratch.shape[0] - 2176, 128), BF)
    depth_halves(info, 3, scratch, *outs)


def copy_rows(source, out):
    out[...] = source[...]


def add_floats(first, second, out):
    out[...] = first[...] + second[...]


def stack_rows(*refs):
    out = refs[-1]
    start = 0
    for ref in refs[:-1]:
        out[start : start + ref.shape[0], :] = ref[...]
        start += ref.shape[0]


def gate_back(
    pack, hg, normal, gain, bias, squeeze, fine, coarse, excite, middle,
    rg_out, sums_out, small_out,
):
    y = normal[...] * gain[...] + bias[...]
    narrow_v = y * sigmoid(y)
    fine_rows, coarse_rows, summed, gate_v = gate_path(
        pack, narrow_v, squeeze, fine, coarse, excite
    )
    total = jnp.zeros((128, 512), F32)
    for k, piece in enumerate(back_taps(hg[...].astype(F32))):
        total = total + dot_nt(piece.astype(BF), middle[k])
    gg = total.astype(BF).astype(F32)
    narrow_grad = gg * (1.0 + gate_v)
    excite_grad = (gg * narrow_v * gate_v * (1.0 - gate_v)).astype(BF)
    dexcite = dot_tn(summed, excite_grad)
    summed_low = dot_nt(excite_grad, excite[...]).astype(BF)
    summed_grad = summed_low.astype(F32)
    coarse_low = cell_sum(summed_grad).astype(BF)
    dfine = dot_tn(fine_rows, summed_low)
    dcoarse = 0.25 * dot_tn(coarse_rows, coarse_low)
    spread = dot_nt(summed_low, fine[...])
    change_grad = jnp.zeros((128, 32), F32)
    for k in range(9):
        change_grad = change_grad + shift_rows(
            spread[:, 32 * k : 32 * k + 32], 1 - k // 3, 1 - k % 3
        )
    spread = dot_nt(coarse_low, coarse[96:192, :])
    pooled_grad = jnp.zeros((128, 32), F32)
    for k in range(3):
        pooled_grad = pooled_grad + shift_rows(spread[:, 32 * k : 32 * k + 32], 0, 2 * (1 - k))
    change_grad = change_grad + 0.25 * pooled_grad
    keep = keep_column(pack, 32)
    parts = []
    for hb in range(2):
        step = change_grad[64 * hb : 64 * hb + 64] * keep
        earlier = jnp.concatenate([step[56:], step[:56]], 0)
        parts.append(earlier - step)
    squeezed_grad = jnp.concatenate(parts, 0).astype(BF)
    dsqueeze = dot_tn(squeezed_grad, narrow_v.astype(BF))
    narrow_grad = narrow_grad + dot(squeezed_grad, squeeze[...])
    rg = narrow_grad * swish_slope(y)
    rg_out[...] = rg
    column_sums(sums_out, rg, rg * normal[...])
    small_out[0:32, :] = dsqueeze[:, :256]
    small_out[32:64, :] = dsqueeze[:, 256:]
    small_out[64:96, :] = dexcite[:, :256]
    small_out[96:128, :] = dexcite[:, 256:]
    pieces = [dfine[32 * k : 32 * k + 32] for k in range(9)]
    pieces += [dcoarse[32 * k : 32 * k + 32] for k in range(3)]
    small_out[128:160, :] = jnp.concatenate(pieces[:8], 1)
    small_out[160:192, :] = jnp.concatenate(pieces[8:] + [jnp.zeros((32, 128), F32)], 1)
    small_out[192:256, :] = jnp.zeros((64, 256), F32)


def reduce_back(
    row_total, info, small, rg, grad_sums, saved, gain, og, weight, stem_saved, stem_gain,
    stem_bias, rs_out, sums_out, total_out, dv0, dv1, dv2, dv3, dv_scratch,
):
    sums = summed_up(grad_sums)
    total_out[0:2, :] = sums
    total_out.flush()
    dv = norm_pull(
        rg[...], saved[0:128, :], saved[128:129, :], gain[...], sums, row_total
    ).astype(BF)
    dv_scratch[...] = dv
    for out, block in zip((dv0, dv1, dv2, dv3), block_order(info)):
        out[:, :128] = dv_scratch[:, lanes(128 * block, 128)]
        part = small[pl.ds(pl.multiple_of(64 * block, 64), 64), :].astype(BF)
        out[:64, 128:] = part[:, :128]
        out[64:, 128:] = part[:, 128:]
    wide_grad = dot_nt(dv, weight[...]) + og[...].astype(BF).astype(F32)
    wide_grad = wide_grad.astype(BF).astype(F32)
    first = jnp.zeros((1, 512), F32)
    second = jnp.zeros((1, 512), F32)
    for h in range(8):
        normal = stem_saved[64 * h : 64 * h + 64, :]
        y = normal * stem_gain[...] + stem_bias[...]
        rs = (
            wide_grad[64 * (h // 4) : 64 * (h // 4) + 64, 512 * (h % 4) : 512 * (h % 4) + 512]
            * swish_slope(y)
        )
        rs_out[64 * h : 64 * h + 64, :] = rs
        first = first + jnp.sum(rs, 0, keepdims=True)
        second = second + jnp.sum(rs * normal, 0, keepdims=True)
    spread_sums(sums_out, first, second)


def stem_back(
    stem_total, share, pack, kernel, diff, saved, gain, rs, grad_sums, og_total,
    rg_total, frames_out, tail_out, win, win2, u, u2, lines, tiles,
):
    stem_windows(pack, kernel, diff, win, win2, u, u2, lines, tiles)
    scale = saved[512:513, :]
    totals = fold_lanes(summed_up(grad_sums))
    rows = []
    pairs = []
    for h in range(8):
        part = slice(64 * h, 64 * h + 64)
        normal = saved[part, :]
        pre = norm_pull(rs[part, :], normal, scale, gain[...], totals, stem_total)
        rows.append(pre.astype(BF))
        if h % 2:
            pairs.append((before + pre).astype(BF))
        before = pre
    dv = jnp.concatenate(rows, 0)
    dside = jnp.concatenate(pairs, 0)

    low_half = iota((896, 128), 1) < 64
    du = dot_tn(win[...], dv)
    placed = jnp.zeros((896, 128), F32)
    for q in range(4):
        part = du[:, 128 * q : 128 * q + 128]
        first = pltpu.roll(part, 896 - 2 * q, 0) if q else part
        placed = placed + jnp.where(low_half, first, pltpu.roll(part, 896 - 2 * q - 1, 0))
    placed = placed + pltpu.roll(placed, 64, 1)
    tail_out[0:147, 0:64] = lax.dot_general(
        window_select(896, 147, "stem"), placed, (((0,), (0,)), ((), ())),
        preferred_element_type=F32, precision=lax.Precision.HIGHEST,
    )[:, :64]
    du2 = dot_tn(win2[...], dside)
    placed = jnp.zeros((384, 128), F32)
    for q in range(4):
        part = du2[:, 128 * q : 128 * q + 128]
        placed = placed + (pltpu.roll(part, 384 - 2 * q, 0) if q else part)
    placed = placed + pltpu.roll(placed, 64, 1)
    tail_out[0:54, 64:128] = lax.dot_general(
        window_select(384, 54, "diff"), placed, (((0,), (0,)), ((), ())),
        preferred_element_type=F32, precision=lax.Precision.HIGHEST,
    )[:, :64]

    dwin = dot_nt(dv, u[...])
    dwin2 = dot_nt(dside, u2[...])
    gate = gate_column(pack)
    steps = []
    for h2 in range(4):
        total = jnp.zeros((64, 128), F32)
        for dy in range(3):
            target = h2 + 1 - dy
            if 0 <= target < 4:
                total = total + dwin2[64 * target : 64 * target + 64, 128 * dy : 128 * dy + 128]
        later = pltpu.roll(total, 80, 1)
        later = jnp.concatenate([jnp.zeros((8, 128), F32), later[:-8]], 0)
        step = (total + later) * gate
        steps.append(step - jnp.concatenate([step[8:], jnp.zeros((8, 128), F32)], 0))
    pixels = []
    for h in range(8):
        total = steps[h // 2]
        for dy in range(7):
            target = h + 3 - dy
            if 0 <= target < 8:
                total = total + dwin[64 * target : 64 * target + 64, 128 * dy : 128 * dy + 128]
        pixels.append(total)
    pixels = jnp.concatenate(pixels, 0)
    back = lax.dot_general(
        pixels, gather_select(), (((1,), (1,)), ((), ())),
        preferred_element_type=F32, precision=lax.Precision.HIGHEST,
    )
    mask = own_block()
    for f in range(8):
        for c in range(3):
            for h in range(8):
                line = f * 24 + c * 8 + h
                block = back[h * 64 + f * 8 : h * 64 + f * 8 + 8, c * 128 : c * 128 + 128]
                lines[line : line + 1, :] = jnp.sum(block * mask, 0, keepdims=True)
    flat = lax.dot_general(
        lines[...], spread_select(), (((1,), (1,)), ((), ())),
        preferred_element_type=F32, precision=lax.Precision.HIGHEST,
    )
    frames_out[...] = flat.reshape(8, 3, 8, 64)
    og_all = og_total[0:2, :]
    rg_all = rg_total[0:2, :]
    for q in range(16):
        tail_out[152 + 2 * q : 154 + 2 * q, :] = og_all[:, 128 * q : 128 * q + 128] * share
    for q in range(4):
        tail_out[184 + 2 * q : 186 + 2 * q, :] = rg_all[:, 128 * q : 128 * q + 128] * share
    tail_out[192:194, :] = totals[:, :128] * share


def plane_pieces(near, far):
    return near.at[0], far.at[0], near.at[1], far.at[1]


def send_tiles(tiles, buffer, semaphores):
    copies = []
    for k, (fill, target) in enumerate(tiles):
        fill(buffer.at[k])
        copies.append(pltpu.make_async_copy(buffer.at[k], target, semaphores.at[k]))
        copies[-1].start()
    return copies


def finish_middle(info, near, far, near2, far2, *rest):
    out, token, buffer, semaphores = rest[-4:]
    token[...] = jnp.zeros(token.shape, F32)
    tiles = []
    for one, two, bit, partner in (
        (near, far, info[0], False), (near2, far2, 1 - info[0], True)
    ):
        row = pl.ds(pl.multiple_of(256 * bit, 128), 256)
        for piece, block in zip(plane_pieces(one, two), block_order(info, partner)):

            def fill(target, piece=piece):
                for tap in range(9):
                    target[tap] = piece[256 * tap : 256 * tap + 256, :].astype(F32)

            tiles.append((fill, out.at[:, row, lanes(128 * block, 128)]))
    for copy in send_tiles(tiles, buffer, semaphores):
        copy.wait()


def start_outer(
    first, info, mine, pair, expand_out, reduce_out,
    expand_buffer, reduce_buffer, expand_semaphores, reduce_semaphores,
):
    expand_tiles, reduce_tiles = [], []
    for pieces, bit, partner in ((mine, info[0], False), (pair, 1 - info[0], True)):
        order = block_order(info, partner)
        expand_row = pl.ds(pl.multiple_of(256 * bit, 128), 256)
        reduce_row = pl.ds(pl.multiple_of(1024 * bit, 128), 1024)
        for k, block in enumerate((order[1], order[3]) if first else (order[0], order[2])):

            def fill_expand(target, piece=pieces.at[k]):
                for q in range(4):
                    tile = piece[256 * q : 256 * q + 256, :].astype(F32)
                    target[:, 128 * q : 128 * q + 128] = tile

            def fill_reduce(target, piece=pieces.at[k]):
                target[...] = piece[1024:2048, :].astype(F32)

            expand_tiles.append((fill_expand, expand_out.at[expand_row, lanes(512 * block, 512)]))
            reduce_tiles.append((fill_reduce, reduce_out.at[reduce_row, lanes(128 * block, 128)]))
    copies = send_tiles(expand_tiles, expand_buffer, expand_semaphores)
    return copies + send_tiles(reduce_tiles, reduce_buffer, reduce_semaphores)


def finish_outer(first, info, mine, pair, *rest):
    expand_out, reduce_out, token = rest[-7:-4]
    token[...] = jnp.zeros(token.shape, F32)
    for copy in start_outer(first, info, mine, pair, expand_out, reduce_out, *rest[-4:]):
        copy.wait()


def finish_small(
    info, near, far, near2, far2, tail0, tail1, tail2, tail3,
    dsqueeze, dexcite, dfine, dcoarse, stem_out, diff_out, gain_s, bias_s, gain_r, bias_r,
    gain_x, bias_x, scratch, tail,
):
    for one, two, partner in ((near, far, False), (near2, far2, True)):
        for piece, block in zip(plane_pieces(one, two), block_order(info, partner)):
            rows = pl.ds(pl.multiple_of(64 * block, 64), 64)
            here = jnp.concatenate([piece[0:64, :], piece[64:128, :]], 1).astype(F32)
            scratch[rows, :] = scratch[rows, :] + here if partner else here
    tail[...] = tail0[...] + tail1[...] + tail2[...] + tail3[...]
    rows = scratch[...]
    dsqueeze[:, :256] = rows[0:32]
    dsqueeze[:, 256:] = rows[32:64]
    dexcite[:, :256] = rows[64:96]
    dexcite[:, 256:] = rows[96:128]
    for k in range(8):
        dfine[k] = rows[128:160, 32 * k : 32 * k + 32]
    dfine[8] = rows[160:192, 0:32]
    for k in range(9):
        dcoarse[k] = (
            rows[160:192, 32 * (k - 2) : 32 * (k - 2) + 32]
            if 3 <= k < 6
            else jnp.zeros((32, 32), F32)
        )
    stem_out[...] = tail[0:152, :].T[0:64, 0:147]
    for k in range(9):
        diff_out[k] = tail[6 * k : 6 * k + 6, 64:128]
    for q in range(16):
        bias_x[:, 128 * q : 128 * q + 128] = tail[152 + 2 * q : 153 + 2 * q, :]
        gain_x[:, 128 * q : 128 * q + 128] = tail[153 + 2 * q : 154 + 2 * q, :]
    for q in range(4):
        bias_r[:, 128 * q : 128 * q + 128] = tail[184 + 2 * q : 185 + 2 * q, :]
        gain_r[:, 128 * q : 128 * q + 128] = tail[185 + 2 * q : 186 + 2 * q, :]
    bias_s[...] = tail[192:193, :64]
    gain_s[...] = tail[193:194, :64]


def finish_rest(info, near, far, near2, far2, tail0, tail1, tail2, tail3, frames, *rest):
    rest[1][0] = frames[...]
    finish_small(info, near, far, near2, far2, tail0, tail1, tail2, tail3, *rest[2:])


def shape(dims, dtype=F32):
    return jax.ShapeDtypeStruct(dims, dtype)


def whole(dims):
    count = len(dims)
    return pl.BlockSpec(dims, lambda i, *scalars: (0,) * count)


class Far:
    def __init__(self, array, start=0, rows=None, clip=False, split=False, other=None):
        self.array, self.start, self.rows, self.clip = array, start, rows, clip
        self.split, self.other = split, other

    def copies(self):
        return self.array.shape[0] if self.split else 1

    def arrays(self):
        return [self.array] if self.other is None else [self.array, self.other]

    def buffer(self):
        dims = self.array.shape
        if self.clip:
            dims = dims[1:]
        elif self.rows is not None:
            dims = (self.rows,) + dims[1:]
        return pltpu.VMEM(dims, self.array.dtype)

    def source(self, ref, scalars):
        if self.clip:
            return ref.at[scalars[0][0]]
        if self.rows is not None:
            return ref.at[pl.ds(self.start, self.rows)]
        return ref


jax.tree_util.register_pytree_node(
    Far,
    lambda far: ((far.array, far.other), (far.start, far.rows, far.clip, far.split)),
    lambda rest, children: Far(children[0], *rest, children[1]),
)


class FarRef:
    def __init__(self, sources, buffer, semaphores, info):
        self.buffer, self.shape = buffer, buffer.shape
        source = sources[0]
        if len(semaphores) == 1:
            self.copies = [pltpu.make_async_copy(source, buffer, semaphores[0])]
        else:
            self.copies = [
                pltpu.make_async_copy(source.at[k], buffer.at[k], semaphore)
                for k, semaphore in enumerate(semaphores)
            ]
        if len(sources) == 1:
            for copy in self.copies:
                copy.start()
        else:
            other = pltpu.make_async_copy(sources[1], buffer, semaphores[0])
            pl.when(info[info.shape[0] - 1] == 1)(self.copies[0].start)
            pl.when(info[info.shape[0] - 1] == 0)(other.start)
        self.pending = set(range(len(self.copies)))

    def wait(self, part=None):
        for k in sorted(self.pending if part is None else self.pending & {part}):
            self.copies[k].wait()
            self.pending.discard(k)

    def __getitem__(self, place):
        self.wait(place if len(self.copies) > 1 and isinstance(place, int) else None)
        return self.buffer[place]


class FarOut:
    def __init__(self, out, parts=None):
        self.out = out
        self.parts = parts or [(0, out.shape[0])]


class FarOutRef:
    def __init__(self, buffer, home, semaphores, parts):
        self.buffer, self.shape = buffer, buffer.shape
        self.copies = [
            pltpu.make_async_copy(
                buffer.at[pl.ds(start, rows)], home.at[pl.ds(start, rows)], semaphore
            )
            for (start, rows), semaphore in zip(parts, semaphores)
        ]
        self.started = 0

    def __getitem__(self, place):
        return self.buffer[place]

    def __setitem__(self, place, value):
        self.buffer[place] = value

    def flush(self):
        self.copies[self.started].start()
        self.started += 1

    def finish(self):
        while self.started < len(self.copies):
            self.flush()
        for copy in self.copies:
            copy.wait()


def run(
    kernel, outs, arrays, scalars=(), scratch=(), choose=None, deps=(), cost=COST
):
    flat, tree = jax.tree.flatten(tuple(arrays), is_leaf=lambda x: isinstance(x, Far))
    operands, in_specs, places = [], [], []
    for array in flat:
        places.append(len(operands))
        if isinstance(array, Far):
            for piece in array.arrays():
                operands.append(pltpu.with_memory_space_constraint(piece, pltpu.HBM))
                in_specs.append(pl.BlockSpec(memory_space=pltpu.HBM))
            continue
        operands.append(array)
        in_specs.append(whole(array.shape))
    read = len(operands)
    for array in deps:
        operands.append(array)
        in_specs.append(pl.BlockSpec(memory_space=pl.ANY))
    out_specs, out_shape = [], []
    for out in outs:
        if isinstance(out, FarOut):
            out_specs.append(pl.BlockSpec(memory_space=pltpu.HBM))
            out_shape.append(pltpu.HBM(out.out.shape, out.out.dtype))
        else:
            out_specs.append(whole(out.shape))
            out_shape.append(out)
    far_in = [p for p, array in enumerate(flat) if isinstance(array, Far)]
    far_out = [p for p, out in enumerate(outs) if isinstance(out, FarOut)]
    buffers = [flat[p].buffer() for p in far_in]
    buffers += [pltpu.VMEM(outs[p].out.shape, outs[p].out.dtype) for p in far_out]
    moves = len(buffers)
    semaphore_count = sum(flat[p].copies() for p in far_in)
    semaphore_count += sum(len(outs[p].parts) for p in far_out)
    prefetched = tuple(scalars) if choose is None else tuple(scalars) + (choose,)

    def regrouped(*refs):
        first = len(prefetched)
        last = first + len(operands)
        end = last + len(outs)
        near, results = refs[first : first + read], list(refs[last:end])
        kept = refs[end : end + moves]
        semaphores = refs[end + moves] if moves else None
        rest = refs[end + moves + 1 :] if moves else refs[end:]
        ins = [near[place] for place in places]
        used = 0
        for k, p in enumerate(far_in):
            far = flat[p]
            own = [semaphores.at[used + n] for n in range(far.copies())]
            used += far.copies()
            sources = [
                far.source(near[places[p] + j], refs[:first]) for j in range(len(far.arrays()))
            ]
            ins[p] = FarRef(sources, kept[k], own, refs[first - 1])
        for k, p in enumerate(far_out):
            parts = outs[p].parts
            own = [semaphores.at[used + n] for n in range(len(parts))]
            used += len(parts)
            results[p] = FarOutRef(kept[len(far_in) + k], results[p], own, parts)
        kernel(*refs[: len(scalars)], *jax.tree.unflatten(tree, ins), *results, *rest)
        for p in far_in:
            ins[p].wait()
        for p in far_out:
            results[p].finish()

    return pl.pallas_call(
        regrouped,
        grid_spec=pltpu.PrefetchScalarGridSpec(
            num_scalar_prefetch=len(prefetched),
            grid=(1,),
            in_specs=in_specs,
            out_specs=out_specs,
            scratch_shapes=buffers
            + ([pltpu.SemaphoreType.DMA((semaphore_count,))] if moves else [])
            + list(scratch),
        ),
        out_shape=out_shape,
        compiler_params=pltpu.CompilerParams(vmem_limit_bytes=VMEM_BYTES),
        cost_estimate=pl.CostEstimate(flops=cost, bytes_accessed=cost, transcendentals=0),
    )(*prefetched, *operands)


ALL = ("z", "y", "x", "c")


def exchange(value, partner, whole_route=False):
    count = lax.axis_size(ALL)
    route = [(i, partner(i)) for i in range(count) if whole_route or partner(i) != i]
    return lax.ppermute(value, ALL, route)


def by_mask(value, mask):
    return exchange(value, lambda i: i ^ mask)


def bit_count(n):
    count = n.bit_length() - 1
    assert n == 1 << count
    return count


def swap_bits(i, first, second):
    if (i >> first & 1) != (i >> second & 1):
        i ^= (1 << first) | (1 << second)
    return i


def finish(kernel, info, pieces, outs, scratch, into=(), deps=()):
    far = [pl.BlockSpec(memory_space=pltpu.HBM)]
    first = 1 + len(pieces) + len(deps)
    return pl.pallas_call(
        kernel,
        grid_spec=pltpu.PrefetchScalarGridSpec(
            num_scalar_prefetch=1,
            grid=(1,),
            in_specs=[whole(piece.shape) for piece in pieces]
            + [pl.BlockSpec(memory_space=pl.ANY)] * len(deps)
            + far * len(into),
            out_specs=far * len(outs) + [whole((8, 128))],
            scratch_shapes=scratch,
        ),
        out_shape=[pltpu.HBM(out.shape, out.dtype) for out in outs] + [shape((8, 128))],
        input_output_aliases={first + k: k for k in range(len(into))},
        compiler_params=pltpu.CompilerParams(vmem_limit_bytes=VMEM_BYTES),
    )(info, *pieces, *deps, *(pltpu.with_memory_space_constraint(a, pltpu.HBM) for a in into))


def body(
    frames,
    cut_mask,
    offsets,
    stem_kernel,
    diff_kernel,
    stem_gain,
    stem_bias,
    reduce_weight,
    reduce_gain,
    reduce_bias,
    squeeze_weight,
    fine_kernel,
    coarse_kernel,
    excite_weight,
    middle_kernel,
    expand_weight,
    expand_gain,
    expand_bias,
    cotangent,
):
    depth = lax.axis_size("z")
    groups = 2 * depth
    assert frames.shape[0] == MICRO
    bits = bit_count(depth) + 3
    index = lax.axis_index(ALL)
    stem_total = float(4096 * groups)
    row_total = float(128 * groups)
    clip = lax.rem(index, 4).astype(jnp.int32)
    place = clip.reshape(1)
    bit_list = [lax.rem(lax.div(index, 1 << b), 2) for b in range(bits)]
    stays = jnp.where(bit_list[0] == bit_list[2], 1, 0)
    info = jnp.stack(bit_list + [stays]).astype(jnp.int32)
    plane = [(1, 2), (2, 1)]
    plane_mask = 6
    fine_flat = fine_kernel.reshape(288, 32)
    coarse_flat = coarse_kernel.reshape(288, 32)
    gain_s = jnp.tile(stem_gain, 8)[None]
    bias_s = jnp.tile(stem_bias, 8)[None]
    gain_r = reduce_gain[None]
    bias_r = reduce_bias[None]
    gain_x = expand_gain[None]
    bias_x = expand_bias[None]

    def swapped(value, whole_route=False):
        return exchange(value, lambda i: swap_bits(i, 0, 2), whole_route)

    def along(value, choice):
        return exchange(value, lambda i: i ^ (1 << choice[i & 1]))

    def pooled_sum(value):
        return depth_pieces(value + by_mask(value, 1))

    def depth_pieces(value):
        if depth > 4:
            return (lax.psum(value, "z"),)
        return (value,) + tuple(by_mask(value, m << 3) for m in reversed(range(1, depth)))

    def sums_shape(width):
        return shape((2, width))

    def to_plane(pieces):
        own, first, second, both = pieces
        both = by_mask(both, plane_mask)
        return own, along(first, plane[0]), along(second, plane[1]), both

    def padded(rows):
        unit = 16 * depth
        return -(-rows // unit) * unit

    def far(*arrays):
        return tuple(Far(array) for array in arrays)

    def stack(*pieces, deps=()):
        rows = sum(piece.shape[0] for piece in pieces)
        return run(stack_rows, [shape((rows, pieces[0].shape[1]), BF)], pieces, deps=deps)[0]

    def add(first, second, deps=()):
        return run(add_floats, [shape(first.shape)], (first, second), deps=deps)[0]

    def halves(kernel, rows, arrays, deps=()):
        return run(
            kernel, [shape((rows // 2, 128), BF)] * 2, arrays, (info,),
            [pltpu.VMEM((rows, 128), BF)], deps=deps,
        )

    (pack,) = run(
        pack_clip,
        [shape((208, 64), BF)],
        (*far(cut_mask, offsets[None]), Far(frames, clip=True)),
        (place,),
    )
    pack = (pack, swapped(pack))

    def far_pack():
        return Far(pack[0], other=pack[1])

    stem_scratch = [
        pltpu.VMEM((512, 896), BF),
        pltpu.VMEM((256, 384), BF),
        pltpu.VMEM((896, 512), BF),
        pltpu.VMEM((384, 512), BF),
        pltpu.VMEM((192, 128), F32),
        pltpu.VMEM((512, 384), F32),
    ]
    stem_weights = far(stem_kernel.T, diff_kernel)
    v, stem_sums = run(
        stem_front,
        [shape((512, 512)), sums_shape(512)],
        (pack, *stem_weights),
        (info,),
        stem_scratch,
    )
    stem_sums = pooled_sum(stem_sums)
    (cot,) = run(
        lambda place, *refs: copy_rows(*refs),
        [FarOut(shape(cotangent.shape[1:], BF))],
        (Far(cotangent, clip=True),),
        (place,),
        deps=(stem_sums[0],),
    )
    cot_got = swapped(cot)
    stem_norm = far(gain_s, bias_s)
    wide, wide_keep, send, red, red_sums, stem_saved = run(
        functools.partial(stem_close, stem_total),
        [
            FarOut(shape((128, 2048), BF)),
            shape((128, 1024), BF),
            shape((128, 1024), BF),
            shape((128, 512)),
            sums_shape(512),
            FarOut(shape((520, 512))),
        ],
        (v, stem_sums, *stem_norm, Far(reduce_weight)),
        (info,),
    )
    wide_pair = by_mask(send, 1)
    red_sums = pooled_sum(red_sums)
    wide_chip = stack(wide_keep, wide_pair, deps=(red_sums[0], cot_got))
    wide_got = along(wide_chip, plane[0])
    gate_weights = far(squeeze_weight.T, fine_flat, coarse_flat, excite_weight)
    gate_weights += (Far(middle_kernel, split=True),)
    both_keep, send, expanded, exp_sums, saved = run(
        functools.partial(gate_front, row_total),
        [
            shape((128, 512), BF),
            shape((128, 512), BF),
            shape((128, 2048)),
            sums_shape(2048),
            FarOut(shape((264, 512)), [(0, 136), (136, 128)]),
        ],
        (
            red, red_sums, far_pack(), *far(gain_r, bias_r), *gate_weights, Far(expand_weight),
        ),
        (info,),
        [pltpu.VMEM((128, 1024), BF)],
        choose=info,
        deps=(wide_chip,),
    )
    both_pair = by_mask(send, 1)
    exp_sums = pooled_sum(exp_sums)
    both_chip = stack(both_keep, both_pair, deps=(exp_sums[0],))
    both_got = along(both_chip, plane[0])
    wide_near = stack(wide_chip, wide_got, deps=(both_chip,))
    wide_far = along(wide_near, plane[1])
    og_sums, out_saved = run(
        functools.partial(out_back, row_total),
        [
            sums_shape(2048),
            FarOut(shape((264, 2048)), [(0, 64), (128, 64), (64, 64), (192, 72)]),
        ],
        (expanded, exp_sums, *far(gain_x, bias_x, wide), Far(cot, other=cot_got)),
        choose=info,
        deps=(wide_near,),
    )
    og_sums = pooled_sum(og_sums)
    both_near = stack(both_chip, both_got, deps=(og_sums[0],))
    both_far = along(both_near, plane[1])
    hg, og_total, *blocks = run(
        functools.partial(expand_back, row_total),
        [shape((128, 512), BF), FarOut(shape((8, 2048)))] + [shape((128, 640), BF)] * 4,
        (og_sums, Far(out_saved), Far(saved, 136, 128), *far(gain_x, expand_weight)),
        (info,),
        [pltpu.VMEM((128, 512), BF), pltpu.VMEM((128, 2048), BF)],
        deps=(both_near,),
    )
    blocks = to_plane(blocks)
    rg, rg_sums, small = run(
        gate_back,
        [shape((128, 512)), sums_shape(512), shape((256, 256))],
        (far_pack(), hg, Far(saved, 0, 128), *far(gain_r, bias_r), *gate_weights),
        choose=info,
        deps=(wide_far, both_far),
    )
    rg_sums = pooled_sum(rg_sums)
    blocks = stack(*blocks, deps=(rg_sums[0],))
    blocks_pair = by_mask(blocks, 1)

    middle_rows = padded(2304)
    outer_rows = padded(2176)
    depth_bits = list(range(3, bits))
    have = {}
    held = [tuple(rg_sums[1:])]

    def waits():
        deps, held[0] = held[0], ()
        return deps

    def paired(value, rows):
        return value.reshape(2, rows, 128), by_mask(value, 1).reshape(2, rows, 128)

    def halve(name):
        deps = waits()
        for bit in depth_bits[1:]:
            keep, got = have[name]
            keep, send = halves(
                functools.partial(add_halves, bit), keep.shape[0], (keep, got), deps
            )
            have[name] = keep, by_mask(send, 1 << bit)
            deps = ()
        return keep

    def sum_up(name):
        keep, got = have[name]
        (value,) = run(add_rows, [shape(keep.shape, BF)], (keep, got), deps=waits())
        have[name] = value, by_mask(value, 1 << depth_bits[-1])
        return value

    def join(name, depth_range):
        deps = waits()
        for bit in depth_range:
            value, got = have[name]
            rows, width = value.shape
            (value,) = run(
                functools.partial(join_halves, bit),
                [shape((2 * rows, width), BF)],
                (value, got),
                (info,),
                deps=deps,
            )
            if bit > 3:
                have[name] = value, by_mask(value, 1 << (bit - 1))
            deps = ()
        if depth_range[-1] == 3:
            have[name] = value, along(value, plane[1])
        return value

    def near(name, rows):
        value = stack(*have[name], deps=waits())
        have[name + " far"] = along(value, plane[0])
        have[name + " near"] = paired(value, rows)
        return value

    def middle_kernel_sum():
        keep, send = halves(
            middle_weights, middle_rows, ((both_near, both_far), (blocks, blocks_pair)), waits()
        )
        have["middle"] = keep, by_mask(send, 8)
        return keep

    def reduction_back():
        rs, rs_sums, rg_total, *late = run(
            functools.partial(reduce_back, row_total),
            [shape((512, 512)), sums_shape(512), FarOut(shape((8, 512)))]
            + [shape((128, 256), BF)] * 4,
            (
                small, rg, rg_sums, Far(saved, 0, 136), Far(gain_r), Far(out_saved, 0, 128),
                *far(reduce_weight, stem_saved), *stem_norm,
            ),
            (info,),
            [pltpu.VMEM((128, 512), BF)],
            deps=waits(),
        )
        have["rs"] = rs, rs_sums, rg_total
        have["late"] = to_plane(late)
        return rs

    def stem_sum():
        rs_sums = have["rs"][1]
        have["rs here"] = add(rs_sums, by_mask(rs_sums, 1), waits())
        return have["rs here"]

    def late_rows():
        have["late"] = stack(*have["late"], deps=waits())
        have["late pair"] = by_mask(have["late"], 1)
        return have["late"]

    def outer_kernel_sum():
        keep, send = halves(
            outer_weights,
            outer_rows,
            (
                (both_near, both_far), (blocks, blocks_pair), (wide_near, wide_far),
                (have["late"], have["late pair"]),
            ),
            waits(),
        )
        have["outer"] = keep, by_mask(send, 8)
        return keep

    def stem_pieces():
        have["rs pieces"] = depth_pieces(have["rs here"])
        return held[0] + have["rs pieces"]

    def stem_gradient():
        rs, _, rg_total = have["rs"]
        have["frame"], have["tail"] = run(
            functools.partial(stem_back, stem_total, 1.0 / groups),
            [shape((8, 3, 8, 64)), shape((200, 128))],
            (
                far_pack(), *stem_weights, Far(stem_saved), stem_norm[0], rs, have["rs pieces"],
                Far(og_total), Far(rg_total),
            ),
            scratch=stem_scratch,
            choose=info,
            deps=waits(),
        )
        return have["tail"]

    def tail_add(bits_here):
        deps = waits()
        for bit in bits_here:
            have["tail"] = add(have["tail"], by_mask(have["tail"], 1 << bit), deps)
            deps = ()
        return have["tail"]

    def middle_far_rows():
        value = stack(have["middle far"], deps=waits())
        have["middle far"] = paired(value, middle_rows)
        return value

    outer_scratch = [
        pltpu.VMEM((4, 256, 512), F32),
        pltpu.VMEM((4, 1024, 128), F32),
        pltpu.SemaphoreType.DMA((4,)),
        pltpu.SemaphoreType.DMA((4,)),
    ]

    def middle_finish():
        one, two = have["middle near"], have["middle far"]
        have["dmiddle"], token = finish(
            finish_middle,
            info,
            (one[0], two[0], one[1], two[1]),
            [shape((9, 512, 512))],
            [pltpu.VMEM((8, 9, 256, 128), F32), pltpu.SemaphoreType.DMA((8,))],
            deps=waits(),
        )
        return token

    def outer_finish():
        dexpand, dreduce, token = finish(
            functools.partial(finish_outer, False),
            info,
            have["outer near"],
            [shape((512, 2048)), shape((2048, 512))],
            outer_scratch,
            deps=waits(),
        )
        have["outer out"] = dexpand, dreduce
        return token

    steps = {
        "K": middle_kernel_sum,
        "R": reduction_back,
        "Ma": lambda: halve("middle"),
        "Mb": lambda: sum_up("middle"),
        "Mc": lambda: join("middle", depth_bits[:0:-1]),
        "Md": lambda: join("middle", depth_bits[:1]),
        "Mn": lambda: near("middle", middle_rows),
        "Mf": middle_far_rows,
        "Rs": stem_sum,
        "St": late_rows,
        "O": outer_kernel_sum,
        "Oa": lambda: halve("outer"),
        "Ob": lambda: sum_up("outer"),
        "Oc": lambda: join("outer", depth_bits[:0:-1]),
        "Od": lambda: join("outer", depth_bits[:1]),
        "On": lambda: near("outer", outer_rows),
        "Z": stem_pieces,
        "B": stem_gradient,
        "T0": lambda: tail_add([0]),
        "T3": lambda: tail_add(depth_bits[:-1]),
        "T4": lambda: tail_add(depth_bits[-1:]),
        "F": middle_finish,
        "G": outer_finish,
    }
    for name in ORDER:
        result = steps[name]()
        held[0] = result if isinstance(result, tuple) else (result,)
    frame_grad, tail = have["frame"], have["tail"]
    dmiddle = have["dmiddle"]
    dexpand, dreduce = have["outer out"]
    outer_near = have["outer near"]
    token = held[0][0]
    outer_far = have["outer far"]
    frame_grad = swapped(frame_grad, True)
    outer_far = stack(outer_far, deps=(token,))
    outer_far = paired(outer_far, outer_rows)
    tail = (tail,) + tuple(by_mask(tail, mask) for mask in (6, 4, 2))
    dexpand, dreduce, token = finish(
        functools.partial(finish_outer, True),
        info,
        outer_far,
        [shape((512, 2048)), shape((2048, 512))],
        outer_scratch,
        (dexpand, dreduce),
    )
    outer = (outer_near[0], outer_far[0], outer_near[1], outer_far[1])
    small_shapes = ((1, 8, 3, 8, 64), (32, 512), (32, 512), (9, 32, 32), (9, 32, 32), (64, 147))
    small_shapes += ((9, 6, 64),) + tuple((1, n) for n in (64, 64, 512, 512, 2048, 2048))
    (
        frame_grad, dsqueeze, dexcite, dfine, dcoarse, dstem, ddiff, gain_s, bias_s, gain_r,
        bias_r, gain_x, bias_x,
    ) = pl.pallas_call(
        finish_rest,
        grid_spec=pltpu.PrefetchScalarGridSpec(
            num_scalar_prefetch=1,
            grid=(1,),
            in_specs=[pl.BlockSpec((2, 128, 128), lambda i, info: (0, 16, 0))] * 4
            + [whole((200, 128))] * 4
            + [whole((8, 3, 8, 64)), pl.BlockSpec(memory_space=pl.ANY)],
            out_specs=[whole(d) for d in small_shapes],
            scratch_shapes=[pltpu.VMEM((256, 256), F32), pltpu.VMEM((200, 128), F32)],
        ),
        out_shape=[shape(d) for d in small_shapes],
        compiler_params=pltpu.CompilerParams(vmem_limit_bytes=FINISH_BYTES),
    )(info, *outer, *tail, frame_grad, token)
    return (
        frame_grad,
        dstem.T,
        ddiff,
        gain_s[0],
        bias_s[0],
        dreduce,
        gain_r[0],
        bias_r[0],
        dsqueeze.T,
        dfine,
        dcoarse,
        dexcite,
        dmiddle,
        dexpand,
        gain_x[0],
        bias_x[0],
    )


def solution(mesh):
    split = jax.sharding.Mesh(mesh.devices.reshape(-1, 2, 2, 2), ALL)
    copied = P()
    by_group = P(("z", "y"))
    in_specs = (by_group,) * 3 + (copied,) * 15 + (by_group,)
    out_specs = (P(ALL),) + (copied,) * 15
    return jax.shard_map(body, mesh=split, in_specs=in_specs, out_specs=out_specs, check_vma=False)
```

```python
import functools

import jax
import jax.numpy as jnp
from jax import lax
from jax.experimental import pallas as pl
from jax.experimental.pallas import tpu as pltpu
from jax.sharding import PartitionSpec as P

FRAMES = 8
MICRO = 4
EPSILON = 1e-05
COST = 1_000_000
ORDER = (
    ("K", "R", "Ma", "St", "Rs", "Mb", "O", "Mc", "Oa", "Z", "Md", "B", "Ob", "Mn", "Oc", "Od")
    + ("T0", "Mf", "T3", "On", "F", "T4", "G")
)
FINISH_BYTES = 16 * 1024 * 1024
VMEM_BYTES = 32 * 1024 * 1024
BF = jnp.bfloat16
F32 = jnp.float32

STEM = 64
SLOT = 16


def dot(left, right):
    return jnp.dot(left, right, preferred_element_type=F32)


def dot_nt(left, right):
    return lax.dot_general(left, right, (((1,), (1,)), ((), ())), preferred_element_type=F32)


def dot_tn(left, right):
    return lax.dot_general(left, right, (((0,), (0,)), ((), ())), preferred_element_type=F32)


def dot_exact(left, right):
    return jnp.dot(left, right, preferred_element_type=F32, precision=lax.Precision.HIGHEST)


def iota(shape, dim):
    return lax.broadcasted_iota(jnp.int32, shape, dim)


def sigmoid(v):
    return 1.0 / (1.0 + jnp.exp(-v))


def swish_slope(v):
    s = sigmoid(v)
    return s * (1.0 + v * (1.0 - s))


def keep_column(pack, lanes):
    rows = pack[192:208, :].astype(F32)
    return jnp.concatenate(
        [jnp.broadcast_to(rows[f : f + 1, :lanes], (8, lanes)) for f in range(FRAMES)], 0
    )


def gate_column(pack):
    keep = keep_column(pack, 64)
    both = jnp.concatenate([keep, keep], 1)
    return jnp.concatenate([jnp.zeros((8, 128), F32), both[:-8]], 0)


def pack_clip(place, cut, offset, frames, out):
    clip = place[0]
    row = cut[pl.ds(clip, 1), :]
    own = iota((1, MICRO), 1) == clip
    stop = jnp.sum(jnp.where(own, offset[...], 0), 1, keepdims=True)
    step = iota(row.shape, 1)
    valid = jnp.where(step + 1 == stop, 0, row).astype(F32)
    spread = iota((16, FRAMES - 1), 0) == iota((16, FRAMES - 1), 1)
    column = jnp.sum(jnp.where(spread, valid, 0.0), 1, keepdims=True)
    out[0:192, :] = frames[...].astype(F32).reshape(192, 64).astype(BF)
    out[192:208, :] = jnp.broadcast_to(column, (16, 64)).astype(BF)


def summed_up(pieces):
    value = pieces[0][...]
    for piece in pieces[1:]:
        value = value + piece[...]
    return value


def spread_sums(out, first, second):
    out[...] = jnp.concatenate([first, second], 0)


def norm_scale(sums, row_total):
    mean = sums[0:1] * (1.0 / row_total)
    variance = sums[1:2] * (1.0 / row_total) - mean * mean
    return mean, lax.rsqrt(variance + EPSILON)


def column_sums(out, first, second):
    spread_sums(out, jnp.sum(first, 0, keepdims=True), jnp.sum(second, 0, keepdims=True))


def fold_lanes(sums):
    for step in (64, 128, 256):
        sums = sums + pltpu.roll(sums, step, 1)
    return sums


def shift_rows(v, dy, dx):
    rows = v.shape[0]
    if dx:
        rolled = pltpu.roll(v, (-dx) % rows, 0)
        wb = lax.rem(iota(v.shape, 0), 8)
        v = jnp.where((wb + dx >= 0) & (wb + dx < 8), rolled, 0.0)
    half = rows // 2
    if dy == 1:
        v = jnp.concatenate([v[half:], jnp.zeros_like(v[half:])], 0)
    elif dy == -1:
        v = jnp.concatenate([jnp.zeros_like(v[:half]), v[:half]], 0)
    return v


def cell_sum(v):
    half = v.shape[0] // 2
    both = v[:half] + v[half:]
    even = lax.rem(iota(both.shape, 0), 2) == 0
    both = both + jnp.where(even, pltpu.roll(both, half - 1, 0), pltpu.roll(both, 1, 0))
    return jnp.concatenate([both, both], 0)


def taps(v):
    return [shift_rows(v, ky - 1, kx - 1) for ky in range(3) for kx in range(3)]


def back_taps(v):
    return [shift_rows(v, 1 - ky, 1 - kx) for ky in range(3) for kx in range(3)]


def coarse_taps(v):
    return [shift_rows(v, 0, 2 * (k - 1)) for k in range(3)]


def window_select(rows, cols, kind):
    place = iota((rows, cols), 0)
    col = iota((rows, cols), 1)
    lane = lax.rem(place, 128)
    tap_row = lax.div(place, 128)
    channel = lax.div(lane, SLOT)
    slot = lax.rem(lane, SLOT)
    if kind == "stem":
        hit = (col == (7 * tap_row + slot) * 3 + channel) & (slot < 7) & (channel < 3)
        return jnp.where(hit, 1.0, 0.0)
    cell = lax.div(slot - 1, 2)
    hit = (col == (3 * tap_row + cell) * 6 + channel) & (slot >= 1) & (slot < 7) & (channel < 6)
    return jnp.where(hit, 0.25, 0.0)


def spread_select():
    w = iota((64, 128), 0)
    lane = iota((64, 128), 1)
    return jnp.where(w == 8 * lax.div(lane, SLOT) + lax.rem(lane, SLOT) - 3, 1.0, 0.0)


def gather_select():
    row = iota((384, 128), 0)
    col = iota((384, 128), 1)
    return jnp.where(col == lax.div(row, 128) * SLOT + lax.rem(row, SLOT), 1.0, 0.0)


def own_block():
    row = iota((8, 128), 0)
    lane = iota((8, 128), 1)
    return jnp.where(lax.div(lane, SLOT) == row, 1.0, 0.0)


def stem_windows(pack, kernel, diff, win, win2, u, u2, spread, tiles):
    spread[...] = dot(pack[0:192, :], spread_select().astype(BF))
    mask = own_block()
    for f in range(8):
        for c in range(3):
            for h in range(8):
                line = f * 24 + c * 8 + h
                tiles[h * 64 + f * 8 : h * 64 + f * 8 + 8, c * 128 : c * 128 + 128] = (
                    jnp.broadcast_to(spread[line : line + 1, :], (8, 128)) * mask
                )
    pixels = dot(tiles[...].astype(BF), gather_select().astype(BF))
    rows = [pixels[64 * h : 64 * h + 64] for h in range(8)]
    gate = gate_column(pack)
    steps = []
    for h2 in range(4):
        both = rows[2 * h2] + rows[2 * h2 + 1]
        step = (both - jnp.concatenate([jnp.zeros((8, 128), F32), both[:-8]], 0)) * gate
        later = jnp.concatenate([step[8:], jnp.zeros((8, 128), F32)], 0)
        steps.append((step + pltpu.roll(later, 48, 1)).astype(BF))
    rows = [r.astype(BF) for r in rows]
    blank = jnp.zeros((64, 128), BF)
    for dy in range(7):
        for h in range(8):
            source = h + dy - 3
            win[64 * h : 64 * h + 64, 128 * dy : 128 * dy + 128] = (
                rows[source] if 0 <= source < 8 else blank
            )
    for dy in range(3):
        for h in range(4):
            source = h + dy - 1
            win2[64 * h : 64 * h + 64, 128 * dy : 128 * dy + 128] = (
                steps[source] if 0 <= source < 4 else blank
            )
    low_half = iota((896, 128), 1) < 64
    wide_kernel = jnp.concatenate([kernel[...], kernel[...]], 0)
    placed = dot_nt(window_select(896, 147, "stem").astype(BF), wide_kernel)
    taps = diff[...].astype(F32)
    rows = jnp.concatenate([taps[k] for k in range(9)], 0)
    wide_diff = jnp.concatenate([rows, rows], 1).astype(BF)
    placed2 = dot(window_select(384, 54, "diff").astype(BF), wide_diff)
    for q in range(4):
        first = pltpu.roll(placed, 2 * q, 0) if q else placed
        second = pltpu.roll(placed, 2 * q + 1, 0)
        u[:, 128 * q : 128 * q + 128] = jnp.where(low_half, first, second).astype(BF)
        u2[:, 128 * q : 128 * q + 128] = (
            pltpu.roll(placed2, 2 * q, 0) if q else placed2
        ).astype(BF)


class Pick:
    def __init__(self, info, own, other):
        self.stays = info[info.shape[0] - 1] == 1
        self.own, self.other = own, other

    def __getitem__(self, place):
        return jnp.where(self.stays, self.own[place], self.other[place])


def stem_front(
    info, pack, kernel, diff, v_out, sums_out, win, win2, u, u2, spread, tiles
):
    stem_windows(Pick(info, *pack), kernel, diff, win, win2, u, u2, spread, tiles)
    v = dot(win[...], u[...])
    side = dot(win2[...], u2[...])
    first = jnp.zeros((1, 512), F32)
    second = jnp.zeros((1, 512), F32)
    for h in range(8):
        piece = v[64 * h : 64 * h + 64] + side[64 * (h // 2) : 64 * (h // 2) + 64]
        v_out[64 * h : 64 * h + 64, :] = piece
        first = first + jnp.sum(piece, 0, keepdims=True)
        second = second + jnp.sum(piece * piece, 0, keepdims=True)
    spread_sums(sums_out, first, second)


def stem_close(
    row_total, info, v, sums, gain, bias, weight, wide_out, keep_out, send_out, red_out, sums_out,
    save,
):
    mean, scale = norm_scale(fold_lanes(summed_up(sums)), row_total)
    save[512:513, :] = scale
    for h in range(8):
        normal = (v[64 * h : 64 * h + 64, :] - mean) * scale
        save[64 * h : 64 * h + 64, :] = normal
        y = normal * gain[...] + bias[...]
        wide_out[
            64 * (h // 4) : 64 * (h // 4) + 64, 512 * (h % 4) : 512 * (h % 4) + 512
        ] = (y * sigmoid(y)).astype(BF)
    save.flush()
    wide_out.flush()
    keep_out[...] = wide_out[:, lanes(1024 * info[0], 1024)]
    send_out[...] = wide_out[:, lanes(1024 * (1 - info[0]), 1024)]
    red = dot(wide_out[...], weight[...])
    red_out[...] = red
    column_sums(sums_out, red, red * red)


def gate_path(pack, narrow, squeeze, fine, coarse, excite):
    squeezed = dot_nt(narrow.astype(BF), squeeze[...])
    keep = keep_column(pack, 32)
    parts = []
    for hb in range(2):
        part = squeezed[64 * hb : 64 * hb + 64]
        later = jnp.concatenate([part[8:], part[:8]], 0)
        parts.append((later - part) * keep)
    change = jnp.concatenate(parts, 0)
    fine_rows = jnp.concatenate(taps(change), 1).astype(BF)
    pooled = 0.25 * cell_sum(change)
    coarse_rows = jnp.concatenate(coarse_taps(pooled), 1).astype(BF)
    summed = (dot(fine_rows, fine[...]) + dot(coarse_rows, coarse[96:192, :])).astype(BF)
    return fine_rows, coarse_rows, summed, sigmoid(dot(summed, excite[...]))


def gate_front(
    row_total, info, red, sums, pack, gain, bias, squeeze, fine, coarse, excite, middle, expand,
    keep_out, send_out, exp_out, sums_out, save, both,
):
    mean, scale = norm_scale(summed_up(sums), row_total)
    normal = (red[...] - mean) * scale
    save[0:128, :] = normal
    save[128:129, :] = scale
    save.flush()
    y = normal * gain[...] + bias[...]
    narrow = y * sigmoid(y)
    gate = gate_path(pack, narrow, squeeze, fine, coarse, excite)[3]
    gated = narrow * (1.0 + gate)
    total = jnp.zeros((128, 512), F32)
    for k, piece in enumerate(taps(gated)):
        total = total + dot(piece.astype(BF), middle[k])
    save[136:264, :] = total
    save.flush()
    hidden = (total * sigmoid(total)).astype(BF)
    for half in range(2):
        part = slice(256 * half, 256 * half + 256)
        both[:, 512 * half : 512 * half + 256] = gated[:, part].astype(BF)
        both[:, 512 * half + 256 : 512 * half + 512] = hidden[:, part]
    keep_out[...] = both[:, lanes(512 * info[0], 512)]
    send_out[...] = both[:, lanes(512 * (1 - info[0]), 512)]
    expanded = dot(hidden, expand[...])
    exp_out[...] = expanded
    column_sums(sums_out, expanded, expanded * expanded)


def out_back(row_total, expanded, sums, gain, bias, wide, cot, sums_out, save, scale_out):
    mean, scale = norm_scale(summed_up(sums), row_total)
    scale_out[0:1, :] = scale
    scale_out.flush()
    first = jnp.zeros((1, 2048), F32)
    second = jnp.zeros((1, 2048), F32)
    for hb in range(2):
        part = slice(64 * hb, 64 * hb + 64)
        if hb:
            save.flush()
            save.flush()
        normal = (expanded[part, :] - mean) * scale
        y = normal * gain[...] + bias[...] + wide[part, :].astype(F32)
        weightless = cot[:, hb, :, :].astype(F32).reshape(64, 2048)
        og = weightless * swish_slope(y)
        save[part, :] = og.astype(BF)
        save[128 + 64 * hb : 192 + 64 * hb, :] = normal.astype(BF)
        first = first + jnp.sum(og, 0, keepdims=True)
        second = second + jnp.sum(og * normal, 0, keepdims=True)
    spread_sums(sums_out, first, second)


def norm_pull(grad, normal, scale, gain, grad_sums, row_total):
    return (
        gain
        * scale
        * (
            grad
            - grad_sums[0:1] * (1.0 / row_total)
            - normal * (grad_sums[1:2] * (1.0 / row_total))
        )
    )


def block_order(info, partner=False):
    block = 2 * info[1] + info[2]
    first = jnp.where((info[0] == 0) != partner, 2, 1)
    return [block, block ^ first, block ^ (3 - first), block ^ 3]


def lanes(start, width):
    return pl.ds(pl.multiple_of(start, 128), width)


def expand_back(
    row_total, info, grad_sums, saved, scale, hpre, gain, expand, hg_out, total_out, *rest
):
    outs, (hg_scratch, dv_scratch) = rest[:4], rest[4:]
    sums = summed_up(grad_sums)
    total_out[0:2, :] = sums
    total_out.flush()
    dv = norm_pull(
        saved[0:128, :].astype(F32), saved[128:256, :].astype(F32), scale[0:1, :], gain[...],
        sums, row_total,
    ).astype(BF)
    dv_scratch[...] = dv
    dhid = dot_nt(dv, expand[...]).astype(BF).astype(F32)
    hg = (dhid * swish_slope(hpre[...])).astype(BF)
    hg_out[...] = hg
    hg_scratch[...] = hg
    for out, block in zip(outs, block_order(info)):
        out[:, :128] = hg_scratch[:, lanes(128 * block, 128)]
        out[:, 128:] = dv_scratch[:, lanes(512 * block, 512)]


def all_rows(refs):
    return jnp.concatenate([ref[...] for ref in refs], 0)


def clip_rows(mine, pair, columns):
    rows = []
    for k, other in enumerate((0, 2, 1, 3)):
        rows.append(mine[128 * k : 128 * k + 128, columns])
        rows.append(pair[128 * other : 128 * other + 128, columns])
    return rows


def depth_halves(info, bit, scratch, keep_out, send_out):
    rows = keep_out.shape[0]
    mine = info[bit]
    keep_out[...] = scratch[pl.ds(pl.multiple_of(mine * rows, 16), rows), :]
    send_out[...] = scratch[pl.ds(pl.multiple_of((1 - mine) * rows, 16), rows), :]


def add_halves(bit, info, keep, got, keep_out, send_out, scratch):
    scratch[...] = (keep[...].astype(F32) + got[...].astype(F32)).astype(BF)
    depth_halves(info, bit, scratch, keep_out, send_out)


def add_rows(keep, got, out):
    out[...] = (keep[...].astype(F32) + got[...].astype(F32)).astype(BF)


def join_halves(bit, info, own, got, out):
    rows = own.shape[0]
    mine = info[bit]
    out[pl.ds(pl.multiple_of(mine * rows, 16), rows), :] = own[...]
    out[pl.ds(pl.multiple_of((1 - mine) * rows, 16), rows), :] = got[...]


def middle_weights(info, left_refs, right_refs, *rest):
    outs, (scratch,) = rest[:-1], rest[-1:]
    left = jnp.concatenate([ref[:, :256] for ref in left_refs], 0).T
    clips = [
        back_taps(rows.astype(F32)) for rows in clip_rows(*right_refs, slice(0, 128))
    ]
    for k in range(9):
        right = jnp.concatenate([clip[k] for clip in clips], 0).astype(BF)
        scratch[256 * k : 256 * k + 256, :] = dot(left, right).astype(BF)
    if scratch.shape[0] > 2304:
        scratch[2304:, :] = jnp.zeros((scratch.shape[0] - 2304, 128), BF)
    depth_halves(info, 3, scratch, *outs)


def outer_weights(info, left_refs, right_refs, wide, late, *rest):
    outs, (scratch,) = rest[:-1], rest[-1:]
    left = jnp.concatenate([ref[:, 256:] for ref in left_refs], 0)
    right = jnp.concatenate(clip_rows(*right_refs, slice(128, 640)), 0)
    result = dot_tn(left, right).astype(BF)
    for q in range(4):
        scratch[256 * q : 256 * q + 256, :] = result[:, 128 * q : 128 * q + 128]
    right = jnp.concatenate(clip_rows(*late, slice(0, 128)), 0)
    scratch[1024:2048, :] = dot_tn(all_rows(wide), right).astype(BF)
    small = [late[0][128 * k : 128 * k + 128, 128:].astype(F32) for k in range(4)]
    scratch[2048:2176, :] = sum(small).astype(BF)
    if scratch.shape[0] > 2176:
        scratch[2176:, :] = jnp.zeros((scratch.shape[0] - 2176, 128), BF)
    depth_halves(info, 3, scratch, *outs)


def copy_rows(source, out):
    out[...] = source[...]


def add_floats(first, second, out):
    out[...] = first[...] + second[...]


def stack_rows(*refs):
    out = refs[-1]
    start = 0
    for ref in refs[:-1]:
        out[start : start + ref.shape[0], :] = ref[...]
        start += ref.shape[0]


def gate_back(
    pack, hg, normal, gain, bias, squeeze, fine, coarse, excite, middle,
    rg_out, sums_out, small_out,
):
    y = normal[...] * gain[...] + bias[...]
    narrow_v = y * sigmoid(y)
    fine_rows, coarse_rows, summed, gate_v = gate_path(
        pack, narrow_v, squeeze, fine, coarse, excite
    )
    total = jnp.zeros((128, 512), F32)
    for k, piece in enumerate(back_taps(hg[...].astype(F32))):
        total = total + dot_nt(piece.astype(BF), middle[k])
    gg = total.astype(BF).astype(F32)
    narrow_grad = gg * (1.0 + gate_v)
    excite_grad = (gg * narrow_v * gate_v * (1.0 - gate_v)).astype(BF)
    dexcite = dot_tn(summed, excite_grad)
    summed_low = dot_nt(excite_grad, excite[...]).astype(BF)
    summed_grad = summed_low.astype(F32)
    coarse_low = cell_sum(summed_grad).astype(BF)
    dfine = dot_tn(fine_rows, summed_low)
    dcoarse = 0.25 * dot_tn(coarse_rows, coarse_low)
    spread = dot_nt(summed_low, fine[...])
    change_grad = jnp.zeros((128, 32), F32)
    for k in range(9):
        change_grad = change_grad + shift_rows(
            spread[:, 32 * k : 32 * k + 32], 1 - k // 3, 1 - k % 3
        )
    spread = dot_nt(coarse_low, coarse[96:192, :])
    pooled_grad = jnp.zeros((128, 32), F32)
    for k in range(3):
        pooled_grad = pooled_grad + shift_rows(spread[:, 32 * k : 32 * k + 32], 0, 2 * (1 - k))
    change_grad = change_grad + 0.25 * pooled_grad
    keep = keep_column(pack, 32)
    parts = []
    for hb in range(2):
        step = change_grad[64 * hb : 64 * hb + 64] * keep
        earlier = jnp.concatenate([step[56:], step[:56]], 0)
        parts.append(earlier - step)
    squeezed_grad = jnp.concatenate(parts, 0).astype(BF)
    dsqueeze = dot_tn(squeezed_grad, narrow_v.astype(BF))
    narrow_grad = narrow_grad + dot(squeezed_grad, squeeze[...])
    rg = narrow_grad * swish_slope(y)
    rg_out[...] = rg
    column_sums(sums_out, rg, rg * normal[...])
    small_out[0:32, :] = dsqueeze[:, :256]
    small_out[32:64, :] = dsqueeze[:, 256:]
    small_out[64:96, :] = dexcite[:, :256]
    small_out[96:128, :] = dexcite[:, 256:]
    pieces = [dfine[32 * k : 32 * k + 32] for k in range(9)]
    pieces += [dcoarse[32 * k : 32 * k + 32] for k in range(3)]
    small_out[128:160, :] = jnp.concatenate(pieces[:8], 1)
    small_out[160:192, :] = jnp.concatenate(pieces[8:] + [jnp.zeros((32, 128), F32)], 1)
    small_out[192:256, :] = jnp.zeros((64, 256), F32)


def reduce_back(
    row_total, info, small, rg, grad_sums, saved, gain, og, weight, stem_saved, stem_gain,
    stem_bias, rs_out, sums_out, total_out, dv0, dv1, dv2, dv3, dv_scratch,
):
    sums = summed_up(grad_sums)
    total_out[0:2, :] = sums
    total_out.flush()
    dv = norm_pull(
        rg[...], saved[0:128, :], saved[128:129, :], gain[...], sums, row_total
    ).astype(BF)
    dv_scratch[...] = dv
    for out, block in zip((dv0, dv1, dv2, dv3), block_order(info)):
        out[:, :128] = dv_scratch[:, lanes(128 * block, 128)]
        part = small[pl.ds(pl.multiple_of(64 * block, 64), 64), :].astype(BF)
        out[:64, 128:] = part[:, :128]
        out[64:, 128:] = part[:, 128:]
    wide_grad = dot_nt(dv, weight[...]) + og[...].astype(BF).astype(F32)
    wide_grad = wide_grad.astype(BF).astype(F32)
    first = jnp.zeros((1, 512), F32)
    second = jnp.zeros((1, 512), F32)
    for h in range(8):
        normal = stem_saved[64 * h : 64 * h + 64, :]
        y = normal * stem_gain[...] + stem_bias[...]
        rs = (
            wide_grad[64 * (h // 4) : 64 * (h // 4) + 64, 512 * (h % 4) : 512 * (h % 4) + 512]
            * swish_slope(y)
        )
        rs_out[64 * h : 64 * h + 64, :] = rs
        first = first + jnp.sum(rs, 0, keepdims=True)
        second = second + jnp.sum(rs * normal, 0, keepdims=True)
    spread_sums(sums_out, first, second)


def stem_back(
    stem_total, share, pack, kernel, diff, saved, gain, rs, grad_sums, og_total,
    rg_total, frames_out, tail_out, win, win2, u, u2, lines, tiles,
):
    stem_windows(pack, kernel, diff, win, win2, u, u2, lines, tiles)
    scale = saved[512:513, :]
    totals = fold_lanes(summed_up(grad_sums))
    rows = []
    pairs = []
    for h in range(8):
        part = slice(64 * h, 64 * h + 64)
        normal = saved[part, :]
        pre = norm_pull(rs[part, :], normal, scale, gain[...], totals, stem_total)
        rows.append(pre.astype(BF))
        if h % 2:
            pairs.append((before + pre).astype(BF))
        before = pre
    dv = jnp.concatenate(rows, 0)
    dside = jnp.concatenate(pairs, 0)

    low_half = iota((896, 128), 1) < 64
    du = dot_tn(win[...], dv)
    placed = jnp.zeros((896, 128), F32)
    for q in range(4):
        part = du[:, 128 * q : 128 * q + 128]
        first = pltpu.roll(part, 896 - 2 * q, 0) if q else part
        placed = placed + jnp.where(low_half, first, pltpu.roll(part, 896 - 2 * q - 1, 0))
    placed = placed + pltpu.roll(placed, 64, 1)
    tail_out[0:147, 0:64] = lax.dot_general(
        window_select(896, 147, "stem"), placed, (((0,), (0,)), ((), ())),
        preferred_element_type=F32, precision=lax.Precision.HIGHEST,
    )[:, :64]
    du2 = dot_tn(win2[...], dside)
    placed = jnp.zeros((384, 128), F32)
    for q in range(4):
        part = du2[:, 128 * q : 128 * q + 128]
        placed = placed + (pltpu.roll(part, 384 - 2 * q, 0) if q else part)
    placed = placed + pltpu.roll(placed, 64, 1)
    tail_out[0:54, 64:128] = lax.dot_general(
        window_select(384, 54, "diff"), placed, (((0,), (0,)), ((), ())),
        preferred_element_type=F32, precision=lax.Precision.HIGHEST,
    )[:, :64]

    dwin = dot_nt(dv, u[...])
    dwin2 = dot_nt(dside, u2[...])
    gate = gate_column(pack)
    steps = []
    for h2 in range(4):
        total = jnp.zeros((64, 128), F32)
        for dy in range(3):
            target = h2 + 1 - dy
            if 0 <= target < 4:
                total = total + dwin2[64 * target : 64 * target + 64, 128 * dy : 128 * dy + 128]
        later = pltpu.roll(total, 80, 1)
        later = jnp.concatenate([jnp.zeros((8, 128), F32), later[:-8]], 0)
        step = (total + later) * gate
        steps.append(step - jnp.concatenate([step[8:], jnp.zeros((8, 128), F32)], 0))
    pixels = []
    for h in range(8):
        total = steps[h // 2]
        for dy in range(7):
            target = h + 3 - dy
            if 0 <= target < 8:
                total = total + dwin[64 * target : 64 * target + 64, 128 * dy : 128 * dy + 128]
        pixels.append(total)
    pixels = jnp.concatenate(pixels, 0)
    back = lax.dot_general(
        pixels, gather_select(), (((1,), (1,)), ((), ())),
        preferred_element_type=F32, precision=lax.Precision.HIGHEST,
    )
    mask = own_block()
    for f in range(8):
        for c in range(3):
            for h in range(8):
                line = f * 24 + c * 8 + h
                block = back[h * 64 + f * 8 : h * 64 + f * 8 + 8, c * 128 : c * 128 + 128]
                lines[line : line + 1, :] = jnp.sum(block * mask, 0, keepdims=True)
    flat = lax.dot_general(
        lines[...], spread_select(), (((1,), (1,)), ((), ())),
        preferred_element_type=F32, precision=lax.Precision.HIGHEST,
    )
    frames_out[...] = flat.reshape(8, 3, 8, 64)
    og_all = og_total[0:2, :]
    rg_all = rg_total[0:2, :]
    for q in range(16):
        tail_out[152 + 2 * q : 154 + 2 * q, :] = og_all[:, 128 * q : 128 * q + 128] * share
    for q in range(4):
        tail_out[184 + 2 * q : 186 + 2 * q, :] = rg_all[:, 128 * q : 128 * q + 128] * share
    tail_out[192:194, :] = totals[:, :128] * share


def plane_pieces(near, far):
    return near.at[0], far.at[0], near.at[1], far.at[1]


def send_tiles(tiles, buffer, semaphores):
    copies = []
    for k, (fill, target) in enumerate(tiles):
        fill(buffer.at[k])
        copies.append(pltpu.make_async_copy(buffer.at[k], target, semaphores.at[k]))
        copies[-1].start()
    return copies


def finish_middle(info, near, far, near2, far2, *rest):
    out, token, buffer, semaphores = rest[-4:]
    token[...] = jnp.zeros(token.shape, F32)
    tiles = []
    for one, two, bit, partner in (
        (near, far, info[0], False), (near2, far2, 1 - info[0], True)
    ):
        row = pl.ds(pl.multiple_of(256 * bit, 128), 256)
        for piece, block in zip(plane_pieces(one, two), block_order(info, partner)):

            def fill(target, piece=piece):
                for tap in range(9):
                    target[tap] = piece[256 * tap : 256 * tap + 256, :].astype(F32)

            tiles.append((fill, out.at[:, row, lanes(128 * block, 128)]))
    for copy in send_tiles(tiles, buffer, semaphores):
        copy.wait()


def start_outer(
    first, info, mine, pair, expand_out, reduce_out,
    expand_buffer, reduce_buffer, expand_semaphores, reduce_semaphores,
):
    expand_tiles, reduce_tiles = [], []
    for pieces, bit, partner in ((mine, info[0], False), (pair, 1 - info[0], True)):
        order = block_order(info, partner)
        expand_row = pl.ds(pl.multiple_of(256 * bit, 128), 256)
        reduce_row = pl.ds(pl.multiple_of(1024 * bit, 128), 1024)
        for k, block in enumerate((order[1], order[3]) if first else (order[0], order[2])):

            def fill_expand(target, piece=pieces.at[k]):
                for q in range(4):
                    tile = piece[256 * q : 256 * q + 256, :].astype(F32)
                    target[:, 128 * q : 128 * q + 128] = tile

            def fill_reduce(target, piece=pieces.at[k]):
                target[...] = piece[1024:2048, :].astype(F32)

            expand_tiles.append((fill_expand, expand_out.at[expand_row, lanes(512 * block, 512)]))
            reduce_tiles.append((fill_reduce, reduce_out.at[reduce_row, lanes(128 * block, 128)]))
    copies = send_tiles(expand_tiles, expand_buffer, expand_semaphores)
    return copies + send_tiles(reduce_tiles, reduce_buffer, reduce_semaphores)


def finish_outer(first, info, mine, pair, *rest):
    expand_out, reduce_out, token = rest[-7:-4]
    token[...] = jnp.zeros(token.shape, F32)
    for copy in start_outer(first, info, mine, pair, expand_out, reduce_out, *rest[-4:]):
        copy.wait()


def finish_small(
    info, near, far, near2, far2, tail0, tail1, tail2, tail3,
    dsqueeze, dexcite, dfine, dcoarse, stem_out, diff_out, gain_s, bias_s, gain_r, bias_r,
    gain_x, bias_x, scratch, tail,
):
    for one, two, partner in ((near, far, False), (near2, far2, True)):
        for piece, block in zip(plane_pieces(one, two), block_order(info, partner)):
            rows = pl.ds(pl.multiple_of(64 * block, 64), 64)
            here = jnp.concatenate([piece[0:64, :], piece[64:128, :]], 1).astype(F32)
            scratch[rows, :] = scratch[rows, :] + here if partner else here
    tail[...] = tail0[...] + tail1[...] + tail2[...] + tail3[...]
    rows = scratch[...]
    dsqueeze[:, :256] = rows[0:32]
    dsqueeze[:, 256:] = rows[32:64]
    dexcite[:, :256] = rows[64:96]
    dexcite[:, 256:] = rows[96:128]
    for k in range(8):
        dfine[k] = rows[128:160, 32 * k : 32 * k + 32]
    dfine[8] = rows[160:192, 0:32]
    for k in range(9):
        dcoarse[k] = (
            rows[160:192, 32 * (k - 2) : 32 * (k - 2) + 32]
            if 3 <= k < 6
            else jnp.zeros((32, 32), F32)
        )
    stem_out[...] = tail[0:152, :].T[0:64, 0:147]
    for k in range(9):
        diff_out[k] = tail[6 * k : 6 * k + 6, 64:128]
    for q in range(16):
        bias_x[:, 128 * q : 128 * q + 128] = tail[152 + 2 * q : 153 + 2 * q, :]
        gain_x[:, 128 * q : 128 * q + 128] = tail[153 + 2 * q : 154 + 2 * q, :]
    for q in range(4):
        bias_r[:, 128 * q : 128 * q + 128] = tail[184 + 2 * q : 185 + 2 * q, :]
        gain_r[:, 128 * q : 128 * q + 128] = tail[185 + 2 * q : 186 + 2 * q, :]
    bias_s[...] = tail[192:193, :64]
    gain_s[...] = tail[193:194, :64]


def finish_rest(info, near, far, near2, far2, tail0, tail1, tail2, tail3, frames, *rest):
    rest[1][0] = frames[...]
    finish_small(info, near, far, near2, far2, tail0, tail1, tail2, tail3, *rest[2:])


def shape(dims, dtype=F32):
    return jax.ShapeDtypeStruct(dims, dtype)


def whole(dims):
    count = len(dims)
    return pl.BlockSpec(dims, lambda i, *scalars: (0,) * count)


class Far:
    def __init__(self, array, start=0, rows=None, clip=False, split=False, other=None):
        self.array, self.start, self.rows, self.clip = array, start, rows, clip
        self.split, self.other = split, other

    def copies(self):
        return self.array.shape[0] if self.split else 1

    def arrays(self):
        return [self.array] if self.other is None else [self.array, self.other]

    def buffer(self):
        dims = self.array.shape
        if self.clip:
            dims = dims[1:]
        elif self.rows is not None:
            dims = (self.rows,) + dims[1:]
        return pltpu.VMEM(dims, self.array.dtype)

    def source(self, ref, scalars):
        if self.clip:
            return ref.at[scalars[0][0]]
        if self.rows is not None:
            return ref.at[pl.ds(self.start, self.rows)]
        return ref


jax.tree_util.register_pytree_node(
    Far,
    lambda far: ((far.array, far.other), (far.start, far.rows, far.clip, far.split)),
    lambda rest, children: Far(children[0], *rest, children[1]),
)


class FarRef:
    def __init__(self, sources, buffer, semaphores, info):
        self.buffer, self.shape = buffer, buffer.shape
        source = sources[0]
        if len(semaphores) == 1:
            self.copies = [pltpu.make_async_copy(source, buffer, semaphores[0])]
        else:
            self.copies = [
                pltpu.make_async_copy(source.at[k], buffer.at[k], semaphore)
                for k, semaphore in enumerate(semaphores)
            ]
        if len(sources) == 1:
            for copy in self.copies:
                copy.start()
        else:
            other = pltpu.make_async_copy(sources[1], buffer, semaphores[0])
            pl.when(info[info.shape[0] - 1] == 1)(self.copies[0].start)
            pl.when(info[info.shape[0] - 1] == 0)(other.start)
        self.pending = set(range(len(self.copies)))

    def wait(self, part=None):
        for k in sorted(self.pending if part is None else self.pending & {part}):
            self.copies[k].wait()
            self.pending.discard(k)

    def __getitem__(self, place):
        self.wait(place if len(self.copies) > 1 and isinstance(place, int) else None)
        return self.buffer[place]


class FarOut:
    def __init__(self, out, parts=None):
        self.out = out
        self.parts = parts or [(0, out.shape[0])]


class FarOutRef:
    def __init__(self, buffer, home, semaphores, parts):
        self.buffer, self.shape = buffer, buffer.shape
        self.copies = [
            pltpu.make_async_copy(
                buffer.at[pl.ds(start, rows)], home.at[pl.ds(start, rows)], semaphore
            )
            for (start, rows), semaphore in zip(parts, semaphores)
        ]
        self.started = 0

    def __getitem__(self, place):
        return self.buffer[place]

    def __setitem__(self, place, value):
        self.buffer[place] = value

    def flush(self):
        self.copies[self.started].start()
        self.started += 1

    def finish(self):
        while self.started < len(self.copies):
            self.flush()
        for copy in self.copies:
            copy.wait()


def run(
    kernel, outs, arrays, scalars=(), scratch=(), choose=None, deps=(), cost=COST
):
    flat, tree = jax.tree.flatten(tuple(arrays), is_leaf=lambda x: isinstance(x, Far))
    operands, in_specs, places = [], [], []
    for array in flat:
        places.append(len(operands))
        if isinstance(array, Far):
            for piece in array.arrays():
                operands.append(pltpu.with_memory_space_constraint(piece, pltpu.HBM))
                in_specs.append(pl.BlockSpec(memory_space=pltpu.HBM))
            continue
        operands.append(array)
        in_specs.append(whole(array.shape))
    read = len(operands)
    for array in deps:
        operands.append(array)
        in_specs.append(pl.BlockSpec(memory_space=pl.ANY))
    out_specs, out_shape = [], []
    for out in outs:
        if isinstance(out, FarOut):
            out_specs.append(pl.BlockSpec(memory_space=pltpu.HBM))
            out_shape.append(pltpu.HBM(out.out.shape, out.out.dtype))
        else:
            out_specs.append(whole(out.shape))
            out_shape.append(out)
    far_in = [p for p, array in enumerate(flat) if isinstance(array, Far)]
    far_out = [p for p, out in enumerate(outs) if isinstance(out, FarOut)]
    buffers = [flat[p].buffer() for p in far_in]
    buffers += [pltpu.VMEM(outs[p].out.shape, outs[p].out.dtype) for p in far_out]
    moves = len(buffers)
    semaphore_count = sum(flat[p].copies() for p in far_in)
    semaphore_count += sum(len(outs[p].parts) for p in far_out)
    prefetched = tuple(scalars) if choose is None else tuple(scalars) + (choose,)

    def regrouped(*refs):
        first = len(prefetched)
        last = first + len(operands)
        end = last + len(outs)
        near, results = refs[first : first + read], list(refs[last:end])
        kept = refs[end : end + moves]
        semaphores = refs[end + moves] if moves else None
        rest = refs[end + moves + 1 :] if moves else refs[end:]
        ins = [near[place] for place in places]
        used = 0
        for k, p in enumerate(far_in):
            far = flat[p]
            own = [semaphores.at[used + n] for n in range(far.copies())]
            used += far.copies()
            sources = [
                far.source(near[places[p] + j], refs[:first]) for j in range(len(far.arrays()))
            ]
            ins[p] = FarRef(sources, kept[k], own, refs[first - 1])
        for k, p in enumerate(far_out):
            parts = outs[p].parts
            own = [semaphores.at[used + n] for n in range(len(parts))]
            used += len(parts)
            results[p] = FarOutRef(kept[len(far_in) + k], results[p], own, parts)
        kernel(*refs[: len(scalars)], *jax.tree.unflatten(tree, ins), *results, *rest)
        for p in far_in:
            ins[p].wait()
        for p in far_out:
            results[p].finish()

    return pl.pallas_call(
        regrouped,
        grid_spec=pltpu.PrefetchScalarGridSpec(
            num_scalar_prefetch=len(prefetched),
            grid=(1,),
            in_specs=in_specs,
            out_specs=out_specs,
            scratch_shapes=buffers
            + ([pltpu.SemaphoreType.DMA((semaphore_count,))] if moves else [])
            + list(scratch),
        ),
        out_shape=out_shape,
        compiler_params=pltpu.CompilerParams(vmem_limit_bytes=VMEM_BYTES),
        cost_estimate=pl.CostEstimate(flops=cost, bytes_accessed=cost, transcendentals=0),
    )(*prefetched, *operands)


ALL = ("z", "y", "x", "c")


def exchange(value, partner, whole_route=False):
    count = lax.axis_size(ALL)
    route = [(i, partner(i)) for i in range(count) if whole_route or partner(i) != i]
    return lax.ppermute(value, ALL, route)


def by_mask(value, mask):
    return exchange(value, lambda i: i ^ mask)


def bit_count(n):
    count = n.bit_length() - 1
    assert n == 1 << count
    return count


def swap_bits(i, first, second):
    if (i >> first & 1) != (i >> second & 1):
        i ^= (1 << first) | (1 << second)
    return i


def finish(kernel, info, pieces, outs, scratch, into=(), deps=()):
    far = [pl.BlockSpec(memory_space=pltpu.HBM)]
    first = 1 + len(pieces) + len(deps)
    return pl.pallas_call(
        kernel,
        grid_spec=pltpu.PrefetchScalarGridSpec(
            num_scalar_prefetch=1,
            grid=(1,),
            in_specs=[whole(piece.shape) for piece in pieces]
            + [pl.BlockSpec(memory_space=pl.ANY)] * len(deps)
            + far * len(into),
            out_specs=far * len(outs) + [whole((8, 128))],
            scratch_shapes=scratch,
        ),
        out_shape=[pltpu.HBM(out.shape, out.dtype) for out in outs] + [shape((8, 128))],
        input_output_aliases={first + k: k for k in range(len(into))},
        compiler_params=pltpu.CompilerParams(vmem_limit_bytes=VMEM_BYTES),
    )(info, *pieces, *deps, *(pltpu.with_memory_space_constraint(a, pltpu.HBM) for a in into))


def body(
    frames,
    cut_mask,
    offsets,
    stem_kernel,
    diff_kernel,
    stem_gain,
    stem_bias,
    reduce_weight,
    reduce_gain,
    reduce_bias,
    squeeze_weight,
    fine_kernel,
    coarse_kernel,
    excite_weight,
    middle_kernel,
    expand_weight,
    expand_gain,
    expand_bias,
    cotangent,
):
    depth = lax.axis_size("z")
    groups = 2 * depth
    assert frames.shape[0] == MICRO
    bits = bit_count(depth) + 3
    index = lax.axis_index(ALL)
    stem_total = float(4096 * groups)
    row_total = float(128 * groups)
    clip = lax.rem(index, 4).astype(jnp.int32)
    place = clip.reshape(1)
    bit_list = [lax.rem(lax.div(index, 1 << b), 2) for b in range(bits)]
    stays = jnp.where(bit_list[0] == bit_list[2], 1, 0)
    info = jnp.stack(bit_list + [stays]).astype(jnp.int32)
    plane = [(1, 2), (2, 1)]
    plane_mask = 6
    fine_flat = fine_kernel.reshape(288, 32)
    coarse_flat = coarse_kernel.reshape(288, 32)
    gain_s = jnp.tile(stem_gain, 8)[None]
    bias_s = jnp.tile(stem_bias, 8)[None]
    gain_r = reduce_gain[None]
    bias_r = reduce_bias[None]
    gain_x = expand_gain[None]
    bias_x = expand_bias[None]

    def swapped(value, whole_route=False):
        return exchange(value, lambda i: swap_bits(i, 0, 2), whole_route)

    def along(value, choice):
        return exchange(value, lambda i: i ^ (1 << choice[i & 1]))

    def pooled_sum(value):
        return depth_pieces(value + by_mask(value, 1))

    def depth_pieces(value):
        if depth > 4:
            return (lax.psum(value, "z"),)
        return (value,) + tuple(by_mask(value, m << 3) for m in reversed(range(1, depth)))

    def sums_shape(width):
        return shape((2, width))

    def to_plane(pieces):
        own, first, second, both = pieces
        both = by_mask(both, plane_mask)
        return own, along(first, plane[0]), along(second, plane[1]), both

    def padded(rows):
        unit = 16 * depth
        return -(-rows // unit) * unit

    def far(*arrays):
        return tuple(Far(array) for array in arrays)

    def stack(*pieces, deps=()):
        rows = sum(piece.shape[0] for piece in pieces)
        return run(stack_rows, [shape((rows, pieces[0].shape[1]), BF)], pieces, deps=deps)[0]

    def add(first, second, deps=()):
        return run(add_floats, [shape(first.shape)], (first, second), deps=deps)[0]

    def halves(kernel, rows, arrays, deps=()):
        return run(
            kernel, [shape((rows // 2, 128), BF)] * 2, arrays, (info,),
            [pltpu.VMEM((rows, 128), BF)], deps=deps,
        )

    (pack,) = run(
        pack_clip,
        [shape((208, 64), BF)],
        (*far(cut_mask, offsets[None]), Far(frames, clip=True)),
        (place,),
    )
    pack = (pack, swapped(pack))

    def far_pack():
        return Far(pack[0], other=pack[1])

    stem_scratch = [
        pltpu.VMEM((512, 896), BF),
        pltpu.VMEM((256, 384), BF),
        pltpu.VMEM((896, 512), BF),
        pltpu.VMEM((384, 512), BF),
        pltpu.VMEM((192, 128), F32),
        pltpu.VMEM((512, 384), F32),
    ]
    stem_weights = far(stem_kernel.T, diff_kernel)
    v, stem_sums = run(
        stem_front,
        [shape((512, 512)), sums_shape(512)],
        (pack, *stem_weights),
        (info,),
        stem_scratch,
    )
    stem_sums = pooled_sum(stem_sums)
    (cot,) = run(
        lambda place, *refs: copy_rows(*refs),
        [FarOut(shape(cotangent.shape[1:], BF))],
        (Far(cotangent, clip=True),),
        (place,),
        deps=(stem_sums[0],),
    )
    cot_got = swapped(cot)
    stem_norm = far(gain_s, bias_s)
    wide, wide_keep, send, red, red_sums, stem_saved = run(
        functools.partial(stem_close, stem_total),
        [
            FarOut(shape((128, 2048), BF)),
            shape((128, 1024), BF),
            shape((128, 1024), BF),
            shape((128, 512)),
            sums_shape(512),
            FarOut(shape((520, 512))),
        ],
        (v, stem_sums, *stem_norm, Far(reduce_weight)),
        (info,),
    )
    wide_pair = by_mask(send, 1)
    red_sums = pooled_sum(red_sums)
    wide_chip = stack(wide_keep, wide_pair, deps=(red_sums[0], cot_got))
    wide_got = along(wide_chip, plane[0])
    gate_weights = far(squeeze_weight.T, fine_flat, coarse_flat, excite_weight)
    gate_weights += (Far(middle_kernel, split=True),)
    both_keep, send, expanded, exp_sums, saved = run(
        functools.partial(gate_front, row_total),
        [
            shape((128, 512), BF),
            shape((128, 512), BF),
            shape((128, 2048)),
            sums_shape(2048),
            FarOut(shape((264, 512)), [(0, 136), (136, 128)]),
        ],
        (
            red, red_sums, far_pack(), *far(gain_r, bias_r), *gate_weights, Far(expand_weight),
        ),
        (info,),
        [pltpu.VMEM((128, 1024), BF)],
        choose=info,
        deps=(wide_chip,),
    )
    both_pair = by_mask(send, 1)
    exp_sums = pooled_sum(exp_sums)
    both_chip = stack(both_keep, both_pair, deps=(exp_sums[0],))
    both_got = along(both_chip, plane[0])
    wide_near = stack(wide_chip, wide_got, deps=(both_chip,))
    wide_far = along(wide_near, plane[1])
    og_sums, out_saved, out_scale = run(
        functools.partial(out_back, row_total),
        [
            sums_shape(2048),
            FarOut(shape((256, 2048), BF), [(0, 64), (128, 64), (64, 64), (192, 64)]),
            FarOut(shape((8, 2048))),
        ],
        (expanded, exp_sums, *far(gain_x, bias_x, wide), Far(cot, other=cot_got)),
        choose=info,
        deps=(wide_near,),
    )
    og_sums = pooled_sum(og_sums)
    both_near = stack(both_chip, both_got, deps=(og_sums[0],))
    both_far = along(both_near, plane[1])
    hg, og_total, *blocks = run(
        functools.partial(expand_back, row_total),
        [shape((128, 512), BF), FarOut(shape((8, 2048)))] + [shape((128, 640), BF)] * 4,
        (og_sums, *far(out_saved, out_scale), Far(saved, 136, 128), *far(gain_x, expand_weight)),
        (info,),
        [pltpu.VMEM((128, 512), BF), pltpu.VMEM((128, 2048), BF)],
        deps=(both_near,),
    )
    blocks = to_plane(blocks)
    rg, rg_sums, small = run(
        gate_back,
        [shape((128, 512)), sums_shape(512), shape((256, 256))],
        (far_pack(), hg, Far(saved, 0, 128), *far(gain_r, bias_r), *gate_weights),
        choose=info,
        deps=(wide_far, both_far),
    )
    rg_sums = pooled_sum(rg_sums)
    blocks = stack(*blocks, deps=(rg_sums[0],))
    blocks_pair = by_mask(blocks, 1)

    middle_rows = padded(2304)
    outer_rows = padded(2176)
    depth_bits = list(range(3, bits))
    have = {}
    held = [tuple(rg_sums[1:])]

    def waits():
        deps, held[0] = held[0], ()
        return deps

    def paired(value, rows):
        return value.reshape(2, rows, 128), by_mask(value, 1).reshape(2, rows, 128)

    def halve(name):
        deps = waits()
        for bit in depth_bits[1:]:
            keep, got = have[name]
            keep, send = halves(
                functools.partial(add_halves, bit), keep.shape[0], (keep, got), deps
            )
            have[name] = keep, by_mask(send, 1 << bit)
            deps = ()
        return keep

    def sum_up(name):
        keep, got = have[name]
        (value,) = run(add_rows, [shape(keep.shape, BF)], (keep, got), deps=waits())
        have[name] = value, by_mask(value, 1 << depth_bits[-1])
        return value

    def join(name, depth_range):
        deps = waits()
        for bit in depth_range:
            value, got = have[name]
            rows, width = value.shape
            (value,) = run(
                functools.partial(join_halves, bit),
                [shape((2 * rows, width), BF)],
                (value, got),
                (info,),
                deps=deps,
            )
            if bit > 3:
                have[name] = value, by_mask(value, 1 << (bit - 1))
            deps = ()
        if depth_range[-1] == 3:
            have[name] = value, along(value, plane[1])
        return value

    def near(name, rows):
        value = stack(*have[name], deps=waits())
        have[name + " far"] = along(value, plane[0])
        have[name + " near"] = paired(value, rows)
        return value

    def middle_kernel_sum():
        keep, send = halves(
            middle_weights, middle_rows, ((both_near, both_far), (blocks, blocks_pair)), waits()
        )
        have["middle"] = keep, by_mask(send, 8)
        return keep

    def reduction_back():
        rs, rs_sums, rg_total, *late = run(
            functools.partial(reduce_back, row_total),
            [shape((512, 512)), sums_shape(512), FarOut(shape((8, 512)))]
            + [shape((128, 256), BF)] * 4,
            (
                small, rg, rg_sums, Far(saved, 0, 136), Far(gain_r), Far(out_saved, 0, 128),
                *far(reduce_weight, stem_saved), *stem_norm,
            ),
            (info,),
            [pltpu.VMEM((128, 512), BF)],
            deps=waits(),
        )
        have["rs"] = rs, rs_sums, rg_total
        have["late"] = to_plane(late)
        return rs

    def stem_sum():
        rs_sums = have["rs"][1]
        have["rs here"] = add(rs_sums, by_mask(rs_sums, 1), waits())
        return have["rs here"]

    def late_rows():
        have["late"] = stack(*have["late"], deps=waits())
        have["late pair"] = by_mask(have["late"], 1)
        return have["late"]

    def outer_kernel_sum():
        keep, send = halves(
            outer_weights,
            outer_rows,
            (
                (both_near, both_far), (blocks, blocks_pair), (wide_near, wide_far),
                (have["late"], have["late pair"]),
            ),
            waits(),
        )
        have["outer"] = keep, by_mask(send, 8)
        return keep

    def stem_pieces():
        have["rs pieces"] = depth_pieces(have["rs here"])
        return held[0] + have["rs pieces"]

    def stem_gradient():
        rs, _, rg_total = have["rs"]
        have["frame"], have["tail"] = run(
            functools.partial(stem_back, stem_total, 1.0 / groups),
            [shape((8, 3, 8, 64)), shape((200, 128))],
            (
                far_pack(), *stem_weights, Far(stem_saved), stem_norm[0], rs, have["rs pieces"],
                Far(og_total), Far(rg_total),
            ),
            scratch=stem_scratch,
            choose=info,
            deps=waits(),
        )
        return have["tail"]

    def tail_add(bits_here):
        deps = waits()
        for bit in bits_here:
            have["tail"] = add(have["tail"], by_mask(have["tail"], 1 << bit), deps)
            deps = ()
        return have["tail"]

    def middle_far_rows():
        value = stack(have["middle far"], deps=waits())
        have["middle far"] = paired(value, middle_rows)
        return value

    outer_scratch = [
        pltpu.VMEM((4, 256, 512), F32),
        pltpu.VMEM((4, 1024, 128), F32),
        pltpu.SemaphoreType.DMA((4,)),
        pltpu.SemaphoreType.DMA((4,)),
    ]

    def middle_finish():
        one, two = have["middle near"], have["middle far"]
        have["dmiddle"], token = finish(
            finish_middle,
            info,
            (one[0], two[0], one[1], two[1]),
            [shape((9, 512, 512))],
            [pltpu.VMEM((8, 9, 256, 128), F32), pltpu.SemaphoreType.DMA((8,))],
            deps=waits(),
        )
        return token

    def outer_finish():
        dexpand, dreduce, token = finish(
            functools.partial(finish_outer, False),
            info,
            have["outer near"],
            [shape((512, 2048)), shape((2048, 512))],
            outer_scratch,
            deps=waits(),
        )
        have["outer out"] = dexpand, dreduce
        return token

    steps = {
        "K": middle_kernel_sum,
        "R": reduction_back,
        "Ma": lambda: halve("middle"),
        "Mb": lambda: sum_up("middle"),
        "Mc": lambda: join("middle", depth_bits[:0:-1]),
        "Md": lambda: join("middle", depth_bits[:1]),
        "Mn": lambda: near("middle", middle_rows),
        "Mf": middle_far_rows,
        "Rs": stem_sum,
        "St": late_rows,
        "O": outer_kernel_sum,
        "Oa": lambda: halve("outer"),
        "Ob": lambda: sum_up("outer"),
        "Oc": lambda: join("outer", depth_bits[:0:-1]),
        "Od": lambda: join("outer", depth_bits[:1]),
        "On": lambda: near("outer", outer_rows),
        "Z": stem_pieces,
        "B": stem_gradient,
        "T0": lambda: tail_add([0]),
        "T3": lambda: tail_add(depth_bits[:-1]),
        "T4": lambda: tail_add(depth_bits[-1:]),
        "F": middle_finish,
        "G": outer_finish,
    }
    for name in ORDER:
        result = steps[name]()
        held[0] = result if isinstance(result, tuple) else (result,)
    frame_grad, tail = have["frame"], have["tail"]
    dmiddle = have["dmiddle"]
    dexpand, dreduce = have["outer out"]
    outer_near = have["outer near"]
    token = held[0][0]
    outer_far = have["outer far"]
    frame_grad = swapped(frame_grad, True)
    outer_far = stack(outer_far, deps=(token,))
    outer_far = paired(outer_far, outer_rows)
    tail = (tail,) + tuple(by_mask(tail, mask) for mask in (6, 4, 2))
    dexpand, dreduce, token = finish(
        functools.partial(finish_outer, True),
        info,
        outer_far,
        [shape((512, 2048)), shape((2048, 512))],
        outer_scratch,
        (dexpand, dreduce),
    )
    outer = (outer_near[0], outer_far[0], outer_near[1], outer_far[1])
    small_shapes = ((1, 8, 3, 8, 64), (32, 512), (32, 512), (9, 32, 32), (9, 32, 32), (64, 147))
    small_shapes += ((9, 6, 64),) + tuple((1, n) for n in (64, 64, 512, 512, 2048, 2048))
    (
        frame_grad, dsqueeze, dexcite, dfine, dcoarse, dstem, ddiff, gain_s, bias_s, gain_r,
        bias_r, gain_x, bias_x,
    ) = pl.pallas_call(
        finish_rest,
        grid_spec=pltpu.PrefetchScalarGridSpec(
            num_scalar_prefetch=1,
            grid=(1,),
            in_specs=[pl.BlockSpec((2, 128, 128), lambda i, info: (0, 16, 0))] * 4
            + [whole((200, 128))] * 4
            + [whole((8, 3, 8, 64)), pl.BlockSpec(memory_space=pl.ANY)],
            out_specs=[whole(d) for d in small_shapes],
            scratch_shapes=[pltpu.VMEM((256, 256), F32), pltpu.VMEM((200, 128), F32)],
        ),
        out_shape=[shape(d) for d in small_shapes],
        compiler_params=pltpu.CompilerParams(vmem_limit_bytes=FINISH_BYTES),
    )(info, *outer, *tail, frame_grad, token)
    return (
        frame_grad,
        dstem.T,
        ddiff,
        gain_s[0],
        bias_s[0],
        dreduce,
        gain_r[0],
        bias_r[0],
        dsqueeze.T,
        dfine,
        dcoarse,
        dexcite,
        dmiddle,
        dexpand,
        gain_x[0],
        bias_x[0],
    )


def solution(mesh):
    split = jax.sharding.Mesh(mesh.devices.reshape(-1, 2, 2, 2), ALL)
    copied = P()
    by_group = P(("z", "y"))
    in_specs = (by_group,) * 3 + (copied,) * 15 + (by_group,)
    out_specs = (P(ALL),) + (copied,) * 15
    return jax.shard_map(body, mesh=split, in_specs=in_specs, out_specs=out_specs, check_vma=False)
```
